32 devices in a mesh: rep: 4 (over y, x), shard: 8 (over z, core).
Axes of the slice: x: 2, y: 2, z: 4, core: 2. Of those that a mesh axis runs over, the one named last changes fastest.
Arguments:
- tokens: bfloat16 [32768, 768], P(('rep', 'shard')), may hold values from -6 to 6
- cotangent: bfloat16 [32768, 768], P(('rep', 'shard')), may hold values from -6 to 6
- task: int32 [256], P(('rep', 'shard')), may hold values from 0 to 2
- lengths: int32 [256], P(('rep', 'shard')), may hold values from 64 to 128
- task_masks: int32 [3, 32768], P(None, ('rep', 'shard')), may hold values 0 or 1
- w_qkv: bfloat16 [768, 2304], P('shard'), may hold values from -0.21875 to 0.21875
- qv_bias: bfloat16 [1536], P('shard'), may hold values from -3 to 3
- w_out: bfloat16 [768, 768], P('shard'), may hold values from -0.625 to 0.625
- out_bias: bfloat16 [768], P('shard'), may hold values from -3 to 3
- ln1_gain: bfloat16 [768], P('shard'), may hold values from 0.5 to 1.5
- ln1_bias: bfloat16 [768], P('shard'), may hold values from -3 to 3
- w_up: bfloat16 [768, 3072], P('shard'), may hold values from -0.21875 to 0.21875
- up_bias: bfloat16 [3072], P('shard'), may hold values from -3 to 3
- w_down: bfloat16 [3072, 768], P('shard'), may hold values from -0.109375 to 0.109375
- down_bias: bfloat16 [768], P('shard'), may hold values from -3 to 3
- ln2_gain: bfloat16 [768], P('shard'), may hold values from 0.5 to 1.5
- ln2_bias: bfloat16 [768], P('shard'), may hold values from -3 to 3
Outputs:
- output: bfloat16 [32768, 768], P(('rep', 'shard'))
- grad_tokens: bfloat16 [32768, 768], P(('rep', 'shard'))
- grad_w_qkv: float32 [768, 2304], P('shard')
- grad_qv_bias: float32 [1536], P('shard')
- grad_w_out: float32 [768, 768], P('shard')
- grad_out_bias: float32 [768], P('shard')
- grad_ln1_gain: float32 [768], P('shard')
- grad_ln1_bias: float32 [768], P('shard')
- grad_w_up: float32 [768, 3072], P('shard')
- grad_up_bias: float32 [3072], P('shard')
- grad_w_down: float32 [3072, 768], P('shard')
- grad_down_bias: float32 [768], P('shard')
- grad_ln2_gain: float32 [768], P('shard')
- grad_ln2_bias: float32 [768], P('shard')
The draws below stay inside these ranges and needn't reach their ends.
Inputs may be any that keep to these rules, and one draw needn't show every extreme that they name: `task`: 0 masked language, 1 masked region, 2 image-text matching.
All inputs are finite; a program needn't handle non-finite values. No bound on the sum of `task_masks` on one device may be relied on, other than what follows from the above.
Results may differ from the reference program's by a relative error of at most 0.015.
Values may be sent and summed in bfloat16 or wider, within the bound.
No kernel may reach another device: no remote copies, remote signals or barrier semaphores. Data moves between devices by JAX's collectives and lax.ppermute only.
A program may use at most 192 MiB of HBM per device.

```python
from functools import partial
import jax
import jax.numpy as jnp
from jax import lax

D = 768
HD = 64
FF = 3072
LEN = 128
SEQS = 256
TOKENS = 32768


def plant(values, rng, least, largest):
    index_at = [jax.random.randint(jax.random.fold_in(rng, axis), (), 0, length) for axis, length in enumerate(values.shape)]
    main_axis = values.shape.index(max(values.shape))
    neighbour = index_at[:main_axis] + [(index_at[main_axis] + 1) % values.shape[main_axis]] + index_at[main_axis + 1:]
    return values.at[tuple(index_at)].set(least).at[tuple(neighbour)].set(largest)


def steps_of(key, extent, pieces, least, top_value):
    loudness = 1.0
    for dim, shards_of in pieces:
        heights = jax.random.uniform(jax.random.fold_in(jax.random.fold_in(key, 6), dim), (shards_of,), jnp.float32, least / len(pieces), top_value / len(pieces))
        loudness = loudness * jnp.repeat(jnp.exp(heights), extent[dim] // shards_of).reshape((-1,) + (1,) * (len(extent) - 1 - dim))
    return loudness


def normal_values(stream_key, extent, width, reach, split=(), held_as=jnp.bfloat16):
    entries = jax.random.normal(stream_key, extent, jnp.float32) * width
    if len(split) > 0:
        entries = steps_of(stream_key, extent, split, -0.22, 0.18) * entries
    return jnp.clip(entries, min=-reach, max=reach).astype(held_as)


def setup_inputs(seed: int = 0) -> dict:
    keys = jax.random.split(jax.random.key(seed), 18)
    tokens = normal_values(keys[0], (TOKENS, D), 1.0, 6.0, ((0, 32),))
    cotangent = normal_values(keys[1], (TOKENS, D), 1.0, 6.0, ((0, 32),))
    task = plant(jax.random.randint(keys[2], (SEQS,), 0, 3), jax.random.fold_in(keys[2], 1), 0, 2).astype(jnp.int32)
    lengths = plant(jax.random.randint(keys[3], (SEQS,), LEN // 2, LEN + 1), jax.random.fold_in(keys[3], 1), LEN // 2, LEN).astype(jnp.int32)
    task_masks = plant((jax.random.randint(keys[4], (3, TOKENS), 0, 2) < 1).astype(jnp.int32), jax.random.fold_in(keys[4], 1), 0, 1)
    w_qkv = normal_values(keys[5], (D, 3 * D), D ** -0.5, 0.21875, ((0, 8),))
    qv_bias = normal_values(keys[6], (2 * D,), 0.5, 3.0, ((0, 8),))
    w_out = normal_values(keys[7], (D, D), (D // 8) ** -0.5, 0.625, ((0, 8),))
    out_bias = normal_values(keys[8], (D,), 0.5, 3.0, ((0, 8),))
    ln1_gain = jnp.clip(1.0 + 0.1 * jax.random.normal(keys[9], (D,), jnp.float32), 0.5, 1.5).astype(jnp.bfloat16)
    ln1_bias = normal_values(keys[10], (D,), 0.5, 3.0, ((0, 8),))
    w_up = normal_values(keys[11], (D, FF), D ** -0.5, 0.21875, ((0, 8),))
    up_bias = normal_values(keys[12], (FF,), 0.5, 3.0, ((0, 8),))
    w_down = normal_values(keys[13], (FF, D), FF ** -0.5, 0.109375, ((0, 8),))
    down_bias = normal_values(keys[14], (D,), 0.5, 3.0, ((0, 8),))
    ln2_gain = jnp.clip(1.0 + 0.1 * jax.random.normal(keys[15], (D,), jnp.float32), 0.5, 1.5).astype(jnp.bfloat16)
    ln2_bias = normal_values(keys[16], (D,), 0.5, 3.0, ((0, 8),))
    return {"tokens": tokens, "cotangent": cotangent, "task": task, "lengths": lengths, "task_masks": task_masks, "w_qkv": w_qkv, "qv_bias": qv_bias, "w_out": w_out, "out_bias": out_bias, "ln1_gain": ln1_gain, "ln1_bias": ln1_bias, "w_up": w_up, "up_bias": up_bias, "w_down": w_down, "down_bias": down_bias, "ln2_gain": ln2_gain, "ln2_bias": ln2_bias}


EPSILON = 1e-06
HIGHEST = lax.Precision.HIGHEST

@jax.custom_vjp
def low(v):
    return lax.optimization_barrier(v.astype(jnp.bfloat16)).astype(jnp.float32)

@jax.custom_vjp
def low_back(v):
    return v

def low_keep(v):
    return (low(v), None)

def low_pass(kept, grad):
    return (grad,)

def back_keep(v):
    return (v, None)

def back_low(kept, grad):
    return (low(grad),)
low.defvjp(low_keep, low_pass)
low_back.defvjp(back_keep, back_low)

def product(left, right):
    return jnp.dot(left, right, precision=HIGHEST, preferred_element_type=jnp.float32)

def normalize(summed, gain, shift):
    centre = lax.optimization_barrier(jnp.mean(summed, -1, keepdims=True))
    deviation = summed - centre
    variance = lax.optimization_barrier(jnp.mean(deviation * deviation, -1, keepdims=True))
    return deviation * lax.rsqrt(variance + EPSILON) * gain + shift

def block_forward(key_valid, inputs, w_qkv, qv_bias, w_out, out_bias, ln1_gain, ln1_bias, w_up, up_bias, w_down, down_bias, ln2_gain, ln2_bias):
    row_count, model_width = inputs.shape
    seq_count = key_valid.shape[0]
    head_count = model_width // HD
    zero_shift = jnp.zeros((model_width,), jnp.float32)
    qkv_shift = jnp.concatenate([qv_bias[:model_width], zero_shift, qv_bias[model_width:]])
    projected = low(low_back(product(inputs, w_qkv) + qkv_shift))
    packed = projected.reshape(seq_count, LEN, 3, head_count, HD)
    queries = packed[:, :, 0]
    key_rows = packed[:, :, 1]
    value_rows = packed[:, :, 2]
    scores = jnp.einsum('sqhe,skhe->shqk', queries, key_rows, precision=HIGHEST) * 0.125
    scores = low_back(scores)
    masked = jnp.where(key_valid[:, None, None, :], scores, -1000000000.0)
    attention = low(jax.nn.softmax(masked, axis=-1))
    context = jnp.einsum('shqk,skhe->sqhe', attention, value_rows, precision=HIGHEST)
    context = low(low_back(context.reshape(row_count, model_width)))
    attended = low_back(product(context, w_out) + out_bias)
    first_norm = normalize(inputs + attended, ln1_gain, ln1_bias)
    inner = low_back(product(low(first_norm), w_up) + up_bias)
    activated = low(jax.nn.gelu(inner, approximate=False))
    ffn_out = low_back(product(activated, w_down) + down_bias)
    return normalize(first_norm + ffn_out, ln2_gain, ln2_bias)

def reference(tokens, cotangent, task, lengths, task_masks, w_qkv, qv_bias, w_out, out_bias, ln1_gain, ln1_bias, w_up, up_bias, w_down, down_bias, ln2_gain, ln2_bias):
    params = tuple((entry.astype(jnp.float32) for entry in (w_qkv, qv_bias, w_out, out_bias, ln1_gain, ln1_bias, w_up, up_bias, w_down, down_bias, ln2_gain, ln2_bias)))
    model_width = tokens.shape[1]
    group_seqs = 32
    group_count = task.shape[0] // group_seqs
    group_rows = group_seqs * LEN
    token_groups = tokens.reshape(group_count, group_rows, model_width)
    cot_groups = cotangent.reshape(group_count, group_rows, model_width)
    task_groups = task.reshape(group_count, group_seqs)
    length_groups = lengths.reshape(group_count, group_seqs)
    mask_groups = task_masks.reshape(3, group_count, group_rows).transpose(1, 0, 2)

    def step(totals, items):
        token_part, cot_part, task_part, length_part, mask_part = items
        position = jnp.arange(LEN, dtype=jnp.int32)
        key_valid = position[None, :] < length_part[:, None]
        token_task = jnp.repeat(task_part, LEN)
        chosen = jnp.where(token_task == 0, mask_part[0], jnp.where(token_task == 1, mask_part[1], mask_part[2]))
        row_weight = (chosen * key_valid.reshape(group_rows).astype(jnp.int32)).astype(jnp.float32)
        inputs = token_part.astype(jnp.float32)
        result, backward = jax.vjp(partial(block_forward, key_valid), inputs, *params)
        grads = backward(cot_part.astype(jnp.float32) * row_weight[:, None])
        totals = tuple((accum + fresh for accum, fresh in zip(totals, grads[1:])))
        return (totals, (result.astype(jnp.bfloat16), grads[0].astype(jnp.bfloat16)))
    initial = tuple((jnp.zeros(entry.shape, jnp.float32) for entry in params))
    totals, (results, input_grads) = lax.scan(step, initial, (token_groups, cot_groups, task_groups, length_groups, mask_groups))
    return (results.reshape(tokens.shape), input_grads.reshape(tokens.shape), totals[0], totals[1], totals[2], totals[3], totals[4], totals[5], totals[6], totals[7], totals[8], totals[9], totals[10], totals[11])
```

```python
import functools

import jax
import jax.numpy as jnp
from jax import lax
from jax.experimental import pallas as pl
from jax.experimental.pallas import tpu as pltpu
from jax.sharding import PartitionSpec as P

HD = 64
LEN = 128
EPSILON = 1e-06
BF = jnp.bfloat16
F32 = jnp.float32
MIB = 1024 * 1024

TAIL_P = 0.36
TAIL = (0.143717436, 0.141710663, 0.140057471, 0.0256236997, 0.182297768, -0.180751783, 0.0473446063)
DENSITY = 0.3989422804014327


def dot_nn(left, right):
    return jnp.dot(left, right, preferred_element_type=F32)


def dot_nt(left, right):
    return lax.dot_general(left, right, (((1,), (1,)), ((), ())), preferred_element_type=F32)


def dot_tn(left, right):
    return lax.dot_general(left, right, (((0,), (0,)), ((), ())), preferred_element_type=F32)


def gelu_parts(inner):
    size = jnp.abs(inner)
    t = 1.0 / (1.0 + TAIL_P * size)
    bell = jnp.exp(-0.5 * inner * inner)
    poly = TAIL[6]
    for coefficient in TAIL[5::-1]:
        poly = poly * t + coefficient
    tail = poly * t * bell
    phi = jnp.where(inner < 0, tail, 1.0 - tail)
    return inner * phi, phi + inner * (bell * DENSITY)


def norm_parts(summed):
    centre = jnp.mean(summed, -1, keepdims=True)
    deviation = summed - centre
    variance = jnp.mean(deviation * deviation, -1, keepdims=True)
    rscale = lax.rsqrt(variance + EPSILON)
    return deviation * rscale, rscale


def norm_back(grad_norm, normed, rscale):
    first_mean = jnp.mean(grad_norm, -1, keepdims=True)
    second_mean = jnp.mean(grad_norm * normed, -1, keepdims=True)
    return rscale * (grad_norm - first_mean - normed * second_mean)


def add_rows(total_ref, rows):
    @pl.when(pl.program_id(0) == 0)
    def _():
        total_ref[...] = jnp.zeros_like(total_ref)

    for at, values in enumerate(rows):
        total_ref[at : at + 1, :] += jnp.sum(values, 0, keepdims=True)


def cost(flops, moved):
    return pl.CostEstimate(flops=int(flops), bytes_accessed=int(moved), transcendentals=0)


def params(vmem=48):
    return pltpu.CompilerParams(vmem_limit_bytes=vmem * MIB)


def whole(shape):
    return pl.BlockSpec(shape, lambda i, *_: (0,) * len(shape))


def rows_of(block, width):
    return pl.BlockSpec((block, width), lambda i, *_: (i, 0))


def head_masks():
    lane = lax.broadcasted_iota(jnp.int32, (1, 2 * HD), 1)
    return (lane < HD).astype(BF), (lane >= HD).astype(BF)


def stack_heads(pair, masks):
    return jnp.concatenate([pair * masks[0], pair * masks[1]], axis=0)


def attention_forward_kernel(plan, place, lengths, x_ref, shift_ref, *refs):
    pieces, (proj_ref, ctx_ref, lse_ref, w_ref), sems = refs[: len(plan)], refs[len(plan) : len(plan) + 4], refs[len(plan) + 4]
    block, width = x_ref.shape
    step = pl.program_id(0)

    @pl.when(step == 0)
    def _():
        bring(plan, place, pieces, w_ref, sems)

    x = x_ref[...]
    for unit in range(3):
        at = slice(unit * width, (unit + 1) * width)
        proj_ref[:, at] = (dot_nn(x, w_ref[unit]) + shift_ref[:, at]).astype(BF)
    masks = head_masks()
    lane = lax.broadcasted_iota(jnp.int32, (1, LEN), 1)
    for seq in range(block // LEN):
        rows = slice(seq * LEN, (seq + 1) * LEN)
        valid = lane < lengths[step * (block // LEN) + seq]
        lse = jnp.zeros((LEN, LEN), F32)
        for pair in range(width // (2 * HD)):
            at = pair * 2 * HD
            q = proj_ref[rows, at : at + 2 * HD] * BF(0.125)
            k = proj_ref[rows, width + at : width + at + 2 * HD]
            v = proj_ref[rows, 2 * width + at : 2 * width + at + 2 * HD]
            scores = dot_nt(q, stack_heads(k, masks))
            probs = []
            for half in range(2):
                masked = jnp.where(valid, scores[:, half * LEN : (half + 1) * LEN], -1e9)
                top = jnp.max(masked, -1, keepdims=True)
                exponent = jnp.exp(masked - top)
                total = jnp.sum(exponent, -1, keepdims=True)
                probs.append((exponent * (1.0 / total)).astype(BF))
                lse = jnp.where(lane == 2 * pair + half, top + jnp.log(total), lse)
            ctx = dot_nn(jnp.concatenate(probs, axis=1), stack_heads(v, masks))
            ctx_ref[rows, at : at + 2 * HD] = ctx.astype(BF)
        lse_ref[seq] = lse.T[: lse_ref.shape[1]]


def bring(plan, place, pieces, w_ref, sems):
    rep, chip, core = place[0], place[1], place[2]
    copies = []
    for piece, entries in zip(pieces, plan):
        for at, (unit, flip, other, ahead, first, count, depth) in enumerate(entries):
            to_unit = (rep ^ unit) if flip else unit
            shard = 2 * ((chip + ahead) % 4) + (core ^ other)
            row = pl.multiple_of(shard * depth + first, 16)
            copies.append(pltpu.make_async_copy(piece.at[at], w_ref.at[to_unit, pl.ds(row, count)], sems.at[len(copies)]))
    for copy in copies:
        copy.start()
    for copy in copies:
        copy.wait()


def weight_args(weight, shape):
    plan, pieces = weight
    return plan, pieces, [pl.BlockSpec(memory_space=pl.ANY)] * len(pieces), pltpu.SemaphoreType.DMA((sum(len(p) for p in plan),))


def attention_forward(place, lengths, tokens, shift, weight):
    rows, width = tokens.shape
    block = 2 * LEN
    heads = width // HD
    lse_rows = -(-heads // 8) * 8
    plan, pieces, specs, sems = weight_args(weight, None)
    return pl.pallas_call(
        functools.partial(attention_forward_kernel, plan),
        grid_spec=pltpu.PrefetchScalarGridSpec(
            num_scalar_prefetch=2,
            grid=(rows // block,),
            in_specs=[rows_of(block, width), whole((1, 3 * width))] + specs,
            out_specs=[
                rows_of(block, 3 * width),
                rows_of(block, width),
                pl.BlockSpec((block // LEN, lse_rows, LEN), lambda i, *_: (i, 0, 0)),
                whole((4, width, width)),
            ],
            scratch_shapes=[sems],
        ),
        out_shape=[
            jax.ShapeDtypeStruct((rows, 3 * width), BF),
            jax.ShapeDtypeStruct((rows, width), BF),
            jax.ShapeDtypeStruct((rows // LEN, lse_rows, LEN), F32),
            jax.ShapeDtypeStruct((4, width, width), BF),
        ],
        compiler_params=params(),
        cost_estimate=cost(6 * rows * width * width * 2, 14e6),
        name="attention_forward",
    )(place, lengths, tokens, shift, *pieces)


def middle_kernel(plan, place, x_ref, ctx_ref, w_out_ref, vec_ref, up_shift_ref, *refs):
    pieces = refs[: len(plan)]
    norm_ref, scale_ref, low_ref, act_ref, slope_ref, w_ref, sems = refs[len(plan) :]
    width = x_ref.shape[1]

    @pl.when(pl.program_id(0) == 0)
    def _():
        bring(plan, place, pieces, w_ref, sems)

    attended = dot_nn(ctx_ref[...], w_out_ref[0]) + vec_ref[0:1, :]
    normed, rscale = norm_parts(x_ref[...].astype(F32) + attended)
    norm_ref[...] = normed
    scale_ref[...] = rscale
    low = (normed * vec_ref[1:2, :] + vec_ref[2:3, :]).astype(BF)
    low_ref[...] = low
    for unit in range(w_ref.shape[0]):
        at = slice(unit * width, (unit + 1) * width)
        act, slope = gelu_parts(dot_nn(low, w_ref[unit]) + up_shift_ref[:, at])
        act_ref[:, at] = act.astype(BF)
        slope_ref[:, at] = slope.astype(BF)


def middle(place, tokens, context, w_qkvo, vecs, up_shift, weight, block=256):
    rows, width = tokens.shape
    hidden = up_shift.shape[1]
    units = hidden // width
    plan, pieces, specs, sems = weight_args(weight, None)
    return pl.pallas_call(
        functools.partial(middle_kernel, plan),
        grid_spec=pltpu.PrefetchScalarGridSpec(
            num_scalar_prefetch=1,
            grid=(rows // block,),
            in_specs=[
                rows_of(block, width),
                rows_of(block, width),
                pl.BlockSpec((1, width, width), lambda i, *_: (3, 0, 0)),
                whole(vecs.shape),
                whole(up_shift.shape),
            ]
            + specs,
            out_specs=[
                rows_of(block, width),
                rows_of(block, 1),
                rows_of(block, width),
                rows_of(block, hidden),
                rows_of(block, hidden),
                whole((units, width, width)),
            ],
            scratch_shapes=[sems],
        ),
        out_shape=[
            jax.ShapeDtypeStruct((rows, width), F32),
            jax.ShapeDtypeStruct((rows, 1), F32),
            jax.ShapeDtypeStruct((rows, width), BF),
            jax.ShapeDtypeStruct((rows, hidden), BF),
            jax.ShapeDtypeStruct((rows, hidden), BF),
            jax.ShapeDtypeStruct((units, width, width), BF),
        ],
        compiler_params=params(),
        cost_estimate=cost(2 * rows * width * (width + hidden), 25e6),
        name="middle",
    )(place, tokens, context, w_qkvo, vecs, up_shift, *pieces)


def ffn_out_kernel(act_ref, w_ref, norm_ref, cot_ref, weight_ref, vec_ref, out_ref, dz_ref, low_ref, sum_ref):
    first = norm_ref[...] * vec_ref[1:2, :] + vec_ref[2:3, :]
    normed, rscale = norm_parts(first + (dot_nn(act_ref[...], w_ref[...]) + vec_ref[3:4, :]))
    out_ref[...] = (normed * vec_ref[4:5, :] + vec_ref[5:6, :]).astype(BF)
    grad = cot_ref[...].astype(F32) * weight_ref[...]
    dz = norm_back(grad * vec_ref[4:5, :], normed, rscale)
    low = dz.astype(BF)
    dz_ref[...] = dz
    low_ref[...] = low
    add_rows(sum_ref, (grad * normed, grad, low.astype(F32)))


def ffn_out(act, w_down, norm_one, cotangent, row_weight, vecs, block=256):
    rows, width = cotangent.shape
    hidden = act.shape[1]
    return pl.pallas_call(
        ffn_out_kernel,
        grid=(rows // block,),
        in_specs=[
            rows_of(block, hidden),
            whole((hidden, width)),
            rows_of(block, width),
            rows_of(block, width),
            rows_of(block, 1),
            whole(vecs.shape),
        ],
        out_specs=[rows_of(block, width), rows_of(block, width), rows_of(block, width), whole((8, width))],
        out_shape=[
            jax.ShapeDtypeStruct((rows, width), BF),
            jax.ShapeDtypeStruct((rows, width), F32),
            jax.ShapeDtypeStruct((rows, width), BF),
            jax.ShapeDtypeStruct((8, width), F32),
        ],
        compiler_params=params(),
        cost_estimate=cost(2 * rows * width * hidden, 22e6),
        name="ffn_out",
    )(act, w_down, norm_one, cotangent, row_weight, vecs)


def grad_down_kernel(low_ref, act_ref, out_ref, turned_ref):
    @pl.when(pl.program_id(0) == 0)
    def _():
        turned_ref[...] = low_ref[...].T

    grad = dot_nn(turned_ref[...], act_ref[...])
    part = out_ref.shape[2]
    for at in range(out_ref.shape[0]):
        out_ref[at] = grad[:, at * part : (at + 1) * part].astype(BF)


def grad_down_natural(low, act, shards, span=768):
    rows, width = low.shape
    hidden = act.shape[1]
    part = hidden // shards
    each = max(1, span // part)
    return pl.pallas_call(
        grad_down_kernel,
        grid=(shards // each,),
        in_specs=[whole((rows, width)), pl.BlockSpec((rows, each * part), lambda i: (0, i))],
        out_specs=pl.BlockSpec((each, width, part), lambda i: (i, 0, 0)),
        out_shape=jax.ShapeDtypeStruct((shards, width, part), BF),
        scratch_shapes=[pltpu.VMEM((width, rows), BF)],
        compiler_params=params(),
        cost_estimate=cost(2 * rows * width * hidden, 13e6),
        name="grad_down",
    )(low, act)


def inner_grad_kernel(low_ref, w_ref, slope_ref, out_ref, sum_ref):
    width = low_ref.shape[1]

    @pl.when(pl.program_id(0) == 0)
    def _():
        sum_ref[...] = jnp.zeros_like(sum_ref)

    for unit in range(w_ref.shape[0] // width):
        at = slice(unit * width, (unit + 1) * width)
        grad = (dot_nt(low_ref[...], w_ref[at, :]) * slope_ref[:, at].astype(F32)).astype(BF)
        out_ref[:, at] = grad
        sum_ref[0:1, at] += jnp.sum(grad.astype(F32), 0, keepdims=True)


def inner_grad(low, w_down, slope, block=256):
    rows, width = low.shape
    hidden = slope.shape[1]
    return pl.pallas_call(
        inner_grad_kernel,
        grid=(rows // block,),
        in_specs=[rows_of(block, width), whole((hidden, width)), rows_of(block, hidden)],
        out_specs=[rows_of(block, hidden), whole((8, hidden))],
        out_shape=[jax.ShapeDtypeStruct((rows, hidden), BF), jax.ShapeDtypeStruct((8, hidden), F32)],
        compiler_params=params(),
        cost_estimate=cost(2 * rows * width * hidden, 18e6),
        name="inner_grad",
    )(low, w_down, slope)


def unit_grads_kernel(sources, relative, place, *refs):
    lefts, (right_ref, tail_ref) = refs[:sources], refs[sources : sources + 2]
    outs, (turned_ref, grad_ref) = refs[sources + 2 : -2], refs[-2:]
    step = pl.program_id(0)

    @pl.when(step == 0)
    def _():
        turned_ref[...] = lefts[0][...].T

    if sources == 2:

        @pl.when(step == 3)
        def _():
            turned_ref[...] = lefts[1][...].T
            grad_ref[...] = dot_nn(turned_ref[...], tail_ref[...]).astype(BF)

        @pl.when(step < 3)
        def _():
            grad_ref[...] = dot_nn(turned_ref[...], right_ref[...]).astype(BF)
    else:
        grad_ref[...] = dot_nn(turned_ref[...], right_ref[...]).astype(BF)
    if not relative:
        outs[0][0] = grad_ref[...]
        return
    chip, core = place[1], place[2]
    depth = outs[0].shape[2]
    for other in range(4):
        ahead = (other - chip) % 4
        for out, which in zip(outs, (core, 1 - core)):
            row = pl.multiple_of((2 * other + which) * depth, 16)
            out[0, ahead] = grad_ref[pl.ds(row, depth), :]


def unit_grads(place, lefts, right, tail, relative):
    rows, width = lefts[0].shape
    last = right.shape[1] // width - 1
    if relative:
        depth = width // 8
        out_specs = [pl.BlockSpec((1, 4, depth, width), lambda i, place: (i ^ place[0], 0, 0, 0))] * 2
        out_shape = [jax.ShapeDtypeStruct((4, 4, depth, width), BF)] * 2
    else:
        out_specs = [pl.BlockSpec((1, width, width), lambda i, place: (i, 0, 0))]
        out_shape = [jax.ShapeDtypeStruct((4, width, width), BF)]
    return pl.pallas_call(
        functools.partial(unit_grads_kernel, len(lefts), relative),
        grid_spec=pltpu.PrefetchScalarGridSpec(
            num_scalar_prefetch=1,
            grid=(4,),
            in_specs=[whole((rows, width))] * len(lefts)
            + [pl.BlockSpec((rows, width), lambda i, place: (0, jnp.minimum(i, last))), whole((rows, width))],
            out_specs=out_specs,
            scratch_shapes=[pltpu.VMEM((width, rows), BF), pltpu.VMEM((width, width), BF)],
        ),
        out_shape=out_shape,
        compiler_params=params(),
        cost_estimate=cost(2 * rows * width * width * 4, 13e6),
        name="unit_grads",
    )(place, *lefts, right, tail)


def first_grad_kernel(inner_ref, w_ref, dz_ref, norm_ref, scale_ref, vec_ref, w_out_ref, out_ref, low_ref, ctx_ref, sum_ref):
    width = dz_ref.shape[1]
    grad = dz_ref[...]
    for unit in range(w_ref.shape[0]):
        grad += dot_nt(inner_ref[:, unit * width : (unit + 1) * width], w_ref[unit])
    normed = norm_ref[...]
    summed = norm_back(grad * vec_ref[1:2, :], normed, scale_ref[...])
    out_ref[...] = summed
    low = summed.astype(BF)
    low_ref[...] = low
    ctx_ref[...] = dot_nt(low, w_out_ref[0]).astype(BF)
    add_rows(sum_ref, (grad * normed, grad, low.astype(F32)))


def first_grad(inner, w_up, dz, norm_one, scale_one, vecs, w_qkvo, block=256):
    rows, width = dz.shape
    hidden = inner.shape[1]
    return pl.pallas_call(
        first_grad_kernel,
        grid=(rows // block,),
        in_specs=[
            rows_of(block, hidden),
            whole(w_up.shape),
            rows_of(block, width),
            rows_of(block, width),
            rows_of(block, 1),
            whole(vecs.shape),
            pl.BlockSpec((1, width, width), lambda i: (3, 0, 0)),
        ],
        out_specs=[rows_of(block, width), rows_of(block, width), rows_of(block, width), whole((8, width))],
        out_shape=[
            jax.ShapeDtypeStruct((rows, width), F32),
            jax.ShapeDtypeStruct((rows, width), BF),
            jax.ShapeDtypeStruct((rows, width), BF),
            jax.ShapeDtypeStruct((8, width), F32),
        ],
        compiler_params=params(),
        cost_estimate=cost(2 * rows * width * (hidden + width), 25e6),
        name="first_grad",
    )(inner, w_up, dz, norm_one, scale_one, vecs, w_qkvo)


def attention_backward_kernel(lengths, proj_ref, ctx_ref, lse_ref, out_ref, sum_ref):
    block, width = ctx_ref.shape
    step = pl.program_id(0)

    @pl.when(step == 0)
    def _():
        sum_ref[...] = jnp.zeros_like(sum_ref)

    masks = head_masks()
    lane = lax.broadcasted_iota(jnp.int32, (1, 2 * HD), 1)
    key = lax.broadcasted_iota(jnp.int32, (LEN, 1), 0)
    for seq in range(block // LEN):
        rows = slice(seq * LEN, (seq + 1) * LEN)
        valid = key < lengths[step * (block // LEN) + seq]
        for pair in range(width // (2 * HD)):
            at = pair * 2 * HD
            q = proj_ref[rows, at : at + 2 * HD] * BF(0.125)
            k = proj_ref[rows, width + at : width + at + 2 * HD]
            v = proj_ref[rows, 2 * width + at : 2 * width + at + 2 * HD]
            dctx = ctx_ref[rows, at : at + 2 * HD]
            keys = stack_heads(k, masks)
            scores = dot_nt(keys, q)
            dprobs = dot_nt(stack_heads(v, masks), dctx)
            probs, dscores = [], []
            for half in range(2):
                here = slice(half * LEN, (half + 1) * LEN)
                lse = lse_ref[seq, 2 * pair + half : 2 * pair + half + 1, :]
                prob = jnp.exp(jnp.where(valid, scores[here], -1e9) - lse)
                dprob = dprobs[here]
                inner = jnp.sum(prob * dprob, 0, keepdims=True)
                dscores.append((prob * (dprob - inner)).astype(BF))
                probs.append(prob.astype(BF))
            dv = dot_nn(jnp.concatenate(probs, axis=1), stack_heads(dctx, masks)).astype(BF)
            dk = dot_nn(jnp.concatenate(dscores, axis=1), stack_heads(q, masks)).astype(BF)
            dq = (dot_tn(jnp.concatenate(dscores, axis=0), keys) * 0.125).astype(BF)
            for offset, grad in ((0, dq), (width, dk), (2 * width, dv)):
                out_ref[rows, offset + at : offset + at + 2 * HD] = grad
                if offset != width:
                    sum_ref[0:1, offset + at : offset + at + 2 * HD] += jnp.sum(grad.astype(F32), 0, keepdims=True)


def attention_backward(lengths, proj, dctx, lse):
    rows, width = dctx.shape
    block = 2 * LEN
    return pl.pallas_call(
        attention_backward_kernel,
        grid_spec=pltpu.PrefetchScalarGridSpec(
            num_scalar_prefetch=1,
            grid=(rows // block,),
            in_specs=[
                rows_of(block, 3 * width),
                rows_of(block, width),
                pl.BlockSpec((block // LEN,) + lse.shape[1:], lambda i, *_: (i, 0, 0)),
            ],
            out_specs=[rows_of(block, 3 * width), whole((8, 3 * width))],
        ),
        out_shape=[jax.ShapeDtypeStruct((rows, 3 * width), BF), jax.ShapeDtypeStruct((8, 3 * width), F32)],
        compiler_params=params(),
        cost_estimate=cost(9e9, 12e6),
        name="attention_backward",
    )(lengths, proj, dctx, lse)


def input_grad_kernel(proj_ref, w_ref, dz_ref, out_ref):
    width = dz_ref.shape[1]
    grad = dz_ref[...]
    for unit in range(3):
        grad += dot_nt(proj_ref[:, unit * width : (unit + 1) * width], w_ref[unit])
    out_ref[...] = grad.astype(BF)


def input_grad(dproj, w_qkvo, dz, block=256):
    rows, width = dz.shape
    return pl.pallas_call(
        input_grad_kernel,
        grid=(rows // block,),
        in_specs=[rows_of(block, 3 * width), whole((3, width, width)), rows_of(block, width)],
        out_specs=rows_of(block, width),
        out_shape=jax.ShapeDtypeStruct((rows, width), BF),
        compiler_params=params(),
        cost_estimate=cost(6 * rows * width * width, 12e6),
        name="input_grad",
    )(dproj, w_qkvo, dz)


CORES = [(i, i ^ 1) for i in range(8)]


def from_core(value):
    return lax.ppermute(value, "shard", CORES)


def from_chip(value, ahead):
    return lax.ppermute(value, "shard", [((i + 2 * ahead) % 8, i) for i in range(8)])


def to_chip(value, ahead):
    return lax.ppermute(value, "shard", [(i, (i + 2 * ahead) % 8) for i in range(8)])


def from_rep(value, flip):
    return lax.ppermute(value, "rep", [(i, i ^ flip) for i in range(4)])


def joined(*parts):
    return jnp.concatenate(parts, 0)


def gather_units(place, own, direct, after=()):
    depth = own.shape[1]
    mine = lax.dynamic_index_in_dim(own, place[0], 0, keepdims=True)
    if after:
        mine = lax.optimization_barrier((mine,) + tuple(after))[0]
    hops = [from_chip(mine, ahead) for ahead in (1, 2, 3)]
    got = joined(*hops)
    pieces, plan = [own], [[(unit, False, 0, 0, 0, depth, depth) for unit in range(4)]]

    def entries(flips, first, count):
        return [(flip, True, 0, ahead, first, count, depth) for flip in flips for ahead in (1, 2, 3)]

    if direct:
        for flip in range(4):
            pieces.append(from_rep(got, flip) if flip else got)
            plan.append(entries((flip,), 0, depth))
    else:
        half = depth // 2
        low, high = got[:, :half], got[:, half:]
        low = joined(low, from_rep(low, 1))
        high = joined(high, from_rep(high, 2))
        pieces += [low, from_rep(low, 2), high, from_rep(high, 1)]
        plan += [entries((0, 1), 0, half), entries((2, 3), 0, half), entries((0, 2), half, half), entries((1, 3), half, half)]
    pieces += [from_core(piece) for piece in pieces]
    plan += [[entry[:2] + (1,) + entry[3:] for entry in listed] for listed in plan]
    return (plan, pieces), hops


def scatter_units(keep, send, order):
    one, two = order
    other = from_core(send).astype(F32)
    keep = keep.astype(F32) + other
    away = joined(keep[one : one + 1], keep[3:4]).astype(BF)
    got = from_rep(away, one).astype(F32)
    got = from_rep((keep[two] + got[1]).astype(BF), two).astype(F32) + (keep[0] + got[0])
    low = got.astype(BF)
    total = got[0]
    for ahead in (1, 2, 3):
        total = total + to_chip(low[ahead], ahead).astype(F32)
    return share_units(total.astype(BF)[None])


def share_units(own):
    pair = joined(own, from_rep(own, 1))
    return joined(pair, from_rep(pair, 2))


def natural_units(place, units):
    rep = place[0]
    units = jnp.where(rep & 1 == 1, units[jnp.array([1, 0, 3, 2])], units)
    return jnp.where(rep & 2 == 2, units[jnp.array([2, 3, 0, 1])], units)


def per_device(mesh_shape, *arrays):
    (tokens, cotangent, task, lengths, task_masks, w_qkv, qv_bias, w_out, out_bias, ln1_gain, ln1_bias, w_up, up_bias, w_down, down_bias, ln2_gain, ln2_bias) = arrays
    rows, width = tokens.shape
    shards = mesh_shape["shard"]
    hidden = up_bias.shape[0] * shards
    fast = shards == 8 and mesh_shape["rep"] == 4
    place = jnp.stack([lax.axis_index("rep"), lax.axis_index("shard") // 2, lax.axis_index("shard") % 2]).astype(jnp.int32)
    shard = lax.axis_index("shard")

    vectors = (qv_bias, out_bias, ln1_gain, ln1_bias, down_bias, ln2_gain, ln2_bias, up_bias)
    sizes = [v.shape[0] for v in vectors]
    packed = jnp.concatenate(vectors)

    if fast:
        depth = w_qkv.shape[0]
        own_a = jnp.concatenate([w_qkv.reshape(depth, 3, width), w_out.reshape(depth, 1, width)], 1).transpose(1, 0, 2)
        own_b = w_up.reshape(depth, 4, width).transpose(1, 0, 2)
        weight_a, hops = gather_units(place, own_a, True)
        packed_rows = jnp.pad(packed, (0, 16 * width - packed.shape[0])).reshape(1, 16, width)
        vec_rows = joined(packed_rows, *[from_chip(packed_rows, ahead) for ahead in (1, 2, 3)])
        vec_rows = jnp.stack([vec_rows, from_core(vec_rows)], 1).reshape(8, -1)[:, : packed.shape[0]]
        index = jnp.arange(8)
        slot = 2 * ((index // 2 - place[1]) % 4) + ((index % 2) ^ place[2])
        pick = (slot[:, None] == index[None, :]).astype(BF)
        all_vectors = jnp.dot(pick, vec_rows, preferred_element_type=F32)
        weight_b, hops_b = gather_units(place, own_b, False, hops)
        down_full = lax.all_gather(lax.optimization_barrier((w_down,) + tuple(hops))[0], "shard", axis=0, tiled=True)
    else:
        all_vectors = lax.all_gather(packed, "shard", axis=0).astype(F32)
        full_a = jnp.concatenate([lax.all_gather(w_qkv, "shard", axis=0, tiled=True), lax.all_gather(w_out, "shard", axis=0, tiled=True)], 1)
        full_b = lax.all_gather(w_up, "shard", axis=0, tiled=True)
        whole_plan = [[(unit, False, 0, 0, 0, width, 0) for unit in range(4)]]
        weight_a = (whole_plan, [full_a.reshape(width, 4, width).transpose(1, 0, 2)])
        weight_b = (whole_plan, [full_b.reshape(width, 4, width).transpose(1, 0, 2)])
        down_full = lax.all_gather(w_down, "shard", axis=0, tiled=True)

    full, start = [], 0
    for size in sizes:
        full.append(all_vectors[:, start : start + size].reshape(-1))
        start += size
    qv, out_shift, gain_one, shift_one, down_shift, gain_two, shift_two, up_shift = full
    qkv_shift = jnp.concatenate([qv[:width], jnp.zeros((width,), F32), qv[width:]])[None]
    vecs = jnp.stack([out_shift, gain_one, shift_one, down_shift, gain_two, shift_two, shift_two, shift_two])
    up_shift = up_shift[None]

    position = jnp.arange(LEN, dtype=jnp.int32)
    token_task = jnp.repeat(task, LEN)
    chosen = jnp.where(token_task == 0, task_masks[0], jnp.where(token_task == 1, task_masks[1], task_masks[2]))
    row_weight = chosen * (position[None, :] < lengths[:, None]).astype(jnp.int32).reshape(rows)
    row_weight = row_weight.astype(F32)[:, None]

    proj, context, lse, w_a = attention_forward(place, lengths, tokens, qkv_shift, weight_a)
    norm_one, scale_one, first_low, act, slope, w_b = middle(place, tokens, context, w_a, vecs, up_shift, weight_b)
    output, dz_two, dffn, sums_two = ffn_out(act, down_full, norm_one, cotangent, row_weight, vecs)
    grads_c = grad_down_natural(dffn, act, shards)
    dinner, sums_up = inner_grad(dffn, down_full, slope)
    grads_b = unit_grads(place, (first_low,), dinner, dffn, fast)
    dz_one, dattended, dcontext, sums_one = first_grad(dinner, w_b, dz_two, norm_one, scale_one, vecs, w_a)
    dproj, sums_qkv = attention_backward(lengths, proj, dcontext, lse)
    grads_a = unit_grads(place, (tokens, context), dproj, dattended, fast)
    grad_input = input_grad(dproj, w_a, dz_one)

    grad_vectors = (jnp.concatenate([sums_qkv[0, :width], sums_qkv[0, 2 * width :]]), sums_one[2], sums_one[0], sums_one[1], sums_two[2], sums_two[0], sums_two[1], sums_up[0])
    table = jnp.concatenate([g.reshape(shards, -1) for g in grad_vectors], 1)
    table = lax.psum(table, ("rep", "shard"))
    mine = lax.dynamic_index_in_dim(table, shard, 0, keepdims=False)
    final, start = [], 0
    for size in sizes:
        final.append(mine[start : start + size])
        start += size
    f_qv, f_out_shift, f_gain_one, f_shift_one, f_down_shift, f_gain_two, f_shift_two, f_up_shift = final

    final_c = lax.psum_scatter(grads_c, "shard", scatter_dimension=0, tiled=True)
    final_c = lax.psum(final_c.astype(BF), "rep").astype(F32)[0].T
    if fast:
        units_b = natural_units(place, scatter_units(*grads_b, (2, 1)))
        units_a = natural_units(place, scatter_units(*grads_a, (1, 2)))
    else:
        units = []
        for (grads,) in (grads_b, grads_a):
            summed = lax.psum_scatter(grads, "shard", scatter_dimension=1, tiled=True)
            units.append(lax.psum(summed.astype(BF), "rep"))
        units_b, units_a = units
    wide_b = units_b.astype(F32).transpose(1, 0, 2).reshape(-1, hidden)
    wide_a = units_a[:3].astype(F32).transpose(1, 0, 2).reshape(-1, 3 * width)
    return (output, grad_input, wide_a, f_qv, units_a[3].astype(F32), f_out_shift, f_gain_one, f_shift_one, wide_b, f_up_shift, final_c, f_down_shift, f_gain_two, f_shift_two)


def solution(mesh):
    split, shard = P(("rep", "shard"), None), P("shard")
    flat, matrix = P(("rep", "shard")), P("shard", None)
    in_specs = (split, split, flat, flat, P(None, ("rep", "shard")), matrix, shard, matrix, shard, shard, shard, matrix, shard, matrix, shard, shard, shard)
    out_specs = (split, split, matrix, shard, matrix, shard, shard, shard, matrix, shard, matrix, shard, shard, shard)
    return jax.shard_map(
        functools.partial(per_device, dict(mesh.shape)), mesh=mesh, in_specs=in_specs, out_specs=out_specs, check_vma=False
    )
```

```python
import functools
import math

import jax
import jax.numpy as jnp
from jax import lax
from jax.experimental import pallas as pl
from jax.experimental.pallas import tpu as pltpu
from jax.sharding import PartitionSpec as P

HD = 64
LEN = 128
EPSILON = 1e-06
BF = jnp.bfloat16
F32 = jnp.float32
MIB = 1024 * 1024

ROOT_HALF = 0.7071067811865476
DENSITY = 0.3989422804014327


def dot_nn(left, right):
    return jnp.dot(left, right, preferred_element_type=F32)


def dot_nt(left, right):
    return lax.dot_general(left, right, (((1,), (1,)), ((), ())), preferred_element_type=F32)


def dot_tn(left, right):
    return lax.dot_general(left, right, (((0,), (0,)), ((), ())), preferred_element_type=F32)


def gelu_parts(inner):
    phi = 0.5 + 0.5 * lax.erf(inner * ROOT_HALF)
    bell = jnp.exp(inner * inner * -0.5) * DENSITY
    return inner * phi, phi + inner * bell


def norm_parts(summed):
    centre = jnp.mean(summed, -1, keepdims=True)
    deviation = summed - centre
    variance = jnp.mean(deviation * deviation, -1, keepdims=True)
    rscale = lax.rsqrt(variance + EPSILON)
    return deviation * rscale, rscale


def norm_back(grad_norm, normed, rscale):
    first_mean = jnp.mean(grad_norm, -1, keepdims=True)
    second_mean = jnp.mean(grad_norm * normed, -1, keepdims=True)
    return rscale * (grad_norm - first_mean - normed * second_mean)


def add_rows(total_ref, rows):
    @pl.when(pl.program_id(0) == 0)
    def _():
        total_ref[...] = jnp.zeros_like(total_ref)

    for at, values in enumerate(rows):
        total_ref[at : at + 1, :] += jnp.sum(values, 0, keepdims=True)


def cost(flops, moved):
    return pl.CostEstimate(flops=1000, bytes_accessed=1000, transcendentals=0)


def params(vmem=48):
    return pltpu.CompilerParams(vmem_limit_bytes=vmem * MIB)


def rows_at(step, block):
    return pl.ds(pl.multiple_of(step * block, block), block)


def whole(shape):
    return pl.BlockSpec(shape, lambda i, *_: (0,) * len(shape))


def rows_of(block, width):
    return pl.BlockSpec((block, width), lambda i, *_: (i, 0))


def head_masks():
    lane = lax.broadcasted_iota(jnp.int32, (1, 2 * HD), 1)
    return (lane < HD).astype(BF), (lane >= HD).astype(BF)


def stack_heads(pair, masks):
    return jnp.concatenate([pair * masks[0], pair * masks[1]], axis=0)


def attention_forward_kernel(plan, count_of_pieces, place, lengths, x_ref, shift_ref, *refs):
    pieces, (proj_ref, ctx_ref, lse_ref, w_out_ref, w_ref, sems) = refs[: count_of_pieces], refs[count_of_pieces :]
    block, width = x_ref.shape
    step = pl.program_id(0)

    def body(ready):
        x = x_ref[...]
        for i in range(4):
            unit = ready(i)

            @pl.when(unit < 3)
            def _():
                at = pl.ds(pl.multiple_of(unit * width, width), width)
                proj_ref[:, at] = (dot_nn(x, w_ref[unit]) + shift_ref[:, at]).astype(BF)

        masks = head_masks()
        lane = lax.broadcasted_iota(jnp.int32, (1, LEN), 1)
        for seq in range(block // LEN):
            number = step * (block // LEN) + seq
            rows = slice(seq * LEN, (seq + 1) * LEN)
            valid = lane < lengths[number]
            lse = jnp.zeros((LEN, LEN), F32)
            for pair in range(width // (2 * HD)):
                at = pair * 2 * HD
                q = proj_ref[rows, at : at + 2 * HD] * BF(0.125)
                k = proj_ref[rows, width + at : width + at + 2 * HD]
                v = proj_ref[rows, 2 * width + at : 2 * width + at + 2 * HD]
                scores = dot_nt(q, stack_heads(k, masks))
                probs = []
                for half in range(2):
                    masked = jnp.where(valid, scores[:, half * LEN : (half + 1) * LEN], -1e9)
                    top = jnp.max(masked, -1, keepdims=True)
                    exponent = jnp.exp(masked - top)
                    total = jnp.sum(exponent, -1, keepdims=True)
                    probs.append((exponent * (1.0 / total)).astype(BF))
                    lse = jnp.where(lane == 2 * pair + half, top + jnp.log(total), lse)
                ctx = dot_nn(jnp.concatenate(probs, axis=1), stack_heads(v, masks))
                ctx_ref[rows, at : at + 2 * HD] = ctx.astype(BF)
            lse_ref[seq] = lse.T[: lse_ref.shape[1]]

    first_and_later(Bring(plan, place, pieces, w_ref, sems, w_out_ref=w_out_ref), body)


SWAPPED = (0, 2, 1, 3)


def flip_of(position, core):
    return {0: 0, 1: 1 + core, 2: 2 - core, 3: 3}[position]


class Bring:
    def __init__(self, plan, place, pieces, w_ref, sems, rows_first=False, w_out_ref=None):
        self.kind, self.entries = plan
        self.place, self.pieces = place, pieces
        self.w_ref, self.w_out_ref, self.sems, self.rows_first = w_ref, w_out_ref, sems, rows_first
        self.span = w_ref.shape[0] // 4

    def part(self, ref, at):
        return ref.at[rows_at(at, self.span)] if self.rows_first else ref.at[at]

    def unit(self, position, other):
        rep, core = self.place[0], self.place[2]
        return rep ^ (position if self.kind == "direct" else flip_of(position, core ^ other))

    def round(self, i):
        if self.kind == "whole":
            return i
        return (self.place[1] + i) % 4 if self.rows_first else self.unit(i, 0)

    def start(self):
        if self.kind == "whole":
            for at in range(4):
                pltpu.make_async_copy(self.pieces[0].at[at], self.part(self.w_ref, at), self.sems.at[at]).start()
            return
        chip, core = self.place[1], self.place[2]
        for piece, at, unit, position, ahead, depth, other in self.entries:
            to_unit = unit if position is None else self.unit(position, other)
            to_chip = (chip + ahead) % 4
            shard = 2 * to_chip + (core ^ other)
            if self.rows_first:
                first = 4 * shard if to_unit is None else 4 * shard + to_unit
                count = 4 * depth if to_unit is None else depth
                group, to = to_chip, self.w_ref.at[pl.ds(pl.multiple_of(first * depth, 16), count)]
            else:
                group, to = to_unit, self.w_ref.at[to_unit, pl.ds(pl.multiple_of(shard * depth, 16), depth)]
            pltpu.make_async_copy(self.pieces[piece].at[at], to, self.sems.at[group]).start()

    def wait(self, at):
        here = self.part(self.w_ref, at)
        pltpu.make_async_copy(here, here, self.sems.at[at]).wait()
        if self.w_out_ref is not None:
            self.onward(at).start()

    def onward(self, at):
        return pltpu.make_async_copy(self.part(self.w_ref, at), self.part(self.w_out_ref, at), self.sems.at[4 + at])

    def finish(self):
        for at in range(4):
            self.onward(at).wait()


def first_and_later(bring, body):
    @pl.when(pl.program_id(0) == 0)
    def _():
        bring.start()

        def ready(i):
            at = bring.round(i)
            bring.wait(at)
            return at

        body(ready)

    @pl.when(pl.program_id(0) > 0)
    def _():
        body(bring.round)

    if bring.w_out_ref is not None:

        @pl.when(pl.program_id(0) == pl.num_programs(0) - 1)
        def _():
            bring.finish()


ANY = pl.BlockSpec(memory_space=pl.ANY)
HELD = pl.BlockSpec(memory_space=pltpu.VMEM)
FAR = pl.BlockSpec(memory_space=pl.ANY)


def call(kernel, in_specs, out_specs, out_shape, grid, scalars, scratch_shapes, vmem, name):
    def space(spec, shape, result):
        large = math.prod(shape.shape) * shape.dtype.itemsize > MIB // 2
        if spec is HELD:
            return pltpu.VMEM
        return pltpu.HBM if spec is FAR or large and (result or spec is not ANY) else None

    def placed(spec, shape):
        where = space(spec, shape, True)
        return shape if where is None else where(shape.shape, shape.dtype)

    run = pl.pallas_call(
        kernel,
        grid_spec=pltpu.PrefetchScalarGridSpec(
            num_scalar_prefetch=scalars, grid=grid, in_specs=in_specs, out_specs=out_specs, scratch_shapes=scratch_shapes
        ),
        out_shape=[placed(spec, shape) for spec, shape in zip(out_specs, out_shape)],
        compiler_params=params(vmem),
        cost_estimate=cost(0, 0),
        name=name,
    )

    def constrained(spec, arg):
        where = space(spec, arg, False)
        return arg if where is None else pltpu.with_memory_space_constraint(arg, where)

    def apply(*args):
        return run(*args[:scalars], *[constrained(spec, arg) for spec, arg in zip(in_specs, args[scalars:])])

    return apply


WHOLE = ("whole", ())


def attention_forward(place, lengths, tokens, shift, weight):
    rows, width = tokens.shape
    block = 2 * LEN
    heads = width // HD
    lse_rows = -(-heads // 8) * 8
    plan, pieces = weight
    return call(
        functools.partial(attention_forward_kernel, plan, len(pieces)),
        in_specs=[rows_of(block, width), whole((1, 3 * width))] + [ANY] * len(pieces),
        out_specs=[
            rows_of(block, 3 * width),
            rows_of(block, width),
            pl.BlockSpec((block // LEN, lse_rows, LEN), lambda i, *_: (i, 0, 0)),
            ANY,
        ],
        out_shape=[
            jax.ShapeDtypeStruct((rows, 3 * width), BF),
            jax.ShapeDtypeStruct((rows, width), BF),
            jax.ShapeDtypeStruct((rows // LEN, lse_rows, LEN), F32),
            jax.ShapeDtypeStruct((4, width, width), BF),
        ],
        grid=(rows // block,),
        scalars=2,
        scratch_shapes=[pltpu.VMEM((4, width, width), BF), pltpu.SemaphoreType.DMA((8,))],
        vmem=20,
        name="attention_forward",
    )(place, lengths, tokens, shift, *pieces)


def middle_kernel(plan, count_of_pieces, place, x_ref, ctx_ref, w_attn_ref, vec_ref, up_shift_ref, *refs):
    pieces = refs[: count_of_pieces]
    norm_ref, scale_ref, low_ref, act_ref, slope_ref, w_out_ref, w_ref, sems = refs[count_of_pieces :]
    block, width = x_ref.shape
    here = rows_at(pl.program_id(0), block)

    def body(ready):
        attended = dot_nn(ctx_ref[...], w_attn_ref[0]) + vec_ref[0:1, :]
        normed, rscale = norm_parts(x_ref[...].astype(F32) + attended)
        norm_ref[...] = normed.astype(BF)
        scale_ref[...] = rscale
        low = (normed * vec_ref[1:2, :] + vec_ref[2:3, :]).astype(BF)
        low_ref[...] = low
        for i in range(w_ref.shape[0]):
            unit = ready(i)
            at = pl.ds(pl.multiple_of(unit * width, width), width)
            act, slope = gelu_parts(dot_nn(low, w_ref[unit]) + up_shift_ref[:, at])
            act_ref[here, at] = act.astype(BF)
            slope_ref[:, at] = slope.astype(BF)

    first_and_later(Bring(plan, place, pieces, w_ref, sems, w_out_ref=w_out_ref), body)


def middle(place, tokens, context, w_qkvo, vecs, up_shift, weight, block=256):
    rows, width = tokens.shape
    hidden = up_shift.shape[1]
    units = hidden // width
    plan, pieces = weight
    return call(
        functools.partial(middle_kernel, plan, len(pieces)),
        in_specs=[
                rows_of(block, width),
                rows_of(block, width),
                pl.BlockSpec((1, width, width), lambda i, *_: (3, 0, 0)),
                whole(vecs.shape),
                whole(up_shift.shape),
            ]
            + [ANY] * len(pieces),
        out_specs=[rows_of(block, width), rows_of(block, 1), rows_of(block, width), HELD, rows_of(block, hidden), ANY],
        out_shape=[
            jax.ShapeDtypeStruct((rows, width), BF),
            jax.ShapeDtypeStruct((rows, 1), F32),
            jax.ShapeDtypeStruct((rows, width), BF),
            jax.ShapeDtypeStruct((rows, hidden), BF),
            jax.ShapeDtypeStruct((rows, hidden), BF),
            jax.ShapeDtypeStruct((units, width, width), BF),
        ],
        grid=(rows // block,),
        scalars=1,
        scratch_shapes=[pltpu.VMEM((units, width, width), BF), pltpu.SemaphoreType.DMA((8,))],
        vmem=24,
        name="middle",
    )(place, tokens, context, w_qkvo, vecs, up_shift, *pieces)


def ffn_kernel(plan, count_of_pieces, relative, place, act_ref, norm_ref, cot_ref, weight_ref, vec_ref, *refs):
    pieces, refs = refs[: count_of_pieces], refs[count_of_pieces :]
    out_ref, low_ref, sum_ref, w_out_ref, *refs = refs
    outs, refs = refs[: 2 if relative else 1], refs[2 if relative else 1 :]
    turned_ref, w_ref, stage_ref, sems, w_sems = refs
    step = pl.program_id(0)
    block, width = cot_ref.shape
    count = act_ref.shape[0] // block
    here = rows_at(jnp.minimum(step, count - 1), block)
    bring = Bring(plan, place, pieces, w_ref, w_sems, rows_first=True, w_out_ref=w_out_ref)

    def finish(ffn):
        first = norm_ref[...].astype(F32) * vec_ref[1:2, :] + vec_ref[2:3, :]
        normed, rscale = norm_parts(first + (ffn + vec_ref[3:4, :]))
        out_ref[...] = (normed * vec_ref[4:5, :] + vec_ref[5:6, :]).astype(BF)
        grad = cot_ref[...].astype(F32) * weight_ref[...]
        low = norm_back(grad * vec_ref[4:5, :], normed, rscale).astype(BF)
        low_ref[here, :] = low
        turned_ref[:, here] = low.T
        for at, values in enumerate((grad * normed, grad, low.astype(F32))):
            sum_ref[at : at + 1, :] += jnp.sum(values, 0, keepdims=True)

    @pl.when(step == 0)
    def _():
        bring.start()
        sum_ref[...] = jnp.zeros_like(sum_ref)
        ffn = 0.0
        for i in range(4):
            part = bring.round(i)
            bring.wait(part)
            at = rows_at(part, bring.span)
            ffn = ffn + dot_nn(act_ref[here, at], w_ref[at, :])
        finish(ffn)

    @pl.when((step > 0) & (step < count))
    def _():
        finish(dot_nn(act_ref[here, :], w_ref[...]))

    def left(slot):
        here = stage_ref.at[slot]
        pltpu.make_async_copy(here, here, sems.at[slot]).wait()

    if relative:

        @pl.when(step >= count + 2)
        def _():
            left(step % 2)

    @pl.when(step >= count)
    def _():
        at = step - count
        columns = pl.ds(pl.multiple_of(at * width, width), width)
        grad = dot_nn(turned_ref[...], act_ref[:, columns]).astype(BF)
        if not relative:
            each, _, part = outs[0].shape
            for i in range(each):
                outs[0][i] = grad[:, i * part : (i + 1) * part]
            return
        rep, chip, core = place[0], place[1], place[2]
        part, depth = width // 2, width // 4
        slot = step % 2
        for half in range(2):
            stage_ref[slot, half] = grad[:, half * part : (half + 1) * part]
        ahead = (at - chip) % 4
        for unit in range(4):
            rows = pl.ds(unit * depth, depth)
            for ref, whose in zip(outs, (core, 1 - core)):
                to = pl.multiple_of((4 * slot_of(unit, rep, whose) + ahead) * depth, 16)
                pltpu.make_async_copy(stage_ref.at[slot, whose, rows], ref.at[pl.ds(to, depth)], sems.at[slot]).start()

    @pl.when(step == pl.num_programs(0) - 1)
    def _():
        bring.finish()
        if relative:
            left(0)
            left(1)


def once(shape):
    return pl.BlockSpec(shape, lambda i, *_: (0,) * len(shape), pipeline_mode=pl.Buffered(1))


def ffn(place, act, weight, norm_one, cotangent, row_weight, vecs, shards, relative, block=256):
    rows, width = cotangent.shape
    hidden = act.shape[1]
    part = hidden // shards
    each = width // part
    count = rows // block
    plan, pieces = weight
    if relative:
        out_specs = [ANY] * 2
        out_shape = [jax.ShapeDtypeStruct((4 * width, part), BF)] * 2
    else:
        out_specs = [pl.BlockSpec((each, width, part), lambda i, *_: (jnp.maximum(i - count, 0), 0, 0))]
        out_shape = [jax.ShapeDtypeStruct((shards, width, part), BF)]
    early = lambda columns: pl.BlockSpec((block, columns), lambda i, *_: (jnp.minimum(i, count - 1), 0))
    output, low, sums, w_down, *grads = call(
        functools.partial(ffn_kernel, plan, len(pieces), relative),
        in_specs=[HELD, early(width), early(width), early(1), whole(vecs.shape)] + [ANY] * len(pieces),
        out_specs=[early(width), HELD, whole((8, width)), ANY] + out_specs,
        out_shape=[
            jax.ShapeDtypeStruct((rows, width), BF),
            jax.ShapeDtypeStruct((rows, width), BF),
            jax.ShapeDtypeStruct((8, width), F32),
            jax.ShapeDtypeStruct((hidden, width), BF),
        ]
        + out_shape,
        grid=(count + shards // each,),
        scalars=1,
        scratch_shapes=[
            pltpu.VMEM((width, rows), BF),
            pltpu.VMEM((hidden, width), BF),
            pltpu.VMEM((2, 2, width, width // 2), BF),
            pltpu.SemaphoreType.DMA((2,)),
            pltpu.SemaphoreType.DMA((8,)),
        ],
        vmem=24,
        name="ffn",
    )(place, act, norm_one, cotangent, row_weight, vecs, *pieces)
    return output, low, sums, w_down, grads


class Outward:
    def __init__(self, stage_ref, sems):
        self.step = pl.program_id(0)
        self.slot = self.step % 2
        self.stage_ref, self.sems = stage_ref, sems

    def free(self):
        @pl.when(self.step >= 2)
        def _():
            self.wait(self.slot)

    def stage(self):
        return self.stage_ref.at[self.slot]

    def send(self, *pairs):
        for source, to in pairs:
            pltpu.make_async_copy(source, to, self.sems.at[self.slot]).start()

    def wait(self, slot):
        here = self.stage_ref.at[slot]
        pltpu.make_async_copy(here, here, self.sems.at[slot]).wait()

    def finish(self):
        @pl.when(self.step == pl.num_programs(0) - 1)
        def _():
            self.wait(1 - self.slot)
            self.wait(self.slot)


def slot_of(unit, rep, core):
    e = unit ^ rep
    return jnp.where(core == 0, 2 * (e % 2) + e // 2, e)


def send_units(place, grad, out, outs, extra, unit=None):
    rep, chip, core = place[0], place[1], place[2]
    depth = grad.shape[0] // 8
    unit = pl.program_id(0) if unit is None else unit
    stage = out.stage()
    stage[...] = grad
    for ref, whose in zip(outs, (core, 1 - core)):
        slot = slot_of(unit, rep, whose)
        for other in range(4):
            ahead = (other - chip) % 4
            to = pl.multiple_of((4 * slot + ahead) * depth + jnp.where(slot >= 2, extra, 0), 16)
            row = pl.multiple_of((2 * other + whose) * depth, 16)
            out.send((stage.at[pl.ds(row, depth)], ref.at[pl.ds(to, depth)]))


def inner_grads_kernel(relative, place, low_ref, w_ref, slope_ref, first_hbm_ref, inner_ref, sum_ref, *refs):
    outs, refs = refs[: 2 if relative else 1], refs[2 if relative else 1 :]
    first_ref, turned_ref, stage_ref, sems, sem = refs
    step = pl.program_id(0)
    rows, width = low_ref.shape
    bring = pltpu.make_async_copy(first_hbm_ref, first_ref, sem)

    @pl.when(step == 0)
    def _():
        bring.start()

    total = 0.0
    for at in range(0, rows, 256):
        here = slice(at, at + 256)
        grad = (dot_nt(low_ref[here, :], w_ref[...]) * slope_ref[here, :].astype(F32)).astype(BF)
        inner_ref[here, :] = grad
        total = total + jnp.sum(grad.astype(F32), 0, keepdims=True)
    sum_ref[0:1, :] = total

    @pl.when(step == 0)
    def _():
        bring.wait()
        turned_ref[...] = first_ref[...].T

    grad = dot_nn(turned_ref[...], inner_ref[...]).astype(BF)
    if relative:
        out = Outward(stage_ref, sems)
        out.free()
        send_units(place, grad, out, outs, 0)
        out.finish()
    else:
        outs[0][0] = grad


def inner_grads(place, low, first, w_down, slope, relative):
    rows, width = low.shape
    hidden = slope.shape[1]
    columns = lambda height: pl.BlockSpec((height, width), lambda i, place: (0, i))
    if relative:
        out_specs = [ANY] * 2
        out_shape = [jax.ShapeDtypeStruct((2 * width, width), BF)] * 2
    else:
        out_specs = [pl.BlockSpec((1, width, width), lambda i, place: (i, 0, 0))]
        out_shape = [jax.ShapeDtypeStruct((4, width, width), BF)]
    inner, sums, *grads = call(
        functools.partial(inner_grads_kernel, relative),
        in_specs=[HELD, pl.BlockSpec((width, width), lambda i, place: (i, 0)), columns(rows), FAR],
        out_specs=[columns(rows), columns(8)] + out_specs,
        out_shape=[jax.ShapeDtypeStruct((rows, hidden), BF), jax.ShapeDtypeStruct((8, hidden), F32)] + out_shape,
        grid=(hidden // width,),
        scalars=1,
        scratch_shapes=[
            pltpu.VMEM((rows, width), BF),
            pltpu.VMEM((width, rows), BF),
            pltpu.VMEM((2, width, width), BF),
            pltpu.SemaphoreType.DMA((2,)),
            pltpu.SemaphoreType.DMA,
        ],
        vmem=32,
        name="inner_grads",
    )(place, low, w_down, slope, first)
    return inner, sums, grads


def first_grad_kernel(inner_ref, w_hbm_ref, low_in_ref, norm_ref, scale_ref, vec_ref, w_attn_ref, low_ref, ctx_ref, sum_ref, w_ref, sems):
    block, width = norm_ref.shape
    here = rows_at(pl.program_id(0), block)

    def body(ready):
        grad = low_in_ref[here, :].astype(F32)
        for unit in range(4):
            ready(unit)
            grad += dot_nt(inner_ref[:, unit * width : (unit + 1) * width], w_ref[unit])
        normed = norm_ref[...].astype(F32)
        low = norm_back(grad * vec_ref[1:2, :], normed, scale_ref[...]).astype(BF)
        low_ref[here, :] = low
        ctx_ref[here, :] = dot_nt(low, w_attn_ref[0]).astype(BF)
        add_rows(sum_ref, (grad * normed, grad, low.astype(F32)))

    first_and_later(Bring(WHOLE, (0, 0, 0), [w_hbm_ref], w_ref, sems), body)


def first_grad(inner, w_up, low, norm_one, scale_one, vecs, w_qkvo, block=256):
    rows, width = low.shape
    hidden = inner.shape[1]
    return call(
        first_grad_kernel,
        in_specs=[
            rows_of(block, hidden),
            FAR,
            HELD,
            rows_of(block, width),
            rows_of(block, 1),
            whole(vecs.shape),
            pl.BlockSpec((1, width, width), lambda i: (3, 0, 0)),
        ],
        out_specs=[HELD, HELD, whole((8, width))],
        out_shape=[
            jax.ShapeDtypeStruct((rows, width), BF),
            jax.ShapeDtypeStruct((rows, width), BF),
            jax.ShapeDtypeStruct((8, width), F32),
        ],
        grid=(rows // block,),
        scalars=0,
        scratch_shapes=[pltpu.VMEM(w_up.shape, BF), pltpu.SemaphoreType.DMA((4,))],
        vmem=28,
        name="first_grad",
    )(inner, w_up, low, norm_one, scale_one, vecs, w_qkvo)


def attention_back_kernel(relative, place, lengths, proj_ref, dctx_ref, lse_ref, pre_ref, attn_ref, x_hbm_ref, ctx_hbm_ref, held_ref, *refs):
    outs, refs = refs[: 2 if relative else 1], refs[2 if relative else 1 :]
    sum_ref, x_ref, ctx_ref, turned_ref, stage_ref, sums_ref, sems, sum_sems, late_sem = refs
    step = pl.program_id(0)
    width = dctx_ref.shape[1]
    block = 2 * LEN
    count = held_ref.shape[0] // block
    extra = sums_ref.shape[0]
    late = pltpu.make_async_copy(x_hbm_ref, x_ref, late_sem.at[0])
    late_ctx = pltpu.make_async_copy(ctx_hbm_ref, ctx_ref, late_sem.at[1])

    @pl.when(step == 0)
    def _():
        sum_ref[...] = jnp.zeros_like(sum_ref)
        late.start()
        late_ctx.start()

    @pl.when(step == 1)
    def _():
        late.wait()
        turned_ref[...] = x_ref[...].T

    @pl.when(step < count)
    def _():
        masks = head_masks()
        lane = lax.broadcasted_iota(jnp.int32, (1, 2 * HD), 1)
        key = lax.broadcasted_iota(jnp.int32, (LEN, 1), 0)
        for seq in range(block // LEN):
            number = step * (block // LEN) + seq
            rows = rows_at(number, LEN)
            here_rows = slice(seq * LEN, (seq + 1) * LEN)
            valid = key < lengths[number]
            for pair in range(width // (2 * HD)):
                at = pair * 2 * HD
                q = proj_ref[here_rows, at : at + 2 * HD] * BF(0.125)
                k = proj_ref[here_rows, width + at : width + at + 2 * HD]
                v = proj_ref[here_rows, 2 * width + at : 2 * width + at + 2 * HD]
                dctx = dctx_ref[rows, at : at + 2 * HD]
                queries, grads = stack_heads(q, masks), stack_heads(dctx, masks)
                scores = dot_nt(k, queries)
                dprobs = dot_nt(v, grads)
                probs, dscores = [], []
                for half in range(2):
                    here = slice(half * LEN, (half + 1) * LEN)
                    lse = lse_ref[seq, 2 * pair + half : 2 * pair + half + 1, :]
                    prob = jnp.exp(jnp.where(valid, scores[:, here], -1e9) - lse)
                    dprob = dprobs[:, here]
                    inner = jnp.sum(prob * dprob, 0, keepdims=True)
                    dscores.append((prob * (dprob - inner)).astype(BF))
                    probs.append(prob.astype(BF))
                dv = dot_nn(jnp.concatenate(probs, axis=1), grads).astype(BF)
                dk = dot_nn(jnp.concatenate(dscores, axis=1), queries).astype(BF)
                turned = jnp.concatenate([dscore.T for dscore in dscores], axis=1)
                dq = (dot_nn(turned, stack_heads(k, masks)) * 0.125).astype(BF)
                for offset, grad in ((0, dq), (width, dk), (2 * width, dv)):
                    held_ref[rows, offset + at : offset + at + 2 * HD] = grad
                    if offset != width:
                        sum_ref[0:1, offset + at : offset + at + 2 * HD] += jnp.sum(grad.astype(F32), 0, keepdims=True)
    if relative:
        out = Outward(stage_ref, sems)
        copies = [
            pltpu.make_async_copy(sums_ref, ref.at[pl.ds(width, extra)], sum_sems.at[i])
            for i, ref in enumerate(outs)
        ]

        @pl.when(step == count)
        def _():
            sums_ref[...] = pre_ref[...]
            sums_ref[0:1, :] = sum_ref[0:1, :width].astype(BF)
            sums_ref[1:2, :] = sum_ref[0:1, 2 * width :].astype(BF)
            for copy in copies:
                copy.start()

    def put(unit, grad):
        if not relative:
            outs[0][0] = grad
            return

        @pl.when(step >= count + 2)
        def _():
            out.wait(out.slot)

        send_units(place, grad, out, outs, extra, unit)

    for unit in range(3):

        @pl.when(step == count + unit)
        def _():
            put(unit, dot_nn(turned_ref[...], held_ref[:, unit * width : (unit + 1) * width]).astype(BF))

    @pl.when(step == count + 3)
    def _():
        late_ctx.wait()
        turned_ref[...] = ctx_ref[...].T
        put(3, dot_nn(turned_ref[...], attn_ref[...]).astype(BF))
        if relative:
            for copy in copies:
                copy.wait()

    if relative:
        out.finish()


def attention_back(place, lengths, proj, dctx, lse, tokens, context, dattended, pre, relative):
    rows, width = dctx.shape
    block = 2 * LEN
    count = rows // block
    extra = pre.shape[0]
    if relative:
        out_specs = [ANY] * 2
        out_shape = [jax.ShapeDtypeStruct((2 * width + extra, width), BF)] * 2
    else:
        out_specs = [pl.BlockSpec((1, width, width), lambda i, *_: (jnp.maximum(i - count, 0), 0, 0))]
        out_shape = [jax.ShapeDtypeStruct((4, width, width), BF)]
    dproj, *grads, sums = call(
        functools.partial(attention_back_kernel, relative),
        in_specs=[
                pl.BlockSpec((block, 3 * width), lambda i, *_: (jnp.minimum(i, count - 1), 0)),
                HELD,
                pl.BlockSpec((block // LEN,) + lse.shape[1:], lambda i, *_: (jnp.minimum(i, count - 1), 0, 0)),
                whole(pre.shape),
                HELD,
                FAR,
                FAR,
            ],
        out_specs=[HELD] + out_specs + [whole((8, 3 * width))],
        out_shape=[jax.ShapeDtypeStruct((rows, 3 * width), BF)] + out_shape + [jax.ShapeDtypeStruct((8, 3 * width), F32)],
        grid=(count + 4,),
        scalars=2,
        scratch_shapes=[
                pltpu.VMEM((rows, width), BF),
                pltpu.VMEM((rows, width), BF),
                pltpu.VMEM((width, rows), BF),
                pltpu.VMEM((2, width, width), BF),
                pltpu.VMEM(pre.shape, BF),
                pltpu.SemaphoreType.DMA((2,)),
                pltpu.SemaphoreType.DMA((2,)),
                pltpu.SemaphoreType.DMA((2,)),
            ],
        vmem=28,
        name="attention_back",
    )(place, lengths, proj, dctx, lse, pre, dattended, tokens, context)
    return dproj, grads, sums


def input_grad_kernel(proj_ref, w_hbm_ref, dz_ref, out_ref, w_ref, sems):
    block, width = out_ref.shape
    here = rows_at(pl.program_id(0), block)

    def body(ready):
        grad = dz_ref[here, :].astype(F32)
        for unit in range(3):
            ready(unit)
            grad += dot_nt(proj_ref[here, unit * width : (unit + 1) * width], w_ref[unit])
        ready(3)
        out_ref[...] = grad.astype(BF)

    first_and_later(Bring(WHOLE, (0, 0, 0), [w_hbm_ref], w_ref, sems), body)


def input_grad(dproj, w_qkvo, dz, block=256):
    rows, width = dz.shape
    return call(
        input_grad_kernel,
        in_specs=[HELD, FAR, HELD],
        out_specs=[rows_of(block, width)],
        out_shape=[jax.ShapeDtypeStruct((rows, width), BF)],
        grid=(rows // block,),
        scalars=0,
        scratch_shapes=[pltpu.VMEM((4, width, width), BF), pltpu.SemaphoreType.DMA((4,))],
        vmem=20,
        name="input_grad",
    )(dproj, w_qkvo, dz)[0]


CORES = [(i, i ^ 1) for i in range(8)]


def from_core(value):
    return lax.ppermute(value, "shard", CORES)


def from_chip(value, ahead):
    return lax.ppermute(value, "shard", [((i + 2 * ahead) % 8, i) for i in range(8)])


def to_chip(value, ahead):
    return lax.ppermute(value, "shard", [(i, (i + 2 * ahead) % 8) for i in range(8)])


def from_flip(value, which):
    flip = lambda s: which if s % 2 == 0 else 3 - which
    pairs = [(r * 8 + s, (r ^ flip(s)) * 8 + s) for r in range(4) for s in range(8)]
    return lax.ppermute(value, ("rep", "shard"), pairs)


def from_far(value):
    return lax.ppermute(value, "rep", [(i, i ^ 3) for i in range(4)])


def joined(*parts):
    return jnp.concatenate(parts, 0)


def after(value, *earlier):
    return lax.optimization_barrier((value,) + earlier)[0]


class Gather:
    def __init__(self, mine, own, other, own_places, depth):
        self.hops = [from_chip(mine, ahead) for ahead in (1, 2, 3)]
        self.own, self.other, self.own_places, self.depth = own, other, own_places, depth

    def first(self, *earlier):
        self.got = joined(after(self.hops[0], *earlier), *self.hops[1:])
        self.one = from_flip(self.got, 1)

    def second(self, *earlier):
        self.low = joined(self.got, after(self.one, *earlier))
        self.high = from_flip(self.low, 2)

    def direct(self, *earlier):
        hops = [hop[: self.depth] for hop in self.hops]
        self.got = joined(after(hops[0], *earlier), *hops[1:])
        self.others = [lax.ppermute(self.got, "rep", [(i, i ^ flip) for i in range(4)]) for flip in (1, 2, 3)]

    def hold(self, *earlier):
        self.others = [after(other, *earlier) for other in self.others]

    def weight_direct(self):
        return self.planned([self.got] + self.others, "direct")

    def weight(self):
        return self.planned([self.low, self.high], "skew")

    def planned(self, mine, kind):
        own = [pltpu.with_memory_space_constraint(piece, pltpu.HBM) for piece in self.own]
        pieces = own + self.other + mine + [from_core(piece) for piece in mine]
        count = len(own)
        entries = [
            (i + count * other, at, unit, None, 0, self.depth, other)
            for other in (0, 1)
            for i, places in enumerate(self.own_places)
            for at, unit in places
        ]
        each = 4 // len(mine)
        arriving = []
        for position in range(4):
            for other in (0, 1):
                source = SWAPPED[position] if kind == "skew" and other else position
                piece = 2 * count + len(mine) * other + source // each
                for ahead in (1, 2, 3):
                    at = pl.ds((3 * (source % each) + ahead - 1) * self.depth, self.depth)
                    arriving.append((piece, at, None, source, ahead, self.depth, other))
        if self.own_places[0][0][1] is None:
            arriving.sort(key=lambda entry: entry[4])
        return (kind, tuple(entries + arriving)), pieces


def wide(value):
    return value.astype(F32)


class Reduce:
    def __init__(self, grads, extra=0):
        self.keep, self.send = grads
        self.extra = extra
        self.quarter = (self.keep.shape[0] - extra) // 4
        self.depth = self.quarter // 4

    def cores(self, *earlier):
        self.other = from_core(after(self.send, *earlier) if earlier else self.send)

    def first(self, *earlier):
        self.other = after(self.other, *earlier)
        n = 2 * self.quarter
        self.sent = (wide(self.keep[n:]) + wide(self.other[n:])).astype(BF)
        self.one = from_flip(self.sent, 1)

    def second(self, *earlier):
        self.one = after(self.one, *earlier)
        n, x = self.quarter, self.extra
        total = wide(self.keep[n : 2 * n]) + wide(self.other[n : 2 * n]) + wide(self.one[x + n :])
        if x:
            at = slice(2 * n, 2 * n + x)
            self.vector = wide(self.keep[at]) + wide(self.other[at]) + wide(self.one[:x])
            total = joined(total, self.vector)
        self.sent = total.astype(BF)
        self.two = from_flip(self.sent, 2)

    def chips(self, *earlier):
        self.two = after(self.two, *earlier)
        n, x, depth = self.quarter, self.extra, self.depth
        total = wide(self.keep[:n]) + wide(self.other[:n]) + wide(self.one[x : x + n]) + wide(self.two[:n])
        if x:
            self.vector = self.vector + wide(self.two[n:])
        self.total = total[:depth]
        self.hops = []
        self.sents = []
        for ahead in (1, 2, 3):
            part = total[ahead * depth : (ahead + 1) * depth]
            if x:
                part = joined(part, self.vector)
            self.sents.append(part.astype(BF))
            self.hops.append(to_chip(self.sents[-1], ahead))

    def share(self, *earlier):
        self.hops[0] = after(self.hops[0], *earlier)
        for hop in self.hops:
            self.total = self.total + wide(hop[: self.depth])
            if self.extra:
                self.vector = self.vector + wide(hop[self.depth :])
        self.total = self.total.astype(BF)
        self.backs = [from_flip(self.total, 1), from_flip(self.total, 2), from_far(self.total)]

    def units(self, place):
        at = [self.total] + self.backs
        rep, core = place[0], place[2]
        a, d = at[0], at[3]
        b, c = jnp.where(core == 0, at[1], at[2]), jnp.where(core == 0, at[2], at[1])
        odd, upper = rep % 2 == 1, rep >= 2
        a, b, c, d = jnp.where(odd, b, a), jnp.where(odd, a, b), jnp.where(odd, d, c), jnp.where(odd, c, d)
        return [wide(v) for v in (jnp.where(upper, c, a), jnp.where(upper, d, b), jnp.where(upper, a, c), jnp.where(upper, b, d))]


def row_weights(task, lengths, task_masks):
    token_task = jnp.repeat(task, LEN)
    chosen = jnp.where(token_task == 0, task_masks[0], jnp.where(token_task == 1, task_masks[1], task_masks[2]))
    valid = jnp.arange(LEN, dtype=jnp.int32)[None, :] < lengths[:, None]
    return (chosen * valid.astype(jnp.int32).reshape(-1)).astype(F32)[:, None]


def per_device(mesh_shape, *arrays):
    (tokens, cotangent, task, lengths, task_masks, w_qkv, qv_bias, w_out, out_bias, ln1_gain, ln1_bias, w_up, up_bias, w_down, down_bias, ln2_gain, ln2_bias) = arrays
    rows, width = tokens.shape
    shards = mesh_shape["shard"]
    hidden = up_bias.shape[0] * shards
    fast = shards == 8 and mesh_shape["rep"] == 4
    place = jnp.stack([lax.axis_index("rep"), lax.axis_index("shard") // 2, lax.axis_index("shard") % 2]).astype(jnp.int32)
    shard = lax.axis_index("shard")

    vectors = (qv_bias, out_bias, ln1_gain, ln1_bias, down_bias, ln2_gain, ln2_bias, up_bias)
    sizes = [v.shape[0] for v in vectors]

    if fast:
        depth = w_qkv.shape[0]
        rep = place[0]
        every = slice(None)

        def columns(first, count):
            return [((every, pl.ds(unit * width, width)), first + unit) for unit in range(count)]

        mine = lax.dynamic_slice(w_qkv, (0, jnp.minimum(rep, 2) * width), (depth, width))
        mine = jnp.where(rep == 3, w_out, mine)
        other_qkv, other_out, other_up, other_down = [from_core(after(own, mine)) for own in (w_qkv, w_out, w_up, w_down)]
        gather_a = Gather(mine, [w_qkv, w_out], [other_qkv, other_out], [columns(0, 3), columns(3, 1)], depth)
        gather_a.first(other_qkv, other_out, other_up, other_down)
        packed = jnp.concatenate(after(vectors, gather_a.got))
        packed_rows = jnp.pad(packed, (0, 16 * width - packed.shape[0])).reshape(16, width)
        mine = joined(lax.dynamic_slice(w_up, (0, rep * width), (depth, width)), packed_rows)
        gather_b = Gather(mine, [w_up], [other_up], [columns(0, 4)], depth)
        gather_a.second(mine)
        vec_hops = [after(gather_b.hops[0], gather_a.low)] + gather_b.hops[1:]
        vec_rows = jnp.stack([packed_rows] + [hop[depth:] for hop in vec_hops])
        vec_rows = jnp.stack([vec_rows, from_core(vec_rows)], 1).reshape(8, -1)[:, : packed.shape[0]]
        index = jnp.arange(8)
        slot = 2 * ((index // 2 - place[1]) % 4) + ((index % 2) ^ place[2])
        pick = (slot[:, None] == index[None, :]).astype(BF)
        all_vectors = jnp.dot(pick, vec_rows, preferred_element_type=F32)
        row_weight = row_weights(*after((task, lengths, task_masks), gather_a.low))
    else:
        row_weight = row_weights(task, lengths, task_masks)
        packed = jnp.concatenate(vectors)
        all_vectors = lax.all_gather(packed, "shard", axis=0).astype(F32)
        full_a = jnp.concatenate([lax.all_gather(w_qkv, "shard", axis=0, tiled=True), lax.all_gather(w_out, "shard", axis=0, tiled=True)], 1)
        full_b = lax.all_gather(w_up, "shard", axis=0, tiled=True)
        weight_a = (WHOLE, [full_a.reshape(width, 4, width).transpose(1, 0, 2)])
        weight_b = (WHOLE, [full_b.reshape(width, 4, width).transpose(1, 0, 2)])
        full_c = lax.all_gather(w_down, "shard", axis=0, tiled=True)
        weight_c = (WHOLE, [full_c.reshape(4, -1, width)])

    full, start = [], 0
    for size in sizes:
        full.append(all_vectors[:, start : start + size].reshape(-1))
        start += size
    qv, out_shift, gain_one, shift_one, down_shift, gain_two, shift_two, up_shift = full
    qkv_shift = jnp.concatenate([qv[:width], jnp.zeros((width,), F32), qv[width:]])[None]
    vecs = jnp.stack([out_shift, gain_one, shift_one, down_shift, gain_two, shift_two, shift_two, shift_two])
    up_shift = up_shift[None]

    if fast:
        gather_a.high = after(gather_a.high, qkv_shift, vecs, up_shift, row_weight)
        weight_a = gather_a.weight()
        gather_b.direct(gather_a.high)
        mine = lax.dynamic_slice(w_down, (rep * depth, 0), (depth, width))
        own = [[(pl.ds(0, 4 * depth), None)]]
        mine = after(mine, gather_b.got)
        gather_c = Gather(mine, [w_down], [other_down], own, depth)
        qkv_shift = after(qkv_shift, gather_b.got, mine)
    proj, context, lse, w_a = attention_forward(place, lengths, tokens, qkv_shift, weight_a)
    if fast:
        gather_c.direct(context)
        gather_b.hold(gather_c.got)
        weight_b = gather_b.weight_direct()
        context = after(context, gather_c.got)
    norm_one, scale_one, first_low, act, slope, w_b = middle(place, tokens, context, w_a, vecs, up_shift, weight_b)
    if fast:
        gather_c.hold(act)
        weight_c = gather_c.weight_direct()
    output, dffn, sums_two, down_full, grads_c = ffn(place, act, weight_c, norm_one, cotangent, row_weight, vecs, shards, fast)
    if fast:
        group_c = Reduce(grads_c)
        group_c.cores()
    dinner, sums_up, grads_b = inner_grads(place, dffn, first_low, down_full, slope, fast)
    if fast:
        group_c.first(dinner)
        group_b = Reduce(grads_b)
        group_b.cores(group_c.sent)
        dinner = after(dinner, group_c.sent)
    dattended, dcontext, sums_one = first_grad(dinner, w_b, dffn, norm_one, scale_one, vecs, w_a)
    if fast:
        group_b.first(dcontext)
        group_c.second(dcontext)
        lse = after(lse, group_b.sent, group_c.sent)
    sums = jnp.concatenate([sums_one[2], sums_one[0], sums_one[1], sums_two[2], sums_two[0], sums_two[1], sums_up[0]])
    pre = jnp.pad(sums.reshape(-1, width), ((2, 4), (0, 0))).astype(BF)
    dproj, grads_a, sums_qkv = attention_back(place, lengths, proj, dcontext, lse, tokens, context, dattended, pre, fast)
    if fast:
        group_a = Reduce(grads_a, pre.shape[0])
        group_c.two, group_b.one = after(group_c.two, *grads_a), after(group_b.one, *grads_a)
        group_a.cores(group_c.two, group_b.one)
        group_c.chips()
        group_b.second()
        group_a.first(group_b.sent, *group_c.sents)
        dproj = after(dproj, group_a.sent)
    grad_input = input_grad(dproj, w_a, dattended)

    starts = [0]
    for size in sizes:
        starts.append(starts[-1] + size * shards)
    if fast:
        group_b.chips(grad_input)
        group_c.share(*group_b.sents)
        group_a.second(group_c.total)
        group_b.share(group_a.sent)
        group_a.chips(group_b.total)
        group_c.backs = [after(back, *group_a.sents) for back in group_c.backs]
        group_b.backs = [after(back, *group_a.sents) for back in group_b.backs]
        group_a.share()
        units_a, units_b, units_c = [group.units(place) for group in (group_a, group_b, group_c)]
        sums = group_a.vector.reshape(-1)
    else:
        units = []
        for (grads,) in (grads_b, grads_a):
            summed = lax.psum_scatter(grads, "shard", scatter_dimension=1, tiled=True)
            units.append([wide(unit) for unit in lax.psum(summed.astype(BF), "rep")])
        units_b, units_a = units
        summed = lax.psum(lax.psum_scatter(grads_c[0], "shard", scatter_dimension=0, tiled=True), "rep")[0]
        units_c = [wide(unit) for unit in jnp.split(summed, 4)]
        sums = jnp.concatenate([sums_qkv[0, :width], sums_qkv[0, 2 * width :], sums])
        sums = lax.psum(sums, ("rep", "shard"))
    final = [lax.dynamic_slice(sums, (start + shard * size,), (size,)) for start, size in zip(starts, sizes)]
    f_qv, f_out_shift, f_gain_one, f_shift_one, f_down_shift, f_gain_two, f_shift_two, f_up_shift = final
    wide_b = jnp.concatenate(units_b, 1)
    wide_a = jnp.concatenate(units_a[:3], 1)
    final_c = jnp.concatenate(units_c, 0).T
    return (output, grad_input, wide_a, f_qv, units_a[3], f_out_shift, f_gain_one, f_shift_one, wide_b, f_up_shift, final_c, f_down_shift, f_gain_two, f_shift_two)


def solution(mesh):
    split, shard = P(("rep", "shard"), None), P("shard")
    flat, matrix = P(("rep", "shard")), P("shard", None)
    in_specs = (split, split, flat, flat, P(None, ("rep", "shard")), matrix, shard, matrix, shard, shard, shard, matrix, shard, matrix, shard, shard, shard)
    out_specs = (split, split, matrix, shard, matrix, shard, shard, shard, matrix, shard, matrix, shard, shard, shard)
    return jax.shard_map(
        functools.partial(per_device, dict(mesh.shape)), mesh=mesh, in_specs=in_specs, out_specs=out_specs, check_vma=False
    )
```

```python
import functools
import math

import jax
import jax.numpy as jnp
from jax import lax
from jax.experimental import pallas as pl
from jax.experimental.pallas import tpu as pltpu
from jax.sharding import PartitionSpec as P

HD = 64
LEN = 128
EPSILON = 1e-06
BF = jnp.bfloat16
F32 = jnp.float32
MIB = 1024 * 1024

ROOT_HALF = 0.7071067811865476
DENSITY = 0.3989422804014327


def dot_nn(left, right):
    return jnp.dot(left, right, preferred_element_type=F32)


def dot_nt(left, right):
    return lax.dot_general(left, right, (((1,), (1,)), ((), ())), preferred_element_type=F32)


def dot_tn(left, right):
    return lax.dot_general(left, right, (((0,), (0,)), ((), ())), preferred_element_type=F32)


def gelu_parts(inner):
    phi = 0.5 + 0.5 * lax.erf(inner * ROOT_HALF)
    bell = jnp.exp(inner * inner * -0.5) * DENSITY
    return inner * phi, phi + inner * bell


def norm_parts(summed):
    centre = jnp.mean(summed, -1, keepdims=True)
    deviation = summed - centre
    variance = jnp.mean(deviation * deviation, -1, keepdims=True)
    rscale = lax.rsqrt(variance + EPSILON)
    return deviation * rscale, rscale


def norm_back(grad_norm, normed, rscale):
    first_mean = jnp.mean(grad_norm, -1, keepdims=True)
    second_mean = jnp.mean(grad_norm * normed, -1, keepdims=True)
    return rscale * (grad_norm - first_mean - normed * second_mean)


def add_rows(total_ref, rows):
    @pl.when(pl.program_id(0) == 0)
    def _():
        total_ref[...] = jnp.zeros_like(total_ref)

    for at, values in enumerate(rows):
        total_ref[at : at + 1, :] += jnp.sum(values, 0, keepdims=True)


def cost(flops, moved):
    return pl.CostEstimate(flops=1000, bytes_accessed=1000, transcendentals=0)


def params(vmem=28):
    return pltpu.CompilerParams(vmem_limit_bytes=vmem * MIB)


def halves_of(step, block):
    half = block // 2
    return [(slice(at, at + half), pl.ds(pl.multiple_of(step * block + at, half), half)) for at in (0, half)]


def rows_at(step, block):
    return pl.ds(pl.multiple_of(step * block, block), block)


def whole(shape):
    return pl.BlockSpec(shape, lambda i, *_: (0,) * len(shape))


def rows_of(block, width):
    return pl.BlockSpec((block, width), lambda i, *_: (i, 0))


def head_masks():
    lane = lax.broadcasted_iota(jnp.int32, (1, 2 * HD), 1)
    return (lane < HD).astype(BF), (lane >= HD).astype(BF)


def stack_heads(pair, masks):
    return jnp.concatenate([pair * masks[0], pair * masks[1]], axis=0)


def attention_forward_kernel(plan, count_of_pieces, place, lengths, x_ref, shift_ref, *refs):
    pieces, (proj_ref, ctx_ref, lse_ref, w_out_ref, w_ref, sems) = refs[: count_of_pieces], refs[count_of_pieces :]
    block, width = x_ref.shape
    step = pl.program_id(0)

    def body(ready):
        x = x_ref[...]
        for i in range(4):
            unit = ready(i)

            @pl.when(unit < 3)
            def _():
                at = pl.ds(pl.multiple_of(unit * width, width), width)
                proj_ref[:, at] = (dot_nn(x, w_ref[unit]) + shift_ref[:, at]).astype(BF)

        masks = head_masks()
        lane = lax.broadcasted_iota(jnp.int32, (1, LEN), 1)
        for seq in range(block // LEN):
            number = step * (block // LEN) + seq
            rows = rows_at(number, LEN)
            here = slice(seq * LEN, (seq + 1) * LEN)
            valid = lane < lengths[number]
            lse = jnp.zeros((LEN, LEN), F32)
            pairs = range(width // (2 * HD))

            def part(offset, pair):
                return proj_ref[here, offset + pair * 2 * HD : offset + (pair + 1) * 2 * HD]

            stage = [dot_nt(part(0, pair) * BF(0.125), stack_heads(part(width, pair), masks)) for pair in pairs]
            later = []
            for pair, scores in zip(pairs, stage):
                probs = []
                for half in range(2):
                    masked = jnp.where(valid, scores[:, half * LEN : (half + 1) * LEN], -1e9)
                    top = jnp.max(masked, -1, keepdims=True)
                    exponent = jnp.exp(masked - top)
                    total = jnp.sum(exponent, -1, keepdims=True)
                    probs.append((exponent * (1.0 / total)).astype(BF))
                    lse = jnp.where(lane == 2 * pair + half, top + jnp.log(total), lse)
                later.append(jnp.concatenate(probs, axis=1))
            for pair, probs in zip(pairs, later):
                ctx = dot_nn(probs, stack_heads(part(2 * width, pair), masks))
                ctx_ref[rows, pair * 2 * HD : (pair + 1) * 2 * HD] = ctx.astype(BF)
            lse_ref[number] = lse.T[: lse_ref.shape[1]]

    first_and_later(Bring(plan, place, pieces, w_ref, sems, w_out_ref=w_out_ref), body)


SWAPPED = (0, 2, 1, 3)


def flip_of(position, core):
    return {0: 0, 1: 1 + core, 2: 2 - core, 3: 3}[position]


class Bring:
    def __init__(self, plan, place, pieces, w_ref, sems, rows_first=False, w_out_ref=None):
        self.kind, self.entries = plan
        self.place, self.pieces = place, pieces
        self.w_ref, self.w_out_ref, self.sems, self.rows_first = w_ref, w_out_ref, sems, rows_first
        self.span = w_ref.shape[0] // 4

    def part(self, ref, at):
        return ref.at[rows_at(at, self.span)] if self.rows_first else ref.at[at]

    def unit(self, position, other):
        rep, core = self.place[0], self.place[2]
        return rep ^ (position if self.kind == "direct" else flip_of(position, core ^ other))

    def round(self, i):
        if self.kind == "whole":
            return i
        return (self.place[1] + i) % 4 if self.rows_first else self.unit(i, 0)

    def start(self):
        if self.kind == "whole":
            for at in range(4):
                pltpu.make_async_copy(self.pieces[0].at[at], self.part(self.w_ref, at), self.sems.at[at]).start()
            return
        chip, core = self.place[1], self.place[2]
        for piece, at, unit, position, ahead, depth, other in self.entries:
            to_unit = unit if position is None else self.unit(position, other)
            to_chip = (chip + ahead) % 4
            shard = 2 * to_chip + (core ^ other)
            if self.rows_first:
                first = 4 * shard if to_unit is None else 4 * shard + to_unit
                count = 4 * depth if to_unit is None else depth
                group, to = to_chip, self.w_ref.at[pl.ds(pl.multiple_of(first * depth, 16), count)]
            else:
                group, to = to_unit, self.w_ref.at[to_unit, pl.ds(pl.multiple_of(shard * depth, 16), depth)]
            pltpu.make_async_copy(self.pieces[piece].at[at], to, self.sems.at[group]).start()

    def wait(self, at):
        here = self.part(self.w_ref, at)
        pltpu.make_async_copy(here, here, self.sems.at[at]).wait()
        if self.w_out_ref is not None:
            self.onward(at).start()

    def onward(self, at):
        return pltpu.make_async_copy(self.part(self.w_ref, at), self.part(self.w_out_ref, at), self.sems.at[4 + at])

    def finish(self):
        for at in range(4):
            self.onward(at).wait()


def first_and_later(bring, body):
    @pl.when(pl.program_id(0) == 0)
    def _():
        bring.start()

        def ready(i):
            at = bring.round(i)
            bring.wait(at)
            return at

        body(ready)

    @pl.when(pl.program_id(0) > 0)
    def _():
        body(bring.round)

    if bring.w_out_ref is not None:

        @pl.when(pl.program_id(0) == pl.num_programs(0) - 1)
        def _():
            bring.finish()


ANY = pl.BlockSpec(memory_space=pl.ANY)
HELD = pl.BlockSpec(memory_space=pltpu.VMEM)
FAR = pl.BlockSpec(memory_space=pl.ANY)


def call(kernel, in_specs, out_specs, out_shape, grid, scalars, scratch_shapes, vmem, name):
    def space(spec, shape, result):
        large = math.prod(shape.shape) * shape.dtype.itemsize > MIB // 2
        if spec is HELD:
            return pltpu.VMEM
        return pltpu.HBM if spec is FAR or large and (result or spec is not ANY) else None

    def placed(spec, shape):
        where = space(spec, shape, True)
        return shape if where is None else where(shape.shape, shape.dtype)

    run = pl.pallas_call(
        kernel,
        grid_spec=pltpu.PrefetchScalarGridSpec(
            num_scalar_prefetch=scalars, grid=grid, in_specs=in_specs, out_specs=out_specs, scratch_shapes=scratch_shapes
        ),
        out_shape=[placed(spec, shape) for spec, shape in zip(out_specs, out_shape)],
        compiler_params=params(vmem),
        cost_estimate=cost(0, 0),
        name=name,
    )

    def constrained(spec, arg):
        where = space(spec, arg, False)
        return arg if where is None else pltpu.with_memory_space_constraint(arg, where)

    def apply(*args):
        return run(*args[:scalars], *[constrained(spec, arg) for spec, arg in zip(in_specs, args[scalars:])])

    return apply


WHOLE = ("whole", ())


def attention_forward(place, lengths, tokens, shift, weight):
    rows, width = tokens.shape
    block = 2 * LEN
    heads = width // HD
    lse_rows = -(-heads // 8) * 8
    plan, pieces = weight
    return call(
        functools.partial(attention_forward_kernel, plan, len(pieces)),
        in_specs=[rows_of(block, width), whole((1, 3 * width))] + [FAR] * len(pieces),
        out_specs=[rows_of(block, 3 * width), HELD, HELD, ANY],
        out_shape=[
            jax.ShapeDtypeStruct((rows, 3 * width), BF),
            jax.ShapeDtypeStruct((rows, width), BF),
            jax.ShapeDtypeStruct((rows // LEN, lse_rows, LEN), F32),
            jax.ShapeDtypeStruct((4, width, width), BF),
        ],
        grid=(rows // block,),
        scalars=2,
        scratch_shapes=[pltpu.VMEM((4, width, width), BF), pltpu.SemaphoreType.DMA((8,))],
        vmem=28,
        name="attention_forward",
    )(place, lengths, tokens, shift, *pieces)


def middle_kernel(plan, count_of_pieces, place, x_ref, ctx_ref, w_attn_ref, vec_ref, up_shift_ref, *refs):
    pieces = refs[: count_of_pieces]
    norm_ref, scale_ref, low_ref, act_ref, slope_ref, w_out_ref, w_ref, sems = refs[count_of_pieces :]
    block, width = x_ref.shape

    def body(ready):
        halves = halves_of(pl.program_id(0), block)
        attended = [dot_nn(ctx_ref[here, :], w_attn_ref[0]) + vec_ref[0:1, :] for _, here in halves]
        lows = []
        for (local, here), value in zip(halves, attended):
            normed, rscale = norm_parts(x_ref[local, :].astype(F32) + value)
            norm_ref[here, :] = normed.astype(BF)
            scale_ref[here, :] = rscale
            lows.append((normed * vec_ref[1:2, :] + vec_ref[2:3, :]).astype(BF))
            low_ref[here, :] = lows[-1]
        for i in range(w_ref.shape[0]):
            unit = ready(i)
            at = pl.ds(pl.multiple_of(unit * width, width), width)
            for (_, here), low in zip(halves, lows):
                act, slope = gelu_parts(dot_nn(low, w_ref[unit]) + up_shift_ref[:, at])
                act_ref[here, at] = act.astype(BF)
                slope_ref[here, at] = slope.astype(BF)

    first_and_later(Bring(plan, place, pieces, w_ref, sems, w_out_ref=w_out_ref), body)


def middle(place, tokens, context, w_qkvo, vecs, up_shift, weight, block=512):
    rows, width = tokens.shape
    hidden = up_shift.shape[1]
    units = hidden // width
    plan, pieces = weight
    return call(
        functools.partial(middle_kernel, plan, len(pieces)),
        in_specs=[
                rows_of(block, width),
                HELD,
                pl.BlockSpec((1, width, width), lambda i, *_: (3, 0, 0)),
                whole(vecs.shape),
                whole(up_shift.shape),
            ]
            + [FAR] * len(pieces),
        out_specs=[HELD] * 5 + [ANY],
        out_shape=[
            jax.ShapeDtypeStruct((rows, width), BF),
            jax.ShapeDtypeStruct((rows, 1), F32),
            jax.ShapeDtypeStruct((rows, width), BF),
            jax.ShapeDtypeStruct((rows, hidden), BF),
            jax.ShapeDtypeStruct((rows, hidden), BF),
            jax.ShapeDtypeStruct((units, width, width), BF),
        ],
        grid=(rows // block,),
        scalars=1,
        scratch_shapes=[pltpu.VMEM((units, width, width), BF), pltpu.SemaphoreType.DMA((8,))],
        vmem=28,
        name="middle",
    )(place, tokens, context, w_qkvo, vecs, up_shift, *pieces)


def ffn_kernel(plan, count_of_pieces, relative, place, act_ref, norm_ref, cot_ref, weight_ref, vec_ref, *refs):
    pieces, refs = refs[: count_of_pieces], refs[count_of_pieces :]
    out_ref, low_ref, sum_ref, w_out_ref, *refs = refs
    outs, refs = refs[: 2 if relative else 1], refs[2 if relative else 1 :]
    turned_ref, w_ref, stage_ref, sems, w_sems = refs
    step = pl.program_id(0)
    block, width = cot_ref.shape
    count = act_ref.shape[0] // block
    halves = halves_of(jnp.minimum(step, count - 1), block)
    bring = Bring(plan, place, pieces, w_ref, w_sems, rows_first=True, w_out_ref=w_out_ref)

    def finish(local, here, ffn):
        first = norm_ref[here, :].astype(F32) * vec_ref[1:2, :] + vec_ref[2:3, :]
        normed, rscale = norm_parts(first + (ffn + vec_ref[3:4, :]))
        out_ref[local, :] = (normed * vec_ref[4:5, :] + vec_ref[5:6, :]).astype(BF)
        grad = cot_ref[local, :].astype(F32) * weight_ref[local, :]
        low = norm_back(grad * vec_ref[4:5, :], normed, rscale).astype(BF)
        low_ref[here, :] = low
        turned_ref[:, here] = low.T
        for at, values in enumerate((grad * normed, grad, low.astype(F32))):
            sum_ref[at : at + 1, :] += jnp.sum(values, 0, keepdims=True)

    @pl.when(step == 0)
    def _():
        bring.start()
        sum_ref[...] = jnp.zeros_like(sum_ref)
        ffns = [0.0, 0.0]
        for i in range(4):
            part = bring.round(i)
            bring.wait(part)
            at = rows_at(part, bring.span)
            ffns = [ffn + dot_nn(act_ref[here, at], w_ref[at, :]) for ffn, (_, here) in zip(ffns, halves)]
        for (local, here), ffn in zip(halves, ffns):
            finish(local, here, ffn)

    @pl.when((step > 0) & (step < count))
    def _():
        ffns = [dot_nn(act_ref[here, :], w_ref[...]) for _, here in halves]
        for (local, here), ffn in zip(halves, ffns):
            finish(local, here, ffn)

    def left(slot):
        here = stage_ref.at[slot]
        pltpu.make_async_copy(here, here, sems.at[slot]).wait()

    if relative:

        @pl.when(step >= count + 2)
        def _():
            left(step % 2)

    @pl.when(step >= count)
    def _():
        at = step - count
        columns = pl.ds(pl.multiple_of(at * width, width), width)
        grad = dot_nn(turned_ref[...], act_ref[:, columns]).astype(BF)
        if not relative:
            each, _, part = outs[0].shape
            for i in range(each):
                outs[0][i] = grad[:, i * part : (i + 1) * part]
            return
        rep, chip, core = place[0], place[1], place[2]
        part, depth = width // 2, width // 4
        slot = step % 2
        for half in range(2):
            stage_ref[slot, half] = grad[:, half * part : (half + 1) * part]
        ahead = (at - chip) % 4
        for unit in range(4):
            rows = pl.ds(unit * depth, depth)
            for ref, whose in zip(outs, (core, 1 - core)):
                to = pl.multiple_of((4 * slot_of(unit, rep, whose) + ahead) * depth, 16)
                pltpu.make_async_copy(stage_ref.at[slot, whose, rows], ref.at[pl.ds(to, depth)], sems.at[slot]).start()

    @pl.when(step == pl.num_programs(0) - 1)
    def _():
        bring.finish()
        if relative:
            left(0)
            left(1)


def once(shape):
    return pl.BlockSpec(shape, lambda i, *_: (0,) * len(shape), pipeline_mode=pl.Buffered(1))


def ffn(place, act, weight, norm_one, cotangent, row_weight, vecs, shards, relative, block=512):
    rows, width = cotangent.shape
    hidden = act.shape[1]
    part = hidden // shards
    each = width // part
    count = rows // block
    plan, pieces = weight
    if relative:
        out_specs = [ANY] * 2
        out_shape = [jax.ShapeDtypeStruct((4 * width, part), BF)] * 2
    else:
        out_specs = [pl.BlockSpec((each, width, part), lambda i, *_: (jnp.maximum(i - count, 0), 0, 0))]
        out_shape = [jax.ShapeDtypeStruct((shards, width, part), BF)]
    early = lambda columns: pl.BlockSpec((block, columns), lambda i, *_: (jnp.minimum(i, count - 1), 0))
    output, low, sums, w_down, *grads = call(
        functools.partial(ffn_kernel, plan, len(pieces), relative),
        in_specs=[HELD, HELD, early(width), early(1), whole(vecs.shape)] + [FAR] * len(pieces),
        out_specs=[early(width), HELD, whole((8, width)), ANY] + out_specs,
        out_shape=[
            jax.ShapeDtypeStruct((rows, width), BF),
            jax.ShapeDtypeStruct((rows, width), BF),
            jax.ShapeDtypeStruct((8, width), F32),
            jax.ShapeDtypeStruct((hidden, width), BF),
        ]
        + out_shape,
        grid=(count + shards // each,),
        scalars=1,
        scratch_shapes=[
            pltpu.VMEM((width, rows), BF),
            pltpu.VMEM((hidden, width), BF),
            pltpu.VMEM((2, 2, width, width // 2), BF),
            pltpu.SemaphoreType.DMA((2,)),
            pltpu.SemaphoreType.DMA((8,)),
        ],
        vmem=28,
        name="ffn",
    )(place, act, norm_one, cotangent, row_weight, vecs, *pieces)
    return output, low, sums, w_down, grads


class Outward:
    def __init__(self, stage_ref, sems):
        self.step = pl.program_id(0)
        self.slot = self.step % 2
        self.stage_ref, self.sems = stage_ref, sems

    def free(self):
        @pl.when(self.step >= 2)
        def _():
            self.wait(self.slot)

    def stage(self):
        return self.stage_ref.at[self.slot]

    def send(self, *pairs):
        for source, to in pairs:
            pltpu.make_async_copy(source, to, self.sems.at[self.slot]).start()

    def wait(self, slot):
        here = self.stage_ref.at[slot]
        pltpu.make_async_copy(here, here, self.sems.at[slot]).wait()

    def finish(self):
        @pl.when(self.step == pl.num_programs(0) - 1)
        def _():
            self.wait(1 - self.slot)
            self.wait(self.slot)


def slot_of(unit, rep, core):
    e = unit ^ rep
    return jnp.where(core == 0, 2 * (e % 2) + e // 2, e)


def send_units(place, grad, out, outs, extra, unit=None):
    rep, chip, core = place[0], place[1], place[2]
    depth = grad.shape[0] // 8
    unit = pl.program_id(0) if unit is None else unit
    stage = out.stage()
    stage[...] = grad
    for ref, whose in zip(outs, (core, 1 - core)):
        slot = slot_of(unit, rep, whose)
        for other in range(4):
            ahead = (other - chip) % 4
            to = pl.multiple_of((4 * slot + ahead) * depth + jnp.where(slot >= 2, extra, 0), 16)
            row = pl.multiple_of((2 * other + whose) * depth, 16)
            out.send((stage.at[pl.ds(row, depth)], ref.at[pl.ds(to, depth)]))


def inner_grads_kernel(relative, place, low_ref, w_ref, slope_ref, first_ref, inner_ref, sum_ref, *refs):
    outs, refs = refs[: 2 if relative else 1], refs[2 if relative else 1 :]
    turned_ref, stage_ref, sems = refs
    step = pl.program_id(0)
    rows, width = low_ref.shape
    columns = pl.ds(pl.multiple_of(step * width, width), width)

    @pl.when(step == 0)
    def _():
        turned_ref[...] = first_ref[...].T

    total = 0.0
    for at in range(0, rows, 256):
        here = slice(at, at + 256)
        grad = (dot_nt(low_ref[here, :], w_ref[...]) * slope_ref[here, columns].astype(F32)).astype(BF)
        inner_ref[here, columns] = grad
        total = total + jnp.sum(grad.astype(F32), 0, keepdims=True)
    sum_ref[0:1, :] = total

    grad = dot_nn(turned_ref[...], inner_ref[:, columns]).astype(BF)
    if relative:
        out = Outward(stage_ref, sems)
        out.free()
        send_units(place, grad, out, outs, 0)
        out.finish()
    else:
        outs[0][0] = grad


def inner_grads(place, low, first, w_down, slope, relative):
    rows, width = low.shape
    hidden = slope.shape[1]
    columns = lambda height: pl.BlockSpec((height, width), lambda i, place: (0, i))
    if relative:
        out_specs = [ANY] * 2
        out_shape = [jax.ShapeDtypeStruct((2 * width, width), BF)] * 2
    else:
        out_specs = [pl.BlockSpec((1, width, width), lambda i, place: (i, 0, 0))]
        out_shape = [jax.ShapeDtypeStruct((4, width, width), BF)]
    inner, sums, *grads = call(
        functools.partial(inner_grads_kernel, relative),
        in_specs=[HELD, pl.BlockSpec((width, width), lambda i, place: (i, 0)), HELD, HELD],
        out_specs=[HELD, columns(8)] + out_specs,
        out_shape=[jax.ShapeDtypeStruct((rows, hidden), BF), jax.ShapeDtypeStruct((8, hidden), F32)] + out_shape,
        grid=(hidden // width,),
        scalars=1,
        scratch_shapes=[
            pltpu.VMEM((width, rows), BF),
            pltpu.VMEM((2, width, width), BF),
            pltpu.SemaphoreType.DMA((2,)),
        ],
        vmem=28,
        name="inner_grads",
    )(place, low, w_down, slope, first)
    return inner, sums, grads


def first_grad_kernel(inner_ref, w_hbm_ref, low_in_ref, norm_ref, scale_ref, vec_ref, w_attn_ref, low_ref, ctx_ref, sum_ref, w_ref, sems):
    width = norm_ref.shape[1]
    halves = halves_of(pl.program_id(0), 512)

    @pl.when(pl.program_id(0) == 0)
    def _():
        sum_ref[...] = jnp.zeros_like(sum_ref)

    def body(ready):
        grads = [low_in_ref[here, :].astype(F32) for _, here in halves]
        for unit in range(4):
            ready(unit)
            at = slice(unit * width, (unit + 1) * width)
            grads = [grad + dot_nt(inner_ref[here, at], w_ref[unit]) for grad, (_, here) in zip(grads, halves)]
        for grad, (_, here) in zip(grads, halves):
            normed = norm_ref[here, :].astype(F32)
            low = norm_back(grad * vec_ref[1:2, :], normed, scale_ref[here, :]).astype(BF)
            low_ref[here, :] = low
            ctx_ref[here, :] = dot_nt(low, w_attn_ref[0]).astype(BF)
            for at, values in enumerate((grad * normed, grad, low.astype(F32))):
                sum_ref[at : at + 1, :] += jnp.sum(values, 0, keepdims=True)

    first_and_later(Bring(WHOLE, (0, 0, 0), [w_hbm_ref], w_ref, sems), body)


def first_grad(inner, w_up, low, norm_one, scale_one, vecs, w_qkvo, block=512):
    rows, width = low.shape
    hidden = inner.shape[1]
    return call(
        first_grad_kernel,
        in_specs=[
            HELD,
            FAR,
            HELD,
            HELD,
            HELD,
            whole(vecs.shape),
            pl.BlockSpec((1, width, width), lambda i: (3, 0, 0)),
        ],
        out_specs=[HELD, HELD, whole((8, width))],
        out_shape=[
            jax.ShapeDtypeStruct((rows, width), BF),
            jax.ShapeDtypeStruct((rows, width), BF),
            jax.ShapeDtypeStruct((8, width), F32),
        ],
        grid=(rows // block,),
        scalars=0,
        scratch_shapes=[pltpu.VMEM(w_up.shape, BF), pltpu.SemaphoreType.DMA((4,))],
        vmem=28,
        name="first_grad",
    )(inner, w_up, low, norm_one, scale_one, vecs, w_qkvo)


def attention_back_kernel(relative, place, lengths, proj_ref, dctx_ref, lse_ref, pre_ref, attn_ref, ctx_ref, x_hbm_ref, held_ref, *refs):
    outs, refs = refs[: 2 if relative else 1], refs[2 if relative else 1 :]
    sum_ref, x_ref, turned_ref, stage_ref, sums_ref, sems, sum_sems, late_sem = refs
    step = pl.program_id(0)
    width = dctx_ref.shape[1]
    block = 2 * LEN
    count = held_ref.shape[0] // block
    extra = sums_ref.shape[0]
    late = pltpu.make_async_copy(x_hbm_ref, x_ref, late_sem)

    @pl.when(step == 0)
    def _():
        sum_ref[...] = jnp.zeros_like(sum_ref)
        late.start()

    @pl.when(step == 1)
    def _():
        late.wait()
        turned_ref[...] = x_ref[...].T

    @pl.when(step < count)
    def _():
        masks = head_masks()
        lane = lax.broadcasted_iota(jnp.int32, (1, 2 * HD), 1)
        key = lax.broadcasted_iota(jnp.int32, (LEN, 1), 0)
        for seq in range(block // LEN):
            number = step * (block // LEN) + seq
            rows = rows_at(number, LEN)
            here_rows = slice(seq * LEN, (seq + 1) * LEN)
            valid = key < lengths[number]
            pairs = range(width // (2 * HD))

            def part(ref, where, offset, pair):
                return ref[where, offset + pair * 2 * HD : offset + (pair + 1) * 2 * HD]

            stage = []
            for pair in pairs:
                q = part(proj_ref, here_rows, 0, pair) * BF(0.125)
                dctx = part(dctx_ref, rows, 0, pair)
                queries, grads = stack_heads(q, masks), stack_heads(dctx, masks)
                scores = dot_nt(part(proj_ref, here_rows, width, pair), queries)
                dprobs = dot_nt(part(proj_ref, here_rows, 2 * width, pair), grads)
                stage.append((queries, grads, scores, dprobs))
            later = []
            for pair, (queries, grads, scores, dprobs) in zip(pairs, stage):
                probs, dscores = [], []
                for half in range(2):
                    here = slice(half * LEN, (half + 1) * LEN)
                    lse = lse_ref[number, 2 * pair + half : 2 * pair + half + 1, :]
                    prob = jnp.exp(jnp.where(valid, scores[:, here], -1e9) - lse)
                    dprob = dprobs[:, here]
                    inner = jnp.sum(prob * dprob, 0, keepdims=True)
                    dscores.append((prob * (dprob - inner)).astype(BF))
                    probs.append(prob.astype(BF))
                turned = jnp.concatenate([dscore.T for dscore in dscores], axis=1)
                later.append((queries, grads, jnp.concatenate(probs, axis=1), jnp.concatenate(dscores, axis=1), turned))
            for pair, (queries, grads, probs, dscores, turned) in zip(pairs, later):
                dv = dot_nn(probs, grads).astype(BF)
                dk = dot_nn(dscores, queries).astype(BF)
                dq = (dot_nn(turned, stack_heads(part(proj_ref, here_rows, width, pair), masks)) * 0.125).astype(BF)
                at = pair * 2 * HD
                for offset, grad in ((0, dq), (width, dk), (2 * width, dv)):
                    held_ref[rows, offset + at : offset + at + 2 * HD] = grad
                    if offset != width:
                        sum_ref[0:1, offset + at : offset + at + 2 * HD] += jnp.sum(grad.astype(F32), 0, keepdims=True)

    if relative:
        out = Outward(stage_ref, sems)
        copies = [
            pltpu.make_async_copy(sums_ref, ref.at[pl.ds(width, extra)], sum_sems.at[i])
            for i, ref in enumerate(outs)
        ]

        @pl.when(step == count)
        def _():
            sums_ref[...] = pre_ref[...]
            sums_ref[0:1, :] = sum_ref[0:1, :width].astype(BF)
            sums_ref[1:2, :] = sum_ref[0:1, 2 * width :].astype(BF)
            for copy in copies:
                copy.start()

    def put(unit, grad):
        if not relative:
            outs[0][0] = grad
            return

        @pl.when(step >= count + 2)
        def _():
            out.wait(out.slot)

        send_units(place, grad, out, outs, extra, unit)

    for unit in range(3):

        @pl.when(step == count + unit)
        def _():
            put(unit, dot_nn(turned_ref[...], held_ref[:, unit * width : (unit + 1) * width]).astype(BF))

    @pl.when(step == count + 3)
    def _():
        turned_ref[...] = ctx_ref[...].T
        put(3, dot_nn(turned_ref[...], attn_ref[...]).astype(BF))
        if relative:
            for copy in copies:
                copy.wait()

    if relative:
        out.finish()


def attention_back(place, lengths, proj, dctx, lse, tokens, context, dattended, pre, relative):
    rows, width = dctx.shape
    block = 2 * LEN
    count = rows // block
    extra = pre.shape[0]
    if relative:
        out_specs = [ANY] * 2
        out_shape = [jax.ShapeDtypeStruct((2 * width + extra, width), BF)] * 2
    else:
        out_specs = [pl.BlockSpec((1, width, width), lambda i, *_: (jnp.maximum(i - count, 0), 0, 0))]
        out_shape = [jax.ShapeDtypeStruct((4, width, width), BF)]
    dproj, *grads, sums = call(
        functools.partial(attention_back_kernel, relative),
        in_specs=[
            pl.BlockSpec((block, 3 * width), lambda i, *_: (jnp.minimum(i, count - 1), 0)),
            HELD,
            HELD,
            whole(pre.shape),
            HELD,
            HELD,
            FAR,
            ],
        out_specs=[HELD] + out_specs + [whole((8, 3 * width))],
        out_shape=[jax.ShapeDtypeStruct((rows, 3 * width), BF)] + out_shape + [jax.ShapeDtypeStruct((8, 3 * width), F32)],
        grid=(count + 4,),
        scalars=2,
        scratch_shapes=[
            pltpu.VMEM((rows, width), BF),
            pltpu.VMEM((width, rows), BF),
            pltpu.VMEM((2, width, width), BF),
            pltpu.VMEM(pre.shape, BF),
            pltpu.SemaphoreType.DMA((2,)),
            pltpu.SemaphoreType.DMA((2,)),
            pltpu.SemaphoreType.DMA,
        ],
        vmem=28,
        name="attention_back",
    )(place, lengths, proj, dctx, lse, pre, dattended, context, tokens)
    return dproj, grads, sums


def input_grad_kernel(proj_ref, w_hbm_ref, dz_ref, out_ref, w_ref, sems):
    block, width = out_ref.shape
    here = rows_at(pl.program_id(0), block)

    def body(ready):
        grad = dz_ref[here, :].astype(F32)
        for unit in range(3):
            ready(unit)
            grad += dot_nt(proj_ref[here, unit * width : (unit + 1) * width], w_ref[unit])
        ready(3)
        out_ref[...] = grad.astype(BF)

    first_and_later(Bring(WHOLE, (0, 0, 0), [w_hbm_ref], w_ref, sems), body)


def input_grad(dproj, w_qkvo, dz, block=256):
    rows, width = dz.shape
    return call(
        input_grad_kernel,
        in_specs=[HELD, FAR, HELD],
        out_specs=[rows_of(block, width)],
        out_shape=[jax.ShapeDtypeStruct((rows, width), BF)],
        grid=(rows // block,),
        scalars=0,
        scratch_shapes=[pltpu.VMEM((4, width, width), BF), pltpu.SemaphoreType.DMA((4,))],
        vmem=28,
        name="input_grad",
    )(dproj, w_qkvo, dz)[0]


CORES = [(i, i ^ 1) for i in range(8)]


def from_core(value):
    return lax.ppermute(value, "shard", CORES)


def from_chip(value, ahead):
    return lax.ppermute(value, "shard", [((i + 2 * ahead) % 8, i) for i in range(8)])


def to_chip(value, ahead):
    return lax.ppermute(value, "shard", [(i, (i + 2 * ahead) % 8) for i in range(8)])


def from_flip(value, which):
    flip = lambda s: which if s % 2 == 0 else 3 - which
    pairs = [(r * 8 + s, (r ^ flip(s)) * 8 + s) for r in range(4) for s in range(8)]
    return lax.ppermute(value, ("rep", "shard"), pairs)


def from_far(value):
    return lax.ppermute(value, "rep", [(i, i ^ 3) for i in range(4)])


def joined(*parts):
    return jnp.concatenate(parts, 0)


def after(value, *earlier):
    return lax.optimization_barrier((value,) + earlier)[0]


class Gather:
    def __init__(self, mine, own, other, own_places, depth):
        self.hops = [from_chip(mine, ahead) for ahead in (1, 2, 3)]
        self.own, self.other, self.own_places, self.depth = own, other, own_places, depth

    def collect(self, *earlier):
        hops = [hop[: self.depth] for hop in self.hops]
        self.got = joined(after(hops[0], *earlier), *hops[1:])

    def first(self, *earlier):
        self.collect(*earlier)
        self.one = from_flip(self.got, 1)

    def second(self, *earlier):
        self.low = joined(self.got, after(self.one, *earlier))
        self.high = from_flip(self.low, 2)

    def direct(self, *earlier):
        self.collect(*earlier)
        self.others = [lax.ppermute(self.got, "rep", [(i, i ^ flip) for i in range(4)]) for flip in (1, 2, 3)]

    def hold(self, *earlier):
        self.others = [after(other, *earlier) for other in self.others]

    def weight_direct(self):
        return self.planned([self.got] + self.others, "direct")

    def weight(self):
        return self.planned([self.low, self.high], "skew")

    def planned(self, mine, kind):
        own = [pltpu.with_memory_space_constraint(piece, pltpu.HBM) for piece in self.own]
        pieces = own + self.other + mine + [from_core(piece) for piece in mine]
        count = len(own)
        entries = [
            (i + count * other, at, unit, None, 0, self.depth, other)
            for other in (0, 1)
            for i, places in enumerate(self.own_places)
            for at, unit in places
        ]
        each = 4 // len(mine)
        arriving = []
        for position in range(4):
            for other in (0, 1):
                source = SWAPPED[position] if kind == "skew" and other else position
                piece = 2 * count + len(mine) * other + source // each
                for ahead in (1, 2, 3):
                    at = pl.ds((3 * (source % each) + ahead - 1) * self.depth, self.depth)
                    arriving.append((piece, at, None, source, ahead, self.depth, other))
        if self.own_places[0][0][1] is None:
            arriving.sort(key=lambda entry: entry[4])
        return (kind, tuple(entries + arriving)), pieces


def wide(value):
    return value.astype(F32)


class Reduce:
    def __init__(self, grads, extra=0):
        self.keep, self.send = grads
        self.extra = extra
        self.quarter = (self.keep.shape[0] - extra) // 4
        self.depth = self.quarter // 4

    def cores(self, *earlier):
        self.other = from_core(after(self.send, *earlier) if earlier else self.send)

    def first(self, *earlier):
        self.other = after(self.other, *earlier)
        n = 2 * self.quarter
        self.sent = (wide(self.keep[n:]) + wide(self.other[n:])).astype(BF)
        self.one = from_flip(self.sent, 1)

    def second(self, *earlier):
        self.one = after(self.one, *earlier)
        n, x = self.quarter, self.extra
        total = wide(self.keep[n : 2 * n]) + wide(self.other[n : 2 * n]) + wide(self.one[x + n :])
        if x:
            at = slice(2 * n, 2 * n + x)
            self.vector = wide(self.keep[at]) + wide(self.other[at]) + wide(self.one[:x])
            total = joined(total, self.vector)
        self.sent = total.astype(BF)
        self.two = from_flip(self.sent, 2)

    def chips(self, *earlier):
        self.two = after(self.two, *earlier)
        n, x, depth = self.quarter, self.extra, self.depth
        total = wide(self.keep[:n]) + wide(self.other[:n]) + wide(self.one[x : x + n]) + wide(self.two[:n])
        if x:
            self.vector = self.vector + wide(self.two[n:])
        self.total = total[:depth]
        self.hops = []
        self.sents = []
        for ahead in (1, 2, 3):
            part = total[ahead * depth : (ahead + 1) * depth]
            if x:
                part = joined(part, self.vector)
            self.sents.append(part.astype(BF))
            self.hops.append(to_chip(self.sents[-1], ahead))

    def share(self, *earlier):
        self.hops[0] = after(self.hops[0], *earlier)
        for hop in self.hops:
            self.total = self.total + wide(hop[: self.depth])
            if self.extra:
                self.vector = self.vector + wide(hop[self.depth :])
        self.total = self.total.astype(BF)
        self.backs = [from_flip(self.total, 1), from_flip(self.total, 2), from_far(self.total)]

    def units(self, place):
        at = [self.total] + self.backs
        rep, core = place[0], place[2]
        a, d = at[0], at[3]
        b, c = jnp.where(core == 0, at[1], at[2]), jnp.where(core == 0, at[2], at[1])
        odd, upper = rep % 2 == 1, rep >= 2
        a, b, c, d = jnp.where(odd, b, a), jnp.where(odd, a, b), jnp.where(odd, d, c), jnp.where(odd, c, d)
        return [wide(v) for v in (jnp.where(upper, c, a), jnp.where(upper, d, b), jnp.where(upper, a, c), jnp.where(upper, b, d))]


def row_weights(task, lengths, task_masks):
    token_task = jnp.repeat(task, LEN)
    chosen = jnp.where(token_task == 0, task_masks[0], jnp.where(token_task == 1, task_masks[1], task_masks[2]))
    valid = jnp.arange(LEN, dtype=jnp.int32)[None, :] < lengths[:, None]
    return (chosen * valid.astype(jnp.int32).reshape(-1)).astype(F32)[:, None]


def per_device(mesh_shape, *arrays):
    (tokens, cotangent, task, lengths, task_masks, w_qkv, qv_bias, w_out, out_bias, ln1_gain, ln1_bias, w_up, up_bias, w_down, down_bias, ln2_gain, ln2_bias) = arrays
    rows, width = tokens.shape
    shards = mesh_shape["shard"]
    hidden = up_bias.shape[0] * shards
    fast = shards == 8 and mesh_shape["rep"] == 4
    place = jnp.stack([lax.axis_index("rep"), lax.axis_index("shard") // 2, lax.axis_index("shard") % 2]).astype(jnp.int32)
    shard = lax.axis_index("shard")

    vectors = (qv_bias, out_bias, ln1_gain, ln1_bias, down_bias, ln2_gain, ln2_bias, up_bias)
    sizes = [v.shape[0] for v in vectors]

    if fast:
        depth = w_qkv.shape[0]
        rep = place[0]
        every = slice(None)

        def columns(first, count):
            return [((every, pl.ds(unit * width, width)), first + unit) for unit in range(count)]

        mine = lax.dynamic_slice(w_qkv, (0, jnp.minimum(rep, 2) * width), (depth, width))
        mine = jnp.where(rep == 3, w_out, mine)
        other_qkv, other_out, other_up, other_down = [from_core(after(own, mine)) for own in (w_qkv, w_out, w_up, w_down)]
        gather_a = Gather(mine, [w_qkv, w_out], [other_qkv, other_out], [columns(0, 3), columns(3, 1)], depth)
        gather_a.direct(other_qkv, other_out, other_up, other_down)
        packed = jnp.concatenate(after(vectors, gather_a.got))
        packed_rows = jnp.pad(packed, (0, 16 * width - packed.shape[0])).reshape(16, width)
        mine = joined(lax.dynamic_slice(w_up, (0, rep * width), (depth, width)), packed_rows)
        gather_b = Gather(mine, [w_up], [other_up], [columns(0, 4)], depth)
        vec_hops = [after(gather_b.hops[0], gather_a.got)] + gather_b.hops[1:]
        vec_rows = jnp.stack([packed_rows] + [hop[depth:] for hop in vec_hops])
        vec_rows = jnp.stack([vec_rows, from_core(vec_rows)], 1).reshape(8, -1)[:, : packed.shape[0]]
        index = jnp.arange(8)
        slot = 2 * ((index // 2 - place[1]) % 4) + ((index % 2) ^ place[2])
        pick = (slot[:, None] == index[None, :]).astype(BF)
        all_vectors = jnp.dot(pick, vec_rows, preferred_element_type=F32)
        row_weight = row_weights(*after((task, lengths, task_masks), gather_a.got))
    else:
        row_weight = row_weights(task, lengths, task_masks)
        packed = jnp.concatenate(vectors)
        all_vectors = lax.all_gather(packed, "shard", axis=0).astype(F32)
        full_a = jnp.concatenate([lax.all_gather(w_qkv, "shard", axis=0, tiled=True), lax.all_gather(w_out, "shard", axis=0, tiled=True)], 1)
        full_b = lax.all_gather(w_up, "shard", axis=0, tiled=True)
        weight_a = (WHOLE, [full_a.reshape(width, 4, width).transpose(1, 0, 2)])
        weight_b = (WHOLE, [full_b.reshape(width, 4, width).transpose(1, 0, 2)])
        full_c = lax.all_gather(w_down, "shard", axis=0, tiled=True)
        weight_c = (WHOLE, [full_c.reshape(4, -1, width)])

    full, start = [], 0
    for size in sizes:
        full.append(all_vectors[:, start : start + size].reshape(-1))
        start += size
    qv, out_shift, gain_one, shift_one, down_shift, gain_two, shift_two, up_shift = full
    qkv_shift = jnp.concatenate([qv[:width], jnp.zeros((width,), F32), qv[width:]])[None]
    vecs = jnp.stack([out_shift, gain_one, shift_one, down_shift, gain_two, shift_two, shift_two, shift_two])
    up_shift = up_shift[None]

    if fast:
        gather_a.hold(qkv_shift, vecs, up_shift, row_weight)
        weight_a = gather_a.weight_direct()
        gather_b.first()
        gather_b.second(*gather_a.others)
        mine = lax.dynamic_slice(w_down, (rep * depth, 0), (depth, width))
        own = [[(pl.ds(0, 4 * depth), None)]]
        mine = after(mine, gather_b.low)
        gather_c = Gather(mine, [w_down], [other_down], own, depth)
        qkv_shift = after(qkv_shift, gather_b.low, mine)
    proj, context, lse, w_a = attention_forward(place, lengths, tokens, qkv_shift, weight_a)
    if fast:
        gather_c.direct(context)
        gather_b.high = after(gather_b.high, gather_c.got)
        weight_b = gather_b.weight()
        context = after(context, gather_c.got)
    norm_one, scale_one, first_low, act, slope, w_b = middle(place, tokens, context, w_a, vecs, up_shift, weight_b)
    if fast:
        gather_c.hold(act)
        weight_c = gather_c.weight_direct()
    output, dffn, sums_two, down_full, grads_c = ffn(place, act, weight_c, norm_one, cotangent, row_weight, vecs, shards, fast)
    if fast:
        group_c = Reduce(grads_c)
        group_c.cores()
    dinner, sums_up, grads_b = inner_grads(place, dffn, first_low, down_full, slope, fast)
    if fast:
        group_c.first(dinner)
        group_b = Reduce(grads_b)
        group_b.cores(group_c.sent)
        dinner = after(dinner, group_c.sent)
    dattended, dcontext, sums_one = first_grad(dinner, w_b, dffn, norm_one, scale_one, vecs, w_a)
    if fast:
        group_b.first(dcontext)
        group_c.second(dcontext)
        lse = after(lse, group_b.sent, group_c.sent)
    sums = jnp.concatenate([sums_one[2], sums_one[0], sums_one[1], sums_two[2], sums_two[0], sums_two[1], sums_up[0]])
    pre = jnp.pad(sums.reshape(-1, width), ((2, 4), (0, 0))).astype(BF)
    dproj, grads_a, sums_qkv = attention_back(place, lengths, proj, dcontext, lse, tokens, context, dattended, pre, fast)
    if fast:
        group_a = Reduce(grads_a, pre.shape[0])
        group_c.two, group_b.one = after(group_c.two, *grads_a), after(group_b.one, *grads_a)
        group_a.cores(group_c.two, group_b.one)
        group_c.chips()
        group_a.first(*group_c.sents)
        group_b.second(group_a.sent)
        dproj = after(dproj, group_b.sent)
    grad_input = input_grad(dproj, w_a, dattended)

    starts = [0]
    for size in sizes:
        starts.append(starts[-1] + size * shards)
    if fast:
        group_c.share(grad_input)
        group_b.chips(group_c.total)
        group_a.second(*group_b.sents)
        group_a.chips()
        group_b.share(*group_a.sents)
        group_c.backs = [after(back, *group_a.sents) for back in group_c.backs]
        group_b.backs = [after(back, *group_a.sents) for back in group_b.backs]
        group_a.share()
        units_a, units_b, units_c = [group.units(place) for group in (group_a, group_b, group_c)]
        sums = group_a.vector.reshape(-1)
    else:
        units = []
        for (grads,) in (grads_b, grads_a):
            summed = lax.psum_scatter(grads, "shard", scatter_dimension=1, tiled=True)
            units.append([wide(unit) for unit in lax.psum(summed.astype(BF), "rep")])
        units_b, units_a = units
        summed = lax.psum(lax.psum_scatter(grads_c[0], "shard", scatter_dimension=0, tiled=True), "rep")[0]
        units_c = [wide(unit) for unit in jnp.split(summed, 4)]
        sums = jnp.concatenate([sums_qkv[0, :width], sums_qkv[0, 2 * width :], sums])
        sums = lax.psum(sums, ("rep", "shard"))
    final = [lax.dynamic_slice(sums, (start + shard * size,), (size,)) for start, size in zip(starts, sizes)]
    f_qv, f_out_shift, f_gain_one, f_shift_one, f_down_shift, f_gain_two, f_shift_two, f_up_shift = final
    wide_b = jnp.concatenate(units_b, 1)
    wide_a = jnp.concatenate(units_a[:3], 1)
    final_c = jnp.concatenate(units_c, 0).T
    return (output, grad_input, wide_a, f_qv, units_a[3], f_out_shift, f_gain_one, f_shift_one, wide_b, f_up_shift, final_c, f_down_shift, f_gain_two, f_shift_two)


def solution(mesh):
    split, shard = P(("rep", "shard"), None), P("shard")
    flat, matrix = P(("rep", "shard")), P("shard", None)
    in_specs = (split, split, flat, flat, P(None, ("rep", "shard")), matrix, shard, matrix, shard, shard, shard, matrix, shard, matrix, shard, shard, shard)
    out_specs = (split, split, matrix, shard, matrix, shard, shard, shard, matrix, shard, matrix, shard, shard, shard)
    return jax.shard_map(
        functools.partial(per_device, dict(mesh.shape)), mesh=mesh, in_specs=in_specs, out_specs=out_specs, check_vma=False
    )
```

```python
import functools
import math

import jax
import jax.numpy as jnp
from jax import lax
from jax.experimental import pallas as pl
from jax.experimental.pallas import tpu as pltpu
from jax.sharding import PartitionSpec as P

HD = 64
LEN = 128
EPSILON = 1e-06
BF = jnp.bfloat16
F32 = jnp.float32
MIB = 1024 * 1024

ROOT_HALF = 0.7071067811865476
DENSITY = 0.3989422804014327


def dot_nn(left, right):
    return jnp.dot(left, right, preferred_element_type=F32)


def dot_nt(left, right):
    return lax.dot_general(left, right, (((1,), (1,)), ((), ())), preferred_element_type=F32)


def dot_tn(left, right):
    return lax.dot_general(left, right, (((0,), (0,)), ((), ())), preferred_element_type=F32)


def gelu_parts(inner):
    phi = 0.5 + 0.5 * lax.erf(inner * ROOT_HALF)
    bell = jnp.exp(inner * inner * -0.5) * DENSITY
    return inner * phi, phi + inner * bell


def norm_parts(summed):
    centre = jnp.mean(summed, -1, keepdims=True)
    deviation = summed - centre
    variance = jnp.mean(deviation * deviation, -1, keepdims=True)
    rscale = lax.rsqrt(variance + EPSILON)
    return deviation * rscale, rscale


def norm_back(grad_norm, normed, rscale):
    first_mean = jnp.mean(grad_norm, -1, keepdims=True)
    second_mean = jnp.mean(grad_norm * normed, -1, keepdims=True)
    return rscale * (grad_norm - first_mean - normed * second_mean)


def add_rows(total_ref, rows):
    @pl.when(pl.program_id(0) == 0)
    def _():
        total_ref[...] = jnp.zeros_like(total_ref)

    for at, values in enumerate(rows):
        total_ref[at : at + 1, :] += jnp.sum(values, 0, keepdims=True)


def cost(flops, moved):
    return pl.CostEstimate(flops=1000, bytes_accessed=1000, transcendentals=0)


def params(vmem=28):
    return pltpu.CompilerParams(vmem_limit_bytes=vmem * MIB)


def halves_of(step, block):
    half = block // 2
    return [(slice(at, at + half), pl.ds(pl.multiple_of(step * block + at, half), half)) for at in (0, half)]


def rows_at(step, block):
    return pl.ds(pl.multiple_of(step * block, block), block)


def whole(shape):
    return pl.BlockSpec(shape, lambda i, *_: (0,) * len(shape))


def rows_of(block, width):
    return pl.BlockSpec((block, width), lambda i, *_: (i, 0))


def head_masks():
    lane = lax.broadcasted_iota(jnp.int32, (1, 2 * HD), 1)
    return (lane < HD).astype(BF), (lane >= HD).astype(BF)


def stack_heads(pair, masks):
    return jnp.concatenate([pair * masks[0], pair * masks[1]], axis=0)


def attention_forward_kernel(plan, count_of_pieces, place, lengths, x_ref, shift_ref, *refs):
    pieces, (proj_ref, ctx_ref, lse_ref, w_out_ref, w_ref, sems) = refs[: count_of_pieces], refs[count_of_pieces :]
    block, width = x_ref.shape
    step = pl.program_id(0)

    def body(ready):
        x = x_ref[...]
        for i in range(4):
            unit = ready(i)

            @pl.when(unit < 3)
            def _():
                at = pl.ds(pl.multiple_of(unit * width, width), width)
                proj_ref[:, at] = (dot_nn(x, w_ref[unit]) + shift_ref[:, at]).astype(BF)

        masks = head_masks()
        lane = lax.broadcasted_iota(jnp.int32, (1, LEN), 1)
        for seq in range(block // LEN):
            number = step * (block // LEN) + seq
            rows = rows_at(number, LEN)
            here = slice(seq * LEN, (seq + 1) * LEN)
            valid = lane < lengths[number]
            lse = jnp.zeros((LEN, LEN), F32)
            pairs = range(width // (2 * HD))

            def part(offset, pair):
                return proj_ref[here, offset + pair * 2 * HD : offset + (pair + 1) * 2 * HD]

            stage = [dot_nt(part(0, pair) * BF(0.125), stack_heads(part(width, pair), masks)) for pair in pairs]
            later = []
            for pair, scores in zip(pairs, stage):
                probs = []
                for half in range(2):
                    masked = jnp.where(valid, scores[:, half * LEN : (half + 1) * LEN], -1e9)
                    top = jnp.max(masked, -1, keepdims=True)
                    exponent = jnp.exp(masked - top)
                    total = jnp.sum(exponent, -1, keepdims=True)
                    probs.append((exponent * (1.0 / total)).astype(BF))
                    lse = jnp.where(lane == 2 * pair + half, top + jnp.log(total), lse)
                later.append(jnp.concatenate(probs, axis=1))
            for pair, probs in zip(pairs, later):
                ctx = dot_nn(probs, stack_heads(part(2 * width, pair), masks))
                ctx_ref[rows, pair * 2 * HD : (pair + 1) * 2 * HD] = ctx.astype(BF)
            lse_ref[number] = lse.T[: lse_ref.shape[1]]

    first_and_later(Bring(plan, place, pieces, w_ref, sems, w_out_ref=w_out_ref), body)


SWAPPED = (0, 2, 1, 3)


def flip_of(position, core):
    return {0: 0, 1: 1 + core, 2: 2 - core, 3: 3}[position]


class Bring:
    def __init__(self, plan, place, pieces, w_ref, sems, rows_first=False, w_out_ref=None):
        self.kind, self.entries = plan
        self.place, self.pieces = place, pieces
        self.w_ref, self.w_out_ref, self.sems, self.rows_first = w_ref, w_out_ref, sems, rows_first
        self.span = w_ref.shape[0] // 4

    def part(self, ref, at):
        return ref.at[rows_at(at, self.span)] if self.rows_first else ref.at[at]

    def unit(self, position, other):
        rep, core = self.place[0], self.place[2]
        return rep ^ (position if self.kind == "direct" else flip_of(position, core ^ other))

    def round(self, i):
        if self.kind == "whole":
            return i
        return (self.place[1] + i) % 4 if self.rows_first else self.unit(i, 0)

    def start(self):
        if self.kind == "whole":
            for at in range(4):
                pltpu.make_async_copy(self.pieces[0].at[at], self.part(self.w_ref, at), self.sems.at[at]).start()
            return
        chip, core = self.place[1], self.place[2]
        for piece, at, unit, position, ahead, depth, other in self.entries:
            to_unit = unit if position is None else self.unit(position, other)
            to_chip = (chip + ahead) % 4
            shard = 2 * to_chip + (core ^ other)
            if self.rows_first:
                first = 4 * shard if to_unit is None else 4 * shard + to_unit
                count = 4 * depth if to_unit is None else depth
                group, to = to_chip, self.w_ref.at[pl.ds(pl.multiple_of(first * depth, 16), count)]
            else:
                group, to = to_unit, self.w_ref.at[to_unit, pl.ds(pl.multiple_of(shard * depth, 16), depth)]
            pltpu.make_async_copy(self.pieces[piece].at[at], to, self.sems.at[group]).start()

    def wait(self, at):
        here = self.part(self.w_ref, at)
        pltpu.make_async_copy(here, here, self.sems.at[at]).wait()
        if self.w_out_ref is not None:
            self.onward(at).start()

    def onward(self, at):
        return pltpu.make_async_copy(self.part(self.w_ref, at), self.part(self.w_out_ref, at), self.sems.at[4 + at])

    def finish(self):
        for at in range(4):
            self.onward(at).wait()


def first_and_later(bring, body):
    @pl.when(pl.program_id(0) == 0)
    def _():
        bring.start()

        def ready(i):
            at = bring.round(i)
            bring.wait(at)
            return at

        body(ready)

    @pl.when(pl.program_id(0) > 0)
    def _():
        body(bring.round)

    if bring.w_out_ref is not None:

        @pl.when(pl.program_id(0) == pl.num_programs(0) - 1)
        def _():
            bring.finish()


ANY = pl.BlockSpec(memory_space=pl.ANY)
HELD = pl.BlockSpec(memory_space=pltpu.VMEM)
FAR = pl.BlockSpec(memory_space=pl.ANY)


def call(kernel, in_specs, out_specs, out_shape, grid, scalars, scratch_shapes, vmem, name):
    def space(spec, shape, result):
        large = math.prod(shape.shape) * shape.dtype.itemsize > MIB // 2
        if spec is HELD:
            return pltpu.VMEM
        return pltpu.HBM if spec is FAR or large and (result or spec is not ANY) else None

    def placed(spec, shape):
        where = space(spec, shape, True)
        return shape if where is None else where(shape.shape, shape.dtype)

    run = pl.pallas_call(
        kernel,
        grid_spec=pltpu.PrefetchScalarGridSpec(
            num_scalar_prefetch=scalars, grid=grid, in_specs=in_specs, out_specs=out_specs, scratch_shapes=scratch_shapes
        ),
        out_shape=[placed(spec, shape) for spec, shape in zip(out_specs, out_shape)],
        compiler_params=params(vmem),
        cost_estimate=cost(0, 0),
        name=name,
    )

    def constrained(spec, arg):
        where = space(spec, arg, False)
        return arg if where is None else pltpu.with_memory_space_constraint(arg, where)

    def apply(*args):
        return run(*args[:scalars], *[constrained(spec, arg) for spec, arg in zip(in_specs, args[scalars:])])

    return apply


WHOLE = ("whole", ())


def attention_forward(place, lengths, tokens, shift, weight):
    rows, width = tokens.shape
    block = 2 * LEN
    heads = width // HD
    lse_rows = -(-heads // 8) * 8
    plan, pieces = weight
    return call(
        functools.partial(attention_forward_kernel, plan, len(pieces)),
        in_specs=[rows_of(block, width), whole((1, 3 * width))] + [FAR] * len(pieces),
        out_specs=[rows_of(block, 3 * width), HELD, HELD, ANY],
        out_shape=[
            jax.ShapeDtypeStruct((rows, 3 * width), BF),
            jax.ShapeDtypeStruct((rows, width), BF),
            jax.ShapeDtypeStruct((rows // LEN, lse_rows, LEN), F32),
            jax.ShapeDtypeStruct((4, width, width), BF),
        ],
        grid=(rows // block,),
        scalars=2,
        scratch_shapes=[pltpu.VMEM((4, width, width), BF), pltpu.SemaphoreType.DMA((8,))],
        vmem=28,
        name="attention_forward",
    )(place, lengths, tokens, shift, *pieces)


def middle_kernel(plan, count_of_pieces, place, x_ref, ctx_ref, w_attn_ref, vec_ref, up_shift_ref, *refs):
    pieces = refs[: count_of_pieces]
    norm_ref, scale_ref, low_ref, act_ref, slope_ref, w_out_ref, w_ref, sems = refs[count_of_pieces :]
    block, width = x_ref.shape

    def body(ready):
        halves = halves_of(pl.program_id(0), block)
        attended = [dot_nn(ctx_ref[here, :], w_attn_ref[0]) + vec_ref[0:1, :] for _, here in halves]
        lows = []
        for (local, here), value in zip(halves, attended):
            normed, rscale = norm_parts(x_ref[local, :].astype(F32) + value)
            norm_ref[here, :] = normed.astype(BF)
            scale_ref[here, :] = rscale
            lows.append((normed * vec_ref[1:2, :] + vec_ref[2:3, :]).astype(BF))
            low_ref[here, :] = lows[-1]
        for i in range(w_ref.shape[0]):
            unit = ready(i)
            at = pl.ds(pl.multiple_of(unit * width, width), width)
            for (_, here), low in zip(halves, lows):
                act, slope = gelu_parts(dot_nn(low, w_ref[unit]) + up_shift_ref[:, at])
                act_ref[here, at] = act.astype(BF)
                slope_ref[here, at] = slope.astype(BF)

    first_and_later(Bring(plan, place, pieces, w_ref, sems, w_out_ref=w_out_ref), body)


def middle(place, tokens, context, w_qkvo, vecs, up_shift, weight, block=512):
    rows, width = tokens.shape
    hidden = up_shift.shape[1]
    units = hidden // width
    plan, pieces = weight
    return call(
        functools.partial(middle_kernel, plan, len(pieces)),
        in_specs=[
                rows_of(block, width),
                HELD,
                pl.BlockSpec((1, width, width), lambda i, *_: (3, 0, 0)),
                whole(vecs.shape),
                whole(up_shift.shape),
            ]
            + [FAR] * len(pieces),
        out_specs=[HELD] * 5 + [ANY],
        out_shape=[
            jax.ShapeDtypeStruct((rows, width), BF),
            jax.ShapeDtypeStruct((rows, 1), F32),
            jax.ShapeDtypeStruct((rows, width), BF),
            jax.ShapeDtypeStruct((rows, hidden), BF),
            jax.ShapeDtypeStruct((rows, hidden), BF),
            jax.ShapeDtypeStruct((units, width, width), BF),
        ],
        grid=(rows // block,),
        scalars=1,
        scratch_shapes=[pltpu.VMEM((units, width, width), BF), pltpu.SemaphoreType.DMA((8,))],
        vmem=28,
        name="middle",
    )(place, tokens, context, w_qkvo, vecs, up_shift, *pieces)


def ffn_kernel(plan, count_of_pieces, relative, place, act_ref, norm_ref, cot_ref, weight_ref, vec_ref, *refs):
    pieces, refs = refs[: count_of_pieces], refs[count_of_pieces :]
    out_ref, low_ref, sum_ref, w_out_ref, *refs = refs
    outs, refs = refs[: 2 if relative else 1], refs[2 if relative else 1 :]
    turned_ref, w_ref, stage_ref, sems, w_sems = refs
    step = pl.program_id(0)
    block, width = cot_ref.shape
    count = act_ref.shape[0] // block
    halves = halves_of(jnp.minimum(step, count - 1), block)
    bring = Bring(plan, place, pieces, w_ref, w_sems, rows_first=True, w_out_ref=w_out_ref)

    def finish(local, here, ffn):
        first = norm_ref[here, :].astype(F32) * vec_ref[1:2, :] + vec_ref[2:3, :]
        normed, rscale = norm_parts(first + (ffn + vec_ref[3:4, :]))
        out_ref[local, :] = (normed * vec_ref[4:5, :] + vec_ref[5:6, :]).astype(BF)
        grad = cot_ref[local, :].astype(F32) * weight_ref[local, :]
        low = norm_back(grad * vec_ref[4:5, :], normed, rscale).astype(BF)
        low_ref[here, :] = low
        turned_ref[:, here] = low.T
        for at, values in enumerate((grad * normed, grad, low.astype(F32))):
            sum_ref[at : at + 1, :] += jnp.sum(values, 0, keepdims=True)

    @pl.when(step == 0)
    def _():
        bring.start()
        sum_ref[...] = jnp.zeros_like(sum_ref)
        ffns = [0.0, 0.0]
        for i in range(4):
            part = bring.round(i)
            bring.wait(part)
            at = rows_at(part, bring.span)
            ffns = [ffn + dot_nn(act_ref[here, at], w_ref[at, :]) for ffn, (_, here) in zip(ffns, halves)]
        for (local, here), ffn in zip(halves, ffns):
            finish(local, here, ffn)

    @pl.when((step > 0) & (step < count))
    def _():
        ffns = [dot_nn(act_ref[here, :], w_ref[...]) for _, here in halves]
        for (local, here), ffn in zip(halves, ffns):
            finish(local, here, ffn)

    def left(slot):
        here = stage_ref.at[slot]
        pltpu.make_async_copy(here, here, sems.at[slot]).wait()

    if relative:

        @pl.when(step >= count + 2)
        def _():
            left(step % 2)

    @pl.when(step >= count)
    def _():
        at = step - count
        columns = pl.ds(pl.multiple_of(at * width, width), width)
        grad = dot_nn(turned_ref[...], act_ref[:, columns]).astype(BF)
        if not relative:
            each, _, part = outs[0].shape
            for i in range(each):
                outs[0][i] = grad[:, i * part : (i + 1) * part]
            return
        rep, chip, core = place[0], place[1], place[2]
        part, depth = width // 2, width // 4
        slot = step % 2
        for half in range(2):
            stage_ref[slot, half] = grad[:, half * part : (half + 1) * part]
        ahead = (at - chip) % 4
        for unit in range(4):
            rows = pl.ds(unit * depth, depth)
            for ref, whose in zip(outs, (core, 1 - core)):
                to = pl.multiple_of((4 * slot_of(unit, rep, whose) + ahead) * depth, 16)
                pltpu.make_async_copy(stage_ref.at[slot, whose, rows], ref.at[pl.ds(to, depth)], sems.at[slot]).start()

    @pl.when(step == pl.num_programs(0) - 1)
    def _():
        bring.finish()
        if relative:
            left(0)
            left(1)


def once(shape):
    return pl.BlockSpec(shape, lambda i, *_: (0,) * len(shape), pipeline_mode=pl.Buffered(1))


def ffn(place, act, weight, norm_one, cotangent, row_weight, vecs, shards, relative, block=512):
    rows, width = cotangent.shape
    hidden = act.shape[1]
    part = hidden // shards
    each = width // part
    count = rows // block
    plan, pieces = weight
    if relative:
        out_specs = [ANY] * 2
        out_shape = [jax.ShapeDtypeStruct((4 * width, part), BF)] * 2
    else:
        out_specs = [pl.BlockSpec((each, width, part), lambda i, *_: (jnp.maximum(i - count, 0), 0, 0))]
        out_shape = [jax.ShapeDtypeStruct((shards, width, part), BF)]
    early = lambda columns: pl.BlockSpec((block, columns), lambda i, *_: (jnp.minimum(i, count - 1), 0))
    output, low, sums, w_down, *grads = call(
        functools.partial(ffn_kernel, plan, len(pieces), relative),
        in_specs=[HELD, HELD, early(width), early(1), whole(vecs.shape)] + [FAR] * len(pieces),
        out_specs=[early(width), HELD, whole((8, width)), ANY] + out_specs,
        out_shape=[
            jax.ShapeDtypeStruct((rows, width), BF),
            jax.ShapeDtypeStruct((rows, width), BF),
            jax.ShapeDtypeStruct((8, width), F32),
            jax.ShapeDtypeStruct((hidden, width), BF),
        ]
        + out_shape,
        grid=(count + shards // each,),
        scalars=1,
        scratch_shapes=[
            pltpu.VMEM((width, rows), BF),
            pltpu.VMEM((hidden, width), BF),
            pltpu.VMEM((2, 2, width, width // 2), BF),
            pltpu.SemaphoreType.DMA((2,)),
            pltpu.SemaphoreType.DMA((8,)),
        ],
        vmem=28,
        name="ffn",
    )(place, act, norm_one, cotangent, row_weight, vecs, *pieces)
    return output, low, sums, w_down, grads


class Outward:
    def __init__(self, stage_ref, sems):
        self.step = pl.program_id(0)
        self.slot = self.step % 2
        self.stage_ref, self.sems = stage_ref, sems

    def free(self):
        @pl.when(self.step >= 2)
        def _():
            self.wait(self.slot)

    def stage(self):
        return self.stage_ref.at[self.slot]

    def send(self, *pairs):
        for source, to in pairs:
            pltpu.make_async_copy(source, to, self.sems.at[self.slot]).start()

    def wait(self, slot):
        here = self.stage_ref.at[slot]
        pltpu.make_async_copy(here, here, self.sems.at[slot]).wait()

    def finish(self):
        @pl.when(self.step == pl.num_programs(0) - 1)
        def _():
            self.wait(1 - self.slot)
            self.wait(self.slot)


def slot_of(unit, rep, core):
    e = unit ^ rep
    return jnp.where(core == 0, 2 * (e % 2) + e // 2, e)


def send_units(place, grad, out, outs, extra, unit=None):
    rep, chip, core = place[0], place[1], place[2]
    depth = grad.shape[0] // 8
    unit = pl.program_id(0) if unit is None else unit
    stage = out.stage()
    stage[...] = grad
    for ref, whose in zip(outs, (core, 1 - core)):
        slot = slot_of(unit, rep, whose)
        for other in range(4):
            ahead = (other - chip) % 4
            to = pl.multiple_of((4 * slot + ahead) * depth + jnp.where(slot >= 2, extra, 0), 16)
            row = pl.multiple_of((2 * other + whose) * depth, 16)
            out.send((stage.at[pl.ds(row, depth)], ref.at[pl.ds(to, depth)]))


def inner_grads_kernel(relative, place, low_ref, w_ref, slope_ref, first_ref, inner_ref, sum_ref, *refs):
    outs, refs = refs[: 2 if relative else 1], refs[2 if relative else 1 :]
    turned_ref, stage_ref, sems = refs
    step = pl.program_id(0)
    rows, width = low_ref.shape
    columns = pl.ds(pl.multiple_of(step * width, width), width)

    @pl.when(step == 0)
    def _():
        turned_ref[...] = first_ref[...].T

    total = 0.0
    for at in range(0, rows, 256):
        here = slice(at, at + 256)
        grad = (dot_nt(low_ref[here, :], w_ref[...]) * slope_ref[here, columns].astype(F32)).astype(BF)
        inner_ref[here, columns] = grad
        total = total + jnp.sum(grad.astype(F32), 0, keepdims=True)
    sum_ref[0:1, :] = total

    grad = dot_nn(turned_ref[...], inner_ref[:, columns]).astype(BF)
    if relative:
        out = Outward(stage_ref, sems)
        out.free()
        send_units(place, grad, out, outs, 0)
        out.finish()
    else:
        outs[0][0] = grad


def inner_grads(place, low, first, w_down, slope, relative):
    rows, width = low.shape
    hidden = slope.shape[1]
    columns = lambda height: pl.BlockSpec((height, width), lambda i, place: (0, i))
    if relative:
        out_specs = [ANY] * 2
        out_shape = [jax.ShapeDtypeStruct((2 * width, width), BF)] * 2
    else:
        out_specs = [pl.BlockSpec((1, width, width), lambda i, place: (i, 0, 0))]
        out_shape = [jax.ShapeDtypeStruct((4, width, width), BF)]
    inner, sums, *grads = call(
        functools.partial(inner_grads_kernel, relative),
        in_specs=[HELD, pl.BlockSpec((width, width), lambda i, place: (i, 0)), HELD, HELD],
        out_specs=[HELD, columns(8)] + out_specs,
        out_shape=[jax.ShapeDtypeStruct((rows, hidden), BF), jax.ShapeDtypeStruct((8, hidden), F32)] + out_shape,
        grid=(hidden // width,),
        scalars=1,
        scratch_shapes=[
            pltpu.VMEM((width, rows), BF),
            pltpu.VMEM((2, width, width), BF),
            pltpu.SemaphoreType.DMA((2,)),
        ],
        vmem=28,
        name="inner_grads",
    )(place, low, w_down, slope, first)
    return inner, sums, grads


def first_grad_kernel(inner_ref, w_hbm_ref, low_in_ref, norm_ref, scale_ref, vec_ref, w_attn_ref, low_ref, ctx_ref, sum_ref, w_ref, sems):
    width = norm_ref.shape[1]
    halves = halves_of(pl.program_id(0), 512)

    @pl.when(pl.program_id(0) == 0)
    def _():
        sum_ref[...] = jnp.zeros_like(sum_ref)

    def body(ready):
        grads = [low_in_ref[here, :].astype(F32) for _, here in halves]
        for unit in range(4):
            ready(unit)
            at = slice(unit * width, (unit + 1) * width)
            grads = [grad + dot_nt(inner_ref[here, at], w_ref[unit]) for grad, (_, here) in zip(grads, halves)]
        for grad, (_, here) in zip(grads, halves):
            normed = norm_ref[here, :].astype(F32)
            low = norm_back(grad * vec_ref[1:2, :], normed, scale_ref[here, :]).astype(BF)
            low_ref[here, :] = low
            ctx_ref[here, :] = dot_nt(low, w_attn_ref[0]).astype(BF)
            for at, values in enumerate((grad * normed, grad, low.astype(F32))):
                sum_ref[at : at + 1, :] += jnp.sum(values, 0, keepdims=True)

    first_and_later(Bring(WHOLE, (0, 0, 0), [w_hbm_ref], w_ref, sems), body)


def first_grad(inner, w_up, low, norm_one, scale_one, vecs, w_qkvo, block=512):
    rows, width = low.shape
    hidden = inner.shape[1]
    return call(
        first_grad_kernel,
        in_specs=[
            HELD,
            FAR,
            HELD,
            HELD,
            HELD,
            whole(vecs.shape),
            pl.BlockSpec((1, width, width), lambda i: (3, 0, 0)),
        ],
        out_specs=[HELD, HELD, whole((8, width))],
        out_shape=[
            jax.ShapeDtypeStruct((rows, width), BF),
            jax.ShapeDtypeStruct((rows, width), BF),
            jax.ShapeDtypeStruct((8, width), F32),
        ],
        grid=(rows // block,),
        scalars=0,
        scratch_shapes=[pltpu.VMEM(w_up.shape, BF), pltpu.SemaphoreType.DMA((4,))],
        vmem=28,
        name="first_grad",
    )(inner, w_up, low, norm_one, scale_one, vecs, w_qkvo)


def attention_back_kernel(relative, place, lengths, proj_ref, dctx_ref, lse_ref, one_ref, two_ref, up_ref, attn_ref, ctx_ref, x_hbm_ref, held_ref, *refs):
    outs, refs = refs[: 2 if relative else 1], refs[2 if relative else 1 :]
    sum_ref, x_ref, turned_ref, stage_ref, sums_ref, sems, sum_sems, late_sem = refs
    step = pl.program_id(0)
    width = dctx_ref.shape[1]
    block = 2 * LEN
    count = held_ref.shape[0] // block
    extra = sums_ref.shape[0]
    late = pltpu.make_async_copy(x_hbm_ref, x_ref, late_sem)

    @pl.when(step == 0)
    def _():
        sum_ref[...] = jnp.zeros_like(sum_ref)
        late.start()

    @pl.when(step == 1)
    def _():
        late.wait()
        turned_ref[...] = x_ref[...].T

    @pl.when(step < count)
    def _():
        masks = head_masks()
        lane = lax.broadcasted_iota(jnp.int32, (1, 2 * HD), 1)
        key = lax.broadcasted_iota(jnp.int32, (LEN, 1), 0)
        for seq in range(block // LEN):
            number = step * (block // LEN) + seq
            rows = rows_at(number, LEN)
            here_rows = slice(seq * LEN, (seq + 1) * LEN)
            valid = key < lengths[number]
            pairs = range(width // (2 * HD))

            def part(ref, where, offset, pair):
                return ref[where, offset + pair * 2 * HD : offset + (pair + 1) * 2 * HD]

            stage = []
            for pair in pairs:
                q = part(proj_ref, here_rows, 0, pair) * BF(0.125)
                dctx = part(dctx_ref, rows, 0, pair)
                queries, grads = stack_heads(q, masks), stack_heads(dctx, masks)
                scores = dot_nt(part(proj_ref, here_rows, width, pair), queries)
                dprobs = dot_nt(part(proj_ref, here_rows, 2 * width, pair), grads)
                stage.append((queries, grads, scores, dprobs))
            later = []
            for pair, (queries, grads, scores, dprobs) in zip(pairs, stage):
                probs, dscores = [], []
                for half in range(2):
                    here = slice(half * LEN, (half + 1) * LEN)
                    lse = lse_ref[number, 2 * pair + half : 2 * pair + half + 1, :]
                    prob = jnp.exp(jnp.where(valid, scores[:, here], -1e9) - lse)
                    dprob = dprobs[:, here]
                    inner = jnp.sum(prob * dprob, 0, keepdims=True)
                    dscores.append((prob * (dprob - inner)).astype(BF))
                    probs.append(prob.astype(BF))
                turned = jnp.concatenate([dscore.T for dscore in dscores], axis=1)
                later.append((queries, grads, jnp.concatenate(probs, axis=1), jnp.concatenate(dscores, axis=1), turned))
            for pair, (queries, grads, probs, dscores, turned) in zip(pairs, later):
                dv = dot_nn(probs, grads).astype(BF)
                dk = dot_nn(dscores, queries).astype(BF)
                dq = (dot_nn(turned, stack_heads(part(proj_ref, here_rows, width, pair), masks)) * 0.125).astype(BF)
                at = pair * 2 * HD
                for offset, grad in ((0, dq), (width, dk), (2 * width, dv)):
                    held_ref[rows, offset + at : offset + at + 2 * HD] = grad
                    if offset != width:
                        sum_ref[0:1, offset + at : offset + at + 2 * HD] += jnp.sum(grad.astype(F32), 0, keepdims=True)

    if relative:
        out = Outward(stage_ref, sems)
        copies = [
            pltpu.make_async_copy(sums_ref, ref.at[pl.ds(width, extra)], sum_sems.at[i])
            for i, ref in enumerate(outs)
        ]

        @pl.when(step == count)
        def _():
            rows = [sum_ref[0:1, :width], sum_ref[0:1, 2 * width :], one_ref[2:3, :], one_ref[0:1, :], one_ref[1:2, :]]
            rows += [two_ref[2:3, :], two_ref[0:1, :], two_ref[1:2, :]]
            rows += [up_ref[0:1, at : at + width] for at in range(0, up_ref.shape[1], width)]
            rows += [jnp.zeros((1, width), F32)] * (extra - len(rows))
            sums_ref[...] = jnp.concatenate(rows, axis=0).astype(BF)
            for copy in copies:
                copy.start()

    def put(unit, grad):
        if not relative:
            outs[0][0] = grad
            return

        @pl.when(step >= count + 2)
        def _():
            out.wait(out.slot)

        send_units(place, grad, out, outs, extra, unit)

    for unit in range(3):

        @pl.when(step == count + unit)
        def _():
            put(unit, dot_nn(turned_ref[...], held_ref[:, unit * width : (unit + 1) * width]).astype(BF))

    @pl.when(step == count + 3)
    def _():
        turned_ref[...] = ctx_ref[...].T
        put(3, dot_nn(turned_ref[...], attn_ref[...]).astype(BF))
        if relative:
            for copy in copies:
                copy.wait()

    if relative:
        out.finish()


def attention_back(place, lengths, proj, dctx, lse, tokens, context, dattended, sums, relative):
    rows, width = dctx.shape
    block = 2 * LEN
    count = rows // block
    extra = 16
    if relative:
        out_specs = [ANY] * 2
        out_shape = [jax.ShapeDtypeStruct((2 * width + extra, width), BF)] * 2
    else:
        out_specs = [pl.BlockSpec((1, width, width), lambda i, *_: (jnp.maximum(i - count, 0), 0, 0))]
        out_shape = [jax.ShapeDtypeStruct((4, width, width), BF)]
    dproj, *grads, column_sums = call(
        functools.partial(attention_back_kernel, relative),
        in_specs=[
            pl.BlockSpec((block, 3 * width), lambda i, *_: (jnp.minimum(i, count - 1), 0)),
            HELD,
            HELD,
            whole(sums[0].shape),
            whole(sums[1].shape),
            whole(sums[2].shape),
            HELD,
            HELD,
            FAR,
            ],
        out_specs=[HELD] + out_specs + [whole((8, 3 * width))],
        out_shape=[jax.ShapeDtypeStruct((rows, 3 * width), BF)] + out_shape + [jax.ShapeDtypeStruct((8, 3 * width), F32)],
        grid=(count + 4,),
        scalars=2,
        scratch_shapes=[
            pltpu.VMEM((rows, width), BF),
            pltpu.VMEM((width, rows), BF),
            pltpu.VMEM((2, width, width), BF),
            pltpu.VMEM((extra, width), BF),
            pltpu.SemaphoreType.DMA((2,)),
            pltpu.SemaphoreType.DMA((2,)),
            pltpu.SemaphoreType.DMA,
        ],
        vmem=28,
        name="attention_back",
    )(place, lengths, proj, dctx, lse, *sums, dattended, context, tokens)
    return dproj, grads, column_sums


def input_grad_kernel(proj_ref, w_hbm_ref, dz_ref, out_ref, w_ref, sems):
    block, width = out_ref.shape
    here = rows_at(pl.program_id(0), block)

    def body(ready):
        grad = dz_ref[here, :].astype(F32)
        for unit in range(3):
            ready(unit)
            grad += dot_nt(proj_ref[here, unit * width : (unit + 1) * width], w_ref[unit])
        ready(3)
        out_ref[...] = grad.astype(BF)

    first_and_later(Bring(WHOLE, (0, 0, 0), [w_hbm_ref], w_ref, sems), body)


def input_grad(dproj, w_qkvo, dz, block=256):
    rows, width = dz.shape
    return call(
        input_grad_kernel,
        in_specs=[HELD, FAR, HELD],
        out_specs=[rows_of(block, width)],
        out_shape=[jax.ShapeDtypeStruct((rows, width), BF)],
        grid=(rows // block,),
        scalars=0,
        scratch_shapes=[pltpu.VMEM((4, width, width), BF), pltpu.SemaphoreType.DMA((4,))],
        vmem=28,
        name="input_grad",
    )(dproj, w_qkvo, dz)[0]


def finish_pair_kernel(place, up_ref, down_ref, one_ref, two_ref, far_ref, up_out_ref, down_out_ref, turned_ref):
    depth, width = up_ref.shape
    half = width // 2
    for position, (up, down) in enumerate(
        [(up_ref[...], down_ref[...])] + [(ref[:depth, :], ref[depth:, :]) for ref in (one_ref, two_ref, far_ref)]
    ):
        unit = place[0] ^ flip_of(position, place[2])
        up_out_ref[:, pl.ds(pl.multiple_of(unit * width, width), width)] = up.astype(F32)
        down = down.astype(F32)
        turned_ref[rows_at(unit, 2 * depth), :] = jnp.concatenate([down[:, :half], down[:, half:]], axis=0)
    down_out_ref[...] = turned_ref[...].T


def finish_pair(place, up, down, backs):
    depth, width = up.shape
    out_shape = [jax.ShapeDtypeStruct((depth, 4 * width), F32), jax.ShapeDtypeStruct((width // 2, width), F32)]
    return call(
        finish_pair_kernel,
        in_specs=[whole(up.shape), whole(down.shape)] + [whole(back.shape) for back in backs],
        out_specs=[whole(shape.shape) for shape in out_shape],
        out_shape=out_shape,
        grid=(1,),
        scalars=1,
        scratch_shapes=[pltpu.VMEM((width, width // 2), F32)],
        vmem=28,
        name="finish_pair",
    )(place, up, down, *backs)


def finish_attention_kernel(place, own_ref, one_ref, two_ref, far_ref, qkv_ref, out_ref):
    width = own_ref.shape[1]
    for position, ref in enumerate((own_ref, one_ref, two_ref, far_ref)):
        unit = place[0] ^ flip_of(position, place[2])
        values = ref[...].astype(F32)

        @pl.when(unit < 3)
        def _():
            qkv_ref[:, pl.ds(pl.multiple_of(unit * width, width), width)] = values

        @pl.when(unit == 3)
        def _():
            out_ref[...] = values


def finish_attention(place, own, backs):
    depth, width = own.shape
    out_shape = [jax.ShapeDtypeStruct((depth, 3 * width), F32), jax.ShapeDtypeStruct((depth, width), F32)]
    return call(
        finish_attention_kernel,
        in_specs=[whole(own.shape)] + [whole(back.shape) for back in backs],
        out_specs=[whole(shape.shape) for shape in out_shape],
        out_shape=out_shape,
        grid=(1,),
        scalars=1,
        scratch_shapes=[],
        vmem=28,
        name="finish_attention",
    )(place, own, *backs)


CORES = [(i, i ^ 1) for i in range(8)]


def from_core(value):
    return lax.ppermute(value, "shard", CORES)


def from_chip(value, ahead):
    return lax.ppermute(value, "shard", [((i + 2 * ahead) % 8, i) for i in range(8)])


def to_chip(value, ahead):
    return lax.ppermute(value, "shard", [(i, (i + 2 * ahead) % 8) for i in range(8)])


def from_flip(value, which):
    flip = lambda s: which if s % 2 == 0 else 3 - which
    pairs = [(r * 8 + s, (r ^ flip(s)) * 8 + s) for r in range(4) for s in range(8)]
    return lax.ppermute(value, ("rep", "shard"), pairs)


def from_far(value):
    return lax.ppermute(value, "rep", [(i, i ^ 3) for i in range(4)])


def joined(*parts):
    return jnp.concatenate(parts, 0)


def after(value, *earlier):
    return lax.optimization_barrier((value,) + earlier)[0]


class Gather:
    def __init__(self, mine, own, other, own_places, depth):
        self.hops = [from_chip(mine, ahead) for ahead in (1, 2, 3)]
        self.own, self.other, self.own_places, self.depth = own, other, own_places, depth

    def collect(self, *earlier):
        hops = [hop[: self.depth] for hop in self.hops]
        self.got = joined(after(hops[0], *earlier), *hops[1:])

    def first(self, *earlier):
        self.collect(*earlier)
        self.one = from_flip(self.got, 1)

    def second(self, *earlier):
        self.low = joined(self.got, after(self.one, *earlier))
        self.high = from_flip(self.low, 2)

    def direct(self, *earlier):
        self.collect(*earlier)
        self.others = [lax.ppermute(self.got, "rep", [(i, i ^ flip) for i in range(4)]) for flip in (1, 2, 3)]

    def hold(self, *earlier):
        self.others = [after(other, *earlier) for other in self.others]

    def weight_direct(self):
        return self.planned([self.got] + self.others, "direct")

    def weight(self):
        return self.planned([self.low, self.high], "skew")

    def planned(self, mine, kind):
        own = [pltpu.with_memory_space_constraint(piece, pltpu.HBM) for piece in self.own]
        pieces = own + self.other + mine + [from_core(piece) for piece in mine]
        count = len(own)
        entries = [
            (i + count * other, at, unit, None, 0, self.depth, other)
            for other in (0, 1)
            for i, places in enumerate(self.own_places)
            for at, unit in places
        ]
        each = 4 // len(mine)
        arriving = []
        for position in range(4):
            for other in (0, 1):
                source = SWAPPED[position] if kind == "skew" and other else position
                piece = 2 * count + len(mine) * other + source // each
                for ahead in (1, 2, 3):
                    at = pl.ds((3 * (source % each) + ahead - 1) * self.depth, self.depth)
                    arriving.append((piece, at, None, source, ahead, self.depth, other))
        if self.own_places[0][0][1] is None:
            arriving.sort(key=lambda entry: entry[4])
        return (kind, tuple(entries + arriving)), pieces


def wide(value):
    return value.astype(F32)


def share(total):
    return [from_flip(total, 1), from_flip(total, 2), from_far(total)]


class Reduce:
    def __init__(self, grads, extra=0):
        self.keep, self.send = grads
        self.extra = extra
        self.quarter = (self.keep.shape[0] - extra) // 4
        self.depth = self.quarter // 4

    def cores(self, *earlier):
        self.other = from_core(after(self.send, *earlier) if earlier else self.send)

    def first(self, *earlier):
        self.other = after(self.other, *earlier)
        n = 2 * self.quarter
        self.sent = (wide(self.keep[n:]) + wide(self.other[n:])).astype(BF)
        self.one = from_flip(self.sent, 1)

    def second(self, *earlier):
        self.one = after(self.one, *earlier)
        n, x = self.quarter, self.extra
        total = wide(self.keep[n : 2 * n]) + wide(self.other[n : 2 * n]) + wide(self.one[x + n :])
        if x:
            at = slice(2 * n, 2 * n + x)
            self.vector = wide(self.keep[at]) + wide(self.other[at]) + wide(self.one[:x])
            total = joined(total, self.vector)
        self.sent = total.astype(BF)
        self.two = from_flip(self.sent, 2)

    def chips(self, *earlier):
        self.two = after(self.two, *earlier)
        n, x, depth = self.quarter, self.extra, self.depth
        total = wide(self.keep[:n]) + wide(self.other[:n]) + wide(self.one[x : x + n]) + wide(self.two[:n])
        if x:
            self.vector = self.vector + wide(self.two[n:])
        self.total = total[:depth]
        self.hops = []
        self.sents = []
        for ahead in (1, 2, 3):
            part = total[ahead * depth : (ahead + 1) * depth]
            if x:
                part = joined(part, self.vector)
            self.sents.append(part.astype(BF))
            self.hops.append(to_chip(self.sents[-1], ahead))

    def collect(self, *earlier):
        self.hops[0] = after(self.hops[0], *earlier)
        for hop in self.hops:
            self.total = self.total + wide(hop[: self.depth])
            if self.extra:
                self.vector = self.vector + wide(hop[self.depth :])
        self.total = self.total.astype(BF)

    def share(self, *earlier):
        self.collect(*earlier)
        self.backs = share(self.total)


def row_weights(task, lengths, task_masks):
    token_task = jnp.repeat(task, LEN)
    chosen = jnp.where(token_task == 0, task_masks[0], jnp.where(token_task == 1, task_masks[1], task_masks[2]))
    valid = jnp.arange(LEN, dtype=jnp.int32)[None, :] < lengths[:, None]
    return (chosen * valid.astype(jnp.int32).reshape(-1)).astype(F32)[:, None]


def per_device(mesh_shape, *arrays):
    (tokens, cotangent, task, lengths, task_masks, w_qkv, qv_bias, w_out, out_bias, ln1_gain, ln1_bias, w_up, up_bias, w_down, down_bias, ln2_gain, ln2_bias) = arrays
    rows, width = tokens.shape
    shards = mesh_shape["shard"]
    hidden = up_bias.shape[0] * shards
    fast = shards == 8 and mesh_shape["rep"] == 4
    place = jnp.stack([lax.axis_index("rep"), lax.axis_index("shard") // 2, lax.axis_index("shard") % 2]).astype(jnp.int32)
    shard = lax.axis_index("shard")

    vectors = (qv_bias, out_bias, ln1_gain, ln1_bias, down_bias, ln2_gain, ln2_bias, up_bias)
    sizes = [v.shape[0] for v in vectors]

    if fast:
        depth = w_qkv.shape[0]
        rep = place[0]
        every = slice(None)

        def columns(first, count):
            return [((every, pl.ds(unit * width, width)), first + unit) for unit in range(count)]

        mine = lax.dynamic_slice(w_qkv, (0, jnp.minimum(rep, 2) * width), (depth, width))
        mine = jnp.where(rep == 3, w_out, mine)
        other_qkv, other_out, other_up, other_down = [from_core(after(own, mine)) for own in (w_qkv, w_out, w_up, w_down)]
        gather_a = Gather(mine, [w_qkv, w_out], [other_qkv, other_out], [columns(0, 3), columns(3, 1)], depth)
        gather_a.direct(other_qkv, other_out, other_up, other_down)
        packed = jnp.concatenate(after(vectors, gather_a.got))
        packed_rows = jnp.pad(packed, (0, 16 * width - packed.shape[0])).reshape(16, width)
        mine = joined(lax.dynamic_slice(w_up, (0, rep * width), (depth, width)), packed_rows)
        gather_b = Gather(mine, [w_up], [other_up], [columns(0, 4)], depth)
        vec_hops = [after(gather_b.hops[0], gather_a.got)] + gather_b.hops[1:]
        vec_rows = jnp.stack([packed_rows] + [hop[depth:] for hop in vec_hops])
        vec_rows = jnp.stack([vec_rows, from_core(vec_rows)], 1).reshape(8, -1)[:, : packed.shape[0]]
        index = jnp.arange(8)
        slot = 2 * ((index // 2 - place[1]) % 4) + ((index % 2) ^ place[2])
        pick = (slot[:, None] == index[None, :]).astype(BF)
        all_vectors = jnp.dot(pick, vec_rows, preferred_element_type=F32)
        row_weight = row_weights(*after((task, lengths, task_masks), gather_a.got))
    else:
        row_weight = row_weights(task, lengths, task_masks)
        packed = jnp.concatenate(vectors)
        all_vectors = lax.all_gather(packed, "shard", axis=0).astype(F32)
        full_a = jnp.concatenate([lax.all_gather(w_qkv, "shard", axis=0, tiled=True), lax.all_gather(w_out, "shard", axis=0, tiled=True)], 1)
        full_b = lax.all_gather(w_up, "shard", axis=0, tiled=True)
        weight_a = (WHOLE, [full_a.reshape(width, 4, width).transpose(1, 0, 2)])
        weight_b = (WHOLE, [full_b.reshape(width, 4, width).transpose(1, 0, 2)])
        full_c = lax.all_gather(w_down, "shard", axis=0, tiled=True)
        weight_c = (WHOLE, [full_c.reshape(4, -1, width)])

    full, start = [], 0
    for size in sizes:
        full.append(all_vectors[:, start : start + size].reshape(-1))
        start += size
    qv, out_shift, gain_one, shift_one, down_shift, gain_two, shift_two, up_shift = full
    qkv_shift = jnp.concatenate([qv[:width], jnp.zeros((width,), F32), qv[width:]])[None]
    vecs = jnp.stack([out_shift, gain_one, shift_one, down_shift, gain_two, shift_two, shift_two, shift_two])
    up_shift = up_shift[None]

    if fast:
        gather_a.hold(qkv_shift, vecs, up_shift, row_weight)
        weight_a = gather_a.weight_direct()
        gather_b.first()
        gather_b.second(*gather_a.others)
        mine = lax.dynamic_slice(w_down, (rep * depth, 0), (depth, width))
        own = [[(pl.ds(0, 4 * depth), None)]]
        mine = after(mine, gather_b.low)
        gather_c = Gather(mine, [w_down], [other_down], own, depth)
        qkv_shift = after(qkv_shift, gather_b.low, mine)
    proj, context, lse, w_a = attention_forward(place, lengths, tokens, qkv_shift, weight_a)
    if fast:
        gather_c.direct(context)
        gather_b.high = after(gather_b.high, gather_c.got)
        weight_b = gather_b.weight()
        context = after(context, gather_c.got)
    norm_one, scale_one, first_low, act, slope, w_b = middle(place, tokens, context, w_a, vecs, up_shift, weight_b)
    if fast:
        gather_c.hold(act)
        weight_c = gather_c.weight_direct()
    output, dffn, sums_two, down_full, grads_c = ffn(place, act, weight_c, norm_one, cotangent, row_weight, vecs, shards, fast)
    if fast:
        group_c = Reduce(grads_c)
        group_c.cores()
    dinner, sums_up, grads_b = inner_grads(place, dffn, first_low, down_full, slope, fast)
    if fast:
        group_c.first(dinner)
        group_b = Reduce(grads_b)
        group_b.cores(group_c.sent)
        dinner = after(dinner, group_c.sent)
    dattended, dcontext, sums_one = first_grad(dinner, w_b, dffn, norm_one, scale_one, vecs, w_a)
    if fast:
        group_b.first(dcontext)
        group_c.second(dcontext)
        lse = after(lse, group_b.sent, group_c.sent)
    sums = (sums_one, sums_two, sums_up)
    dproj, grads_a, sums_qkv = attention_back(place, lengths, proj, dcontext, lse, tokens, context, dattended, sums, fast)
    if fast:
        group_a = Reduce(grads_a, 16)
        group_c.two, group_b.one = after(group_c.two, *grads_a), after(group_b.one, *grads_a)
        group_a.cores(group_c.two, group_b.one)
        group_c.chips()
        group_a.first(*group_c.sents)
        group_b.second(group_a.sent)
        dproj = after(dproj, group_b.sent)
    grad_input = input_grad(dproj, w_a, dattended)

    starts = [0]
    for size in sizes:
        starts.append(starts[-1] + size * shards)
    if fast:
        group_c.collect(grad_input)
        group_b.chips(group_c.total)
        group_a.second(*group_b.sents)
        group_a.chips()
        group_b.collect(*group_a.sents)
        half = group_c.total.shape[0] // 2
        down = jnp.concatenate([group_c.total[:half], group_c.total[half:]], 1)
        backs = share(joined(group_b.total, down))
        group_a.share()
        wide_b, final_c = finish_pair(place, group_b.total, down, [after(back, group_a.hops[0]) for back in backs])
        wide_a, final_out = finish_attention(place, group_a.total, group_a.backs)
        sums = group_a.vector.reshape(-1)
    else:
        units = []
        for (grads,) in (grads_b, grads_a):
            summed = lax.psum_scatter(grads, "shard", scatter_dimension=1, tiled=True)
            units.append([wide(unit) for unit in lax.psum(summed.astype(BF), "rep")])
        units_b, units_a = units
        summed = lax.psum(lax.psum_scatter(grads_c[0], "shard", scatter_dimension=0, tiled=True), "rep")[0]
        units_c = [wide(unit) for unit in jnp.split(summed, 4)]
        wide_a, wide_b = jnp.concatenate(units_a[:3], 1), jnp.concatenate(units_b, 1)
        final_out, final_c = units_a[3], jnp.concatenate(units_c, 0).T
        sums = jnp.concatenate([sums_qkv[0, :width], sums_qkv[0, 2 * width :], sums_one[2], sums_one[0], sums_one[1], sums_two[2], sums_two[0], sums_two[1], sums_up[0]])
        sums = lax.psum(sums, ("rep", "shard"))
    final = [lax.dynamic_slice(sums, (start + shard * size,), (size,)) for start, size in zip(starts, sizes)]
    f_qv, f_out_shift, f_gain_one, f_shift_one, f_down_shift, f_gain_two, f_shift_two, f_up_shift = final
    return (output, grad_input, wide_a, f_qv, final_out, f_out_shift, f_gain_one, f_shift_one, wide_b, f_up_shift, final_c, f_down_shift, f_gain_two, f_shift_two)


def solution(mesh):
    split, shard = P(("rep", "shard"), None), P("shard")
    flat, matrix = P(("rep", "shard")), P("shard", None)
    in_specs = (split, split, flat, flat, P(None, ("rep", "shard")), matrix, shard, matrix, shard, shard, shard, matrix, shard, matrix, shard, shard, shard)
    out_specs = (split, split, matrix, shard, matrix, shard, shard, shard, matrix, shard, matrix, shard, shard, shard)
    return jax.shard_map(
        functools.partial(per_device, dict(mesh.shape)), mesh=mesh, in_specs=in_specs, out_specs=out_specs, check_vma=False
    )
```

```python
import functools
import math

import jax
import jax.numpy as jnp
from jax import lax
from jax.experimental import pallas as pl
from jax.experimental.pallas import tpu as pltpu
from jax.sharding import PartitionSpec as P

HD = 64
LEN = 128
EPSILON = 1e-06
BF = jnp.bfloat16
F32 = jnp.float32
MIB = 1024 * 1024

ROOT_HALF = 0.7071067811865476
DENSITY = 0.3989422804014327


def dot_nn(left, right):
    return jnp.dot(left, right, preferred_element_type=F32)


def dot_nt(left, right):
    return lax.dot_general(left, right, (((1,), (1,)), ((), ())), preferred_element_type=F32)


def dot_tn(left, right):
    return lax.dot_general(left, right, (((0,), (0,)), ((), ())), preferred_element_type=F32)


def gelu_parts(inner):
    phi = 0.5 + 0.5 * lax.erf(inner * ROOT_HALF)
    bell = jnp.exp(inner * inner * -0.5) * DENSITY
    return inner * phi, phi + inner * bell


def norm_parts(summed):
    centre = jnp.mean(summed, -1, keepdims=True)
    deviation = summed - centre
    variance = jnp.mean(deviation * deviation, -1, keepdims=True)
    rscale = lax.rsqrt(variance + EPSILON)
    return deviation * rscale, rscale


def norm_back(grad_norm, normed, rscale):
    first_mean = jnp.mean(grad_norm, -1, keepdims=True)
    second_mean = jnp.mean(grad_norm * normed, -1, keepdims=True)
    return rscale * (grad_norm - first_mean - normed * second_mean)


def add_rows(total_ref, rows):
    @pl.when(pl.program_id(0) == 0)
    def _():
        total_ref[...] = jnp.zeros_like(total_ref)

    for at, values in enumerate(rows):
        total_ref[at : at + 1, :] += jnp.sum(values, 0, keepdims=True)


def cost(flops, moved):
    return pl.CostEstimate(flops=1000, bytes_accessed=1000, transcendentals=0)


def params(vmem=28):
    return pltpu.CompilerParams(vmem_limit_bytes=vmem * MIB)


def halves_of(step, block):
    half = block // 2
    return [(slice(at, at + half), pl.ds(pl.multiple_of(step * block + at, half), half)) for at in (0, half)]


def rows_at(step, block):
    return pl.ds(pl.multiple_of(step * block, block), block)


def whole(shape):
    return pl.BlockSpec(shape, lambda i, *_: (0,) * len(shape))


def rows_of(block, width):
    return pl.BlockSpec((block, width), lambda i, *_: (i, 0))


def head_masks():
    lane = lax.broadcasted_iota(jnp.int32, (1, 2 * HD), 1)
    return (lane < HD).astype(BF), (lane >= HD).astype(BF)


def stack_heads(pair, masks):
    return jnp.concatenate([pair * masks[0], pair * masks[1]], axis=0)


def attention_forward_kernel(plan, count_of_pieces, place, lengths, x_ref, shift_ref, *refs):
    pieces, (proj_ref, ctx_ref, lse_ref, w_out_ref, w_ref, sems) = refs[: count_of_pieces], refs[count_of_pieces :]
    block, width = x_ref.shape
    step = pl.program_id(0)

    def body(ready):
        x = x_ref[...]
        for i in range(4):
            unit = ready(i)

            @pl.when(unit < 3)
            def _():
                at = pl.ds(pl.multiple_of(unit * width, width), width)
                proj_ref[:, at] = (dot_nn(x, w_ref[unit]) + shift_ref[:, at]).astype(BF)

        masks = head_masks()
        lane = lax.broadcasted_iota(jnp.int32, (1, LEN), 1)
        for seq in range(block // LEN):
            number = step * (block // LEN) + seq
            rows = rows_at(number, LEN)
            here = slice(seq * LEN, (seq + 1) * LEN)
            valid = lane < lengths[number]
            lse = jnp.zeros((LEN, LEN), F32)
            pairs = range(width // (2 * HD))

            def part(offset, pair):
                return proj_ref[here, offset + pair * 2 * HD : offset + (pair + 1) * 2 * HD]

            stage = [dot_nt(part(0, pair) * BF(0.125), stack_heads(part(width, pair), masks)) for pair in pairs]
            later = []
            for pair, scores in zip(pairs, stage):
                probs = []
                for half in range(2):
                    masked = jnp.where(valid, scores[:, half * LEN : (half + 1) * LEN], -1e9)
                    top = jnp.max(masked, -1, keepdims=True)
                    exponent = jnp.exp(masked - top)
                    total = jnp.sum(exponent, -1, keepdims=True)
                    probs.append((exponent * (1.0 / total)).astype(BF))
                    lse = jnp.where(lane == 2 * pair + half, top + jnp.log(total), lse)
                later.append(jnp.concatenate(probs, axis=1))
            for pair, probs in zip(pairs, later):
                ctx = dot_nn(probs, stack_heads(part(2 * width, pair), masks))
                ctx_ref[rows, pair * 2 * HD : (pair + 1) * 2 * HD] = ctx.astype(BF)
            lse_ref[number] = lse.T[: lse_ref.shape[1]]

    first_and_later(Bring(plan, place, pieces, w_ref, sems, w_out_ref=w_out_ref), body)


SWAPPED = (0, 2, 1, 3)


def flip_of(position, core):
    return {0: 0, 1: 1 + core, 2: 2 - core, 3: 3}[position]


class Bring:
    def __init__(self, plan, place, pieces, w_ref, sems, rows_first=False, w_out_ref=None):
        self.kind, self.entries = plan
        self.place, self.pieces = place, pieces
        self.w_ref, self.w_out_ref, self.sems, self.rows_first = w_ref, w_out_ref, sems, rows_first
        self.span = w_ref.shape[0] // 4

    def part(self, ref, at):
        return ref.at[rows_at(at, self.span)] if self.rows_first else ref.at[at]

    def unit(self, position, other):
        rep, core = self.place[0], self.place[2]
        return rep ^ (position if self.kind == "direct" else flip_of(position, core ^ other))

    def round(self, i):
        if self.kind == "whole":
            return i
        return (self.place[1] + i) % 4 if self.rows_first else self.unit(i, 0)

    def start(self):
        if self.kind == "whole":
            for at in range(4):
                pltpu.make_async_copy(self.pieces[0].at[at], self.part(self.w_ref, at), self.sems.at[at]).start()
            return
        chip, core = self.place[1], self.place[2]
        for piece, at, unit, position, ahead, depth, other in self.entries:
            to_unit = unit if position is None else self.unit(position, other)
            to_chip = (chip + ahead) % 4
            shard = 2 * to_chip + (core ^ other)
            if self.rows_first:
                first = 4 * shard if to_unit is None else 4 * shard + to_unit
                count = 4 * depth if to_unit is None else depth
                group, to = to_chip, self.w_ref.at[pl.ds(pl.multiple_of(first * depth, 16), count)]
            else:
                group, to = to_unit, self.w_ref.at[to_unit, pl.ds(pl.multiple_of(shard * depth, 16), depth)]
            pltpu.make_async_copy(self.pieces[piece].at[at], to, self.sems.at[group]).start()

    def wait(self, at):
        here = self.part(self.w_ref, at)
        pltpu.make_async_copy(here, here, self.sems.at[at]).wait()
        if self.w_out_ref is not None:
            self.onward(at).start()

    def onward(self, at):
        return pltpu.make_async_copy(self.part(self.w_ref, at), self.part(self.w_out_ref, at), self.sems.at[4 + at])

    def finish(self):
        for at in range(4):
            self.onward(at).wait()


def first_and_later(bring, body):
    @pl.when(pl.program_id(0) == 0)
    def _():
        bring.start()

        def ready(i):
            at = bring.round(i)
            bring.wait(at)
            return at

        body(ready)

    @pl.when(pl.program_id(0) > 0)
    def _():
        body(bring.round)

    if bring.w_out_ref is not None:

        @pl.when(pl.program_id(0) == pl.num_programs(0) - 1)
        def _():
            bring.finish()


ANY = pl.BlockSpec(memory_space=pl.ANY)
HELD = pl.BlockSpec(memory_space=pltpu.VMEM)
FAR = pl.BlockSpec(memory_space=pl.ANY)


def call(kernel, in_specs, out_specs, out_shape, grid, scalars, scratch_shapes, vmem, name):
    def space(spec, shape, result):
        large = math.prod(shape.shape) * shape.dtype.itemsize > MIB // 2
        if spec is HELD:
            return pltpu.VMEM
        return pltpu.HBM if spec is FAR or large and (result or spec is not ANY) else None

    def placed(spec, shape):
        where = space(spec, shape, True)
        return shape if where is None else where(shape.shape, shape.dtype)

    run = pl.pallas_call(
        kernel,
        grid_spec=pltpu.PrefetchScalarGridSpec(
            num_scalar_prefetch=scalars, grid=grid, in_specs=in_specs, out_specs=out_specs, scratch_shapes=scratch_shapes
        ),
        out_shape=[placed(spec, shape) for spec, shape in zip(out_specs, out_shape)],
        compiler_params=params(vmem),
        cost_estimate=cost(0, 0),
        name=name,
    )

    def constrained(spec, arg):
        where = space(spec, arg, False)
        return arg if where is None else pltpu.with_memory_space_constraint(arg, where)

    def apply(*args):
        return run(*args[:scalars], *[constrained(spec, arg) for spec, arg in zip(in_specs, args[scalars:])])

    return apply


WHOLE = ("whole", ())


def attention_forward(place, lengths, tokens, shift, weight):
    rows, width = tokens.shape
    block = 2 * LEN
    heads = width // HD
    lse_rows = -(-heads // 8) * 8
    plan, pieces = weight
    return call(
        functools.partial(attention_forward_kernel, plan, len(pieces)),
        in_specs=[rows_of(block, width), whole((1, 3 * width))] + [FAR] * len(pieces),
        out_specs=[rows_of(block, 3 * width), HELD, HELD, ANY],
        out_shape=[
            jax.ShapeDtypeStruct((rows, 3 * width), BF),
            jax.ShapeDtypeStruct((rows, width), BF),
            jax.ShapeDtypeStruct((rows // LEN, lse_rows, LEN), F32),
            jax.ShapeDtypeStruct((4, width, width), BF),
        ],
        grid=(rows // block,),
        scalars=2,
        scratch_shapes=[pltpu.VMEM((4, width, width), BF), pltpu.SemaphoreType.DMA((8,))],
        vmem=28,
        name="attention_forward",
    )(place, lengths, tokens, shift, *pieces)


def middle_kernel(plan, count_of_pieces, place, x_ref, ctx_ref, w_attn_ref, vec_ref, up_shift_ref, *refs):
    pieces = refs[: count_of_pieces]
    norm_ref, scale_ref, low_ref, act_ref, slope_ref, w_out_ref, w_ref, sems = refs[count_of_pieces :]
    block, width = x_ref.shape

    def body(ready):
        halves = halves_of(pl.program_id(0), block)
        attended = [dot_nn(ctx_ref[here, :], w_attn_ref[0]) + vec_ref[0:1, :] for _, here in halves]
        lows = []
        for (local, here), value in zip(halves, attended):
            normed, rscale = norm_parts(x_ref[local, :].astype(F32) + value)
            norm_ref[here, :] = normed.astype(BF)
            scale_ref[here, :] = rscale
            lows.append((normed * vec_ref[1:2, :] + vec_ref[2:3, :]).astype(BF))
            low_ref[here, :] = lows[-1]
        for i in range(w_ref.shape[0]):
            unit = ready(i)
            at = pl.ds(pl.multiple_of(unit * width, width), width)
            for (_, here), low in zip(halves, lows):
                act, slope = gelu_parts(dot_nn(low, w_ref[unit]) + up_shift_ref[:, at])
                act_ref[here, at] = act.astype(BF)
                slope_ref[here, at] = slope.astype(BF)

    first_and_later(Bring(plan, place, pieces, w_ref, sems, w_out_ref=w_out_ref), body)


def middle(place, tokens, context, w_qkvo, vecs, up_shift, weight, block=512):
    rows, width = tokens.shape
    hidden = up_shift.shape[1]
    units = hidden // width
    plan, pieces = weight
    return call(
        functools.partial(middle_kernel, plan, len(pieces)),
        in_specs=[
                rows_of(block, width),
                HELD,
                pl.BlockSpec((1, width, width), lambda i, *_: (3, 0, 0)),
                whole(vecs.shape),
                whole(up_shift.shape),
            ]
            + [FAR] * len(pieces),
        out_specs=[HELD] * 5 + [ANY],
        out_shape=[
            jax.ShapeDtypeStruct((rows, width), BF),
            jax.ShapeDtypeStruct((rows, 1), F32),
            jax.ShapeDtypeStruct((rows, width), BF),
            jax.ShapeDtypeStruct((rows, hidden), BF),
            jax.ShapeDtypeStruct((rows, hidden), BF),
            jax.ShapeDtypeStruct((units, width, width), BF),
        ],
        grid=(rows // block,),
        scalars=1,
        scratch_shapes=[pltpu.VMEM((units, width, width), BF), pltpu.SemaphoreType.DMA((8,))],
        vmem=28,
        name="middle",
    )(place, tokens, context, w_qkvo, vecs, up_shift, *pieces)


def ffn_kernel(plan, count_of_pieces, relative, place, act_ref, norm_ref, cot_ref, weight_ref, vec_ref, *refs):
    pieces, refs = refs[: count_of_pieces], refs[count_of_pieces :]
    out_ref, low_ref, sum_ref, w_out_ref, *refs = refs
    outs, refs = refs[: 2 if relative else 1], refs[2 if relative else 1 :]
    turned_ref, w_ref, stage_ref, sems, w_sems = refs
    step = pl.program_id(0)
    block, width = cot_ref.shape
    count = act_ref.shape[0] // block
    halves = halves_of(jnp.minimum(step, count - 1), block)
    bring = Bring(plan, place, pieces, w_ref, w_sems, rows_first=True, w_out_ref=w_out_ref)

    def finish(local, here, ffn):
        first = norm_ref[here, :].astype(F32) * vec_ref[1:2, :] + vec_ref[2:3, :]
        normed, rscale = norm_parts(first + (ffn + vec_ref[3:4, :]))
        out_ref[local, :] = (normed * vec_ref[4:5, :] + vec_ref[5:6, :]).astype(BF)
        grad = cot_ref[local, :].astype(F32) * weight_ref[local, :]
        low = norm_back(grad * vec_ref[4:5, :], normed, rscale).astype(BF)
        low_ref[here, :] = low
        turned_ref[:, here] = low.T
        for at, values in enumerate((grad * normed, grad, low.astype(F32))):
            sum_ref[at : at + 1, :] += jnp.sum(values, 0, keepdims=True)

    @pl.when(step == 0)
    def _():
        bring.start()
        sum_ref[...] = jnp.zeros_like(sum_ref)
        ffns = [0.0, 0.0]
        for i in range(4):
            part = bring.round(i)
            bring.wait(part)
            at = rows_at(part, bring.span)
            ffns = [ffn + dot_nn(act_ref[here, at], w_ref[at, :]) for ffn, (_, here) in zip(ffns, halves)]
        for (local, here), ffn in zip(halves, ffns):
            finish(local, here, ffn)

    @pl.when((step > 0) & (step < count))
    def _():
        ffns = [dot_nn(act_ref[here, :], w_ref[...]) for _, here in halves]
        for (local, here), ffn in zip(halves, ffns):
            finish(local, here, ffn)

    def left(slot):
        here = stage_ref.at[slot]
        pltpu.make_async_copy(here, here, sems.at[slot]).wait()

    if relative:

        @pl.when(step >= count + 2)
        def _():
            left(step % 2)

    @pl.when(step >= count)
    def _():
        at = step - count
        columns = pl.ds(pl.multiple_of(at * width, width), width)
        grad = dot_nn(turned_ref[...], act_ref[:, columns]).astype(BF)
        if not relative:
            each, _, part = outs[0].shape
            for i in range(each):
                outs[0][i] = grad[:, i * part : (i + 1) * part]
            return
        rep, chip, core = place[0], place[1], place[2]
        part, depth = width // 2, width // 4
        slot = step % 2
        for half in range(2):
            stage_ref[slot, half] = grad[:, half * part : (half + 1) * part]
        ahead = (at - chip) % 4
        for unit in range(4):
            rows = pl.ds(unit * depth, depth)
            for ref, whose in zip(outs, (core, 1 - core)):
                to = pl.multiple_of((4 * slot_of(unit, rep, whose) + ahead) * depth, 16)
                pltpu.make_async_copy(stage_ref.at[slot, whose, rows], ref.at[pl.ds(to, depth)], sems.at[slot]).start()

    @pl.when(step == pl.num_programs(0) - 1)
    def _():
        bring.finish()
        if relative:
            left(0)
            left(1)


def once(shape):
    return pl.BlockSpec(shape, lambda i, *_: (0,) * len(shape), pipeline_mode=pl.Buffered(1))


def ffn(place, act, weight, norm_one, cotangent, row_weight, vecs, shards, relative, block=512):
    rows, width = cotangent.shape
    hidden = act.shape[1]
    part = hidden // shards
    each = width // part
    count = rows // block
    plan, pieces = weight
    if relative:
        out_specs = [ANY] * 2
        out_shape = [jax.ShapeDtypeStruct((4 * width, part), BF)] * 2
    else:
        out_specs = [pl.BlockSpec((each, width, part), lambda i, *_: (jnp.maximum(i - count, 0), 0, 0))]
        out_shape = [jax.ShapeDtypeStruct((shards, width, part), BF)]
    early = lambda columns: pl.BlockSpec((block, columns), lambda i, *_: (jnp.minimum(i, count - 1), 0))
    output, low, sums, w_down, *grads = call(
        functools.partial(ffn_kernel, plan, len(pieces), relative),
        in_specs=[HELD, HELD, early(width), early(1), whole(vecs.shape)] + [FAR] * len(pieces),
        out_specs=[early(width), HELD, whole((8, width)), ANY] + out_specs,
        out_shape=[
            jax.ShapeDtypeStruct((rows, width), BF),
            jax.ShapeDtypeStruct((rows, width), BF),
            jax.ShapeDtypeStruct((8, width), F32),
            jax.ShapeDtypeStruct((hidden, width), BF),
        ]
        + out_shape,
        grid=(count + shards // each,),
        scalars=1,
        scratch_shapes=[
            pltpu.VMEM((width, rows), BF),
            pltpu.VMEM((hidden, width), BF),
            pltpu.VMEM((2, 2, width, width // 2), BF),
            pltpu.SemaphoreType.DMA((2,)),
            pltpu.SemaphoreType.DMA((8,)),
        ],
        vmem=28,
        name="ffn",
    )(place, act, norm_one, cotangent, row_weight, vecs, *pieces)
    return output, low, sums, w_down, grads


class Outward:
    def __init__(self, stage_ref, sems):
        self.step = pl.program_id(0)
        self.slot = self.step % 2
        self.stage_ref, self.sems = stage_ref, sems

    def free(self):
        @pl.when(self.step >= 2)
        def _():
            self.wait(self.slot)

    def stage(self):
        return self.stage_ref.at[self.slot]

    def send(self, *pairs):
        for source, to in pairs:
            pltpu.make_async_copy(source, to, self.sems.at[self.slot]).start()

    def wait(self, slot):
        here = self.stage_ref.at[slot]
        pltpu.make_async_copy(here, here, self.sems.at[slot]).wait()

    def finish(self):
        @pl.when(self.step == pl.num_programs(0) - 1)
        def _():
            self.wait(1 - self.slot)
            self.wait(self.slot)


def slot_of(unit, rep, core):
    e = unit ^ rep
    return jnp.where(core == 0, 2 * (e % 2) + e // 2, e)


def send_units(place, grad, out, outs, extra, unit=None):
    rep, chip, core = place[0], place[1], place[2]
    depth = grad.shape[0] // 8
    unit = pl.program_id(0) if unit is None else unit
    stage = out.stage()
    stage[...] = grad
    for ref, whose in zip(outs, (core, 1 - core)):
        slot = slot_of(unit, rep, whose)
        for other in range(4):
            ahead = (other - chip) % 4
            to = pl.multiple_of((4 * slot + ahead) * depth + jnp.where(slot >= 2, extra, 0), 16)
            row = pl.multiple_of((2 * other + whose) * depth, 16)
            out.send((stage.at[pl.ds(row, depth)], ref.at[pl.ds(to, depth)]))


def inner_grads_kernel(relative, place, low_ref, w_ref, slope_ref, first_ref, inner_ref, sum_ref, *refs):
    outs, refs = refs[: 2 if relative else 1], refs[2 if relative else 1 :]
    turned_ref, stage_ref, sems = refs
    step = pl.program_id(0)
    rows, width = low_ref.shape
    columns = pl.ds(pl.multiple_of(step * width, width), width)

    @pl.when(step == 0)
    def _():
        turned_ref[...] = first_ref[...].T

    total = 0.0
    for at in range(0, rows, 256):
        here = slice(at, at + 256)
        grad = (dot_nt(low_ref[here, :], w_ref[...]) * slope_ref[here, columns].astype(F32)).astype(BF)
        inner_ref[here, columns] = grad
        total = total + jnp.sum(grad.astype(F32), 0, keepdims=True)
    sum_ref[0:1, :] = total

    grad = dot_nn(turned_ref[...], inner_ref[:, columns]).astype(BF)
    if relative:
        out = Outward(stage_ref, sems)
        out.free()
        send_units(place, grad, out, outs, 0)
        out.finish()
    else:
        outs[0][0] = grad


def inner_grads(place, low, first, w_down, slope, relative):
    rows, width = low.shape
    hidden = slope.shape[1]
    columns = lambda height: pl.BlockSpec((height, width), lambda i, place: (0, i))
    if relative:
        out_specs = [ANY] * 2
        out_shape = [jax.ShapeDtypeStruct((2 * width, width), BF)] * 2
    else:
        out_specs = [pl.BlockSpec((1, width, width), lambda i, place: (i, 0, 0))]
        out_shape = [jax.ShapeDtypeStruct((4, width, width), BF)]
    inner, sums, *grads = call(
        functools.partial(inner_grads_kernel, relative),
        in_specs=[HELD, pl.BlockSpec((width, width), lambda i, place: (i, 0)), HELD, HELD],
        out_specs=[HELD, columns(8)] + out_specs,
        out_shape=[jax.ShapeDtypeStruct((rows, hidden), BF), jax.ShapeDtypeStruct((8, hidden), F32)] + out_shape,
        grid=(hidden // width,),
        scalars=1,
        scratch_shapes=[
            pltpu.VMEM((width, rows), BF),
            pltpu.VMEM((2, width, width), BF),
            pltpu.SemaphoreType.DMA((2,)),
        ],
        vmem=28,
        name="inner_grads",
    )(place, low, w_down, slope, first)
    return inner, sums, grads


def first_grad_kernel(inner_ref, w_hbm_ref, low_in_ref, norm_ref, scale_ref, vec_ref, w_attn_ref, low_ref, ctx_ref, sum_ref, w_ref, sems):
    width = norm_ref.shape[1]
    halves = halves_of(pl.program_id(0), 512)

    @pl.when(pl.program_id(0) == 0)
    def _():
        sum_ref[...] = jnp.zeros_like(sum_ref)

    def body(ready):
        grads = [low_in_ref[here, :].astype(F32) for _, here in halves]
        for unit in range(4):
            ready(unit)
            at = slice(unit * width, (unit + 1) * width)
            grads = [grad + dot_nt(inner_ref[here, at], w_ref[unit]) for grad, (_, here) in zip(grads, halves)]
        for grad, (_, here) in zip(grads, halves):
            normed = norm_ref[here, :].astype(F32)
            low = norm_back(grad * vec_ref[1:2, :], normed, scale_ref[here, :]).astype(BF)
            low_ref[here, :] = low
            ctx_ref[here, :] = dot_nt(low, w_attn_ref[0]).astype(BF)
            for at, values in enumerate((grad * normed, grad, low.astype(F32))):
                sum_ref[at : at + 1, :] += jnp.sum(values, 0, keepdims=True)

    first_and_later(Bring(WHOLE, (0, 0, 0), [w_hbm_ref], w_ref, sems), body)


def first_grad(inner, w_up, low, norm_one, scale_one, vecs, w_qkvo, block=512):
    rows, width = low.shape
    hidden = inner.shape[1]
    return call(
        first_grad_kernel,
        in_specs=[
            HELD,
            FAR,
            HELD,
            HELD,
            HELD,
            whole(vecs.shape),
            pl.BlockSpec((1, width, width), lambda i: (3, 0, 0)),
        ],
        out_specs=[HELD, HELD, whole((8, width))],
        out_shape=[
            jax.ShapeDtypeStruct((rows, width), BF),
            jax.ShapeDtypeStruct((rows, width), BF),
            jax.ShapeDtypeStruct((8, width), F32),
        ],
        grid=(rows // block,),
        scalars=0,
        scratch_shapes=[pltpu.VMEM(w_up.shape, BF), pltpu.SemaphoreType.DMA((4,))],
        vmem=28,
        name="first_grad",
    )(inner, w_up, low, norm_one, scale_one, vecs, w_qkvo)


def attention_back_kernel(relative, place, lengths, proj_ref, dctx_ref, lse_ref, one_ref, two_ref, up_ref, attn_ref, ctx_ref, x_hbm_ref, held_ref, *refs):
    outs, refs = refs[: 2 if relative else 1], refs[2 if relative else 1 :]
    sum_ref, x_ref, turned_ref, stage_ref, sums_ref, sems, sum_sems, late_sem = refs
    step = pl.program_id(0)
    width = dctx_ref.shape[1]
    block = 2 * LEN
    count = held_ref.shape[0] // block
    extra = sums_ref.shape[0]
    late = pltpu.make_async_copy(x_hbm_ref, x_ref, late_sem)

    @pl.when(step == 0)
    def _():
        sum_ref[...] = jnp.zeros_like(sum_ref)
        late.start()

    @pl.when(step == 1)
    def _():
        late.wait()
        turned_ref[...] = x_ref[...].T

    @pl.when(step < count)
    def _():
        masks = head_masks()
        lane = lax.broadcasted_iota(jnp.int32, (1, 2 * HD), 1)
        key = lax.broadcasted_iota(jnp.int32, (LEN, 1), 0)
        for seq in range(block // LEN):
            number = step * (block // LEN) + seq
            rows = rows_at(number, LEN)
            here_rows = slice(seq * LEN, (seq + 1) * LEN)
            valid = key < lengths[number]
            pairs = range(width // (2 * HD))

            def part(ref, where, offset, pair):
                return ref[where, offset + pair * 2 * HD : offset + (pair + 1) * 2 * HD]

            stage = []
            for pair in pairs:
                q = part(proj_ref, here_rows, 0, pair) * BF(0.125)
                dctx = part(dctx_ref, rows, 0, pair)
                queries, grads = stack_heads(q, masks), stack_heads(dctx, masks)
                scores = dot_nt(part(proj_ref, here_rows, width, pair), queries)
                dprobs = dot_nt(part(proj_ref, here_rows, 2 * width, pair), grads)
                stage.append((queries, grads, scores, dprobs))
            later = []
            for pair, (queries, grads, scores, dprobs) in zip(pairs, stage):
                probs, dscores = [], []
                for half in range(2):
                    here = slice(half * LEN, (half + 1) * LEN)
                    lse = lse_ref[number, 2 * pair + half : 2 * pair + half + 1, :]
                    prob = jnp.exp(jnp.where(valid, scores[:, here], -1e9) - lse)
                    dprob = dprobs[:, here]
                    inner = jnp.sum(prob * dprob, 0, keepdims=True)
                    dscores.append((prob * (dprob - inner)).astype(BF))
                    probs.append(prob.astype(BF))
                turned = jnp.concatenate([dscore.T for dscore in dscores], axis=1)
                later.append((queries, grads, jnp.concatenate(probs, axis=1), jnp.concatenate(dscores, axis=1), turned))
            for pair, (queries, grads, probs, dscores, turned) in zip(pairs, later):
                dv = dot_nn(probs, grads).astype(BF)
                dk = dot_nn(dscores, queries).astype(BF)
                dq = (dot_nn(turned, stack_heads(part(proj_ref, here_rows, width, pair), masks)) * 0.125).astype(BF)
                at = pair * 2 * HD
                for offset, grad in ((0, dq), (width, dk), (2 * width, dv)):
                    held_ref[rows, offset + at : offset + at + 2 * HD] = grad
                    if offset != width:
                        sum_ref[0:1, offset + at : offset + at + 2 * HD] += jnp.sum(grad.astype(F32), 0, keepdims=True)

    if relative:
        out = Outward(stage_ref, sems)
        copies = [
            pltpu.make_async_copy(sums_ref, ref.at[pl.ds(width, extra)], sum_sems.at[i])
            for i, ref in enumerate(outs)
        ]

        @pl.when(step == count)
        def _():
            rows = [sum_ref[0:1, :width], sum_ref[0:1, 2 * width :], one_ref[2:3, :], one_ref[0:1, :], one_ref[1:2, :]]
            rows += [two_ref[2:3, :], two_ref[0:1, :], two_ref[1:2, :]]
            rows += [up_ref[0:1, at : at + width] for at in range(0, up_ref.shape[1], width)]
            rows += [jnp.zeros((1, width), F32)] * (extra - len(rows))
            sums_ref[...] = jnp.concatenate(rows, axis=0).astype(BF)
            for copy in copies:
                copy.start()

    def put(unit, grad):
        if not relative:
            outs[0][0] = grad
            return

        @pl.when(step >= count + 2)
        def _():
            out.wait(out.slot)

        send_units(place, grad, out, outs, extra, unit)

    for unit in range(3):

        @pl.when(step == count + unit)
        def _():
            put(unit, dot_nn(turned_ref[...], held_ref[:, unit * width : (unit + 1) * width]).astype(BF))

    @pl.when(step == count + 3)
    def _():
        turned_ref[...] = ctx_ref[...].T
        put(3, dot_nn(turned_ref[...], attn_ref[...]).astype(BF))
        if relative:
            for copy in copies:
                copy.wait()

    if relative:
        out.finish()


def attention_back(place, lengths, proj, dctx, lse, tokens, context, dattended, sums, relative):
    rows, width = dctx.shape
    block = 2 * LEN
    count = rows // block
    extra = 16
    if relative:
        out_specs = [ANY] * 2
        out_shape = [jax.ShapeDtypeStruct((2 * width + extra, width), BF)] * 2
    else:
        out_specs = [pl.BlockSpec((1, width, width), lambda i, *_: (jnp.maximum(i - count, 0), 0, 0))]
        out_shape = [jax.ShapeDtypeStruct((4, width, width), BF)]
    dproj, *grads, column_sums = call(
        functools.partial(attention_back_kernel, relative),
        in_specs=[
            pl.BlockSpec((block, 3 * width), lambda i, *_: (jnp.minimum(i, count - 1), 0)),
            HELD,
            HELD,
            whole(sums[0].shape),
            whole(sums[1].shape),
            whole(sums[2].shape),
            HELD,
            HELD,
            FAR,
            ],
        out_specs=[HELD] + out_specs + [whole((8, 3 * width))],
        out_shape=[jax.ShapeDtypeStruct((rows, 3 * width), BF)] + out_shape + [jax.ShapeDtypeStruct((8, 3 * width), F32)],
        grid=(count + 4,),
        scalars=2,
        scratch_shapes=[
            pltpu.VMEM((rows, width), BF),
            pltpu.VMEM((width, rows), BF),
            pltpu.VMEM((2, width, width), BF),
            pltpu.VMEM((extra, width), BF),
            pltpu.SemaphoreType.DMA((2,)),
            pltpu.SemaphoreType.DMA((2,)),
            pltpu.SemaphoreType.DMA,
        ],
        vmem=28,
        name="attention_back",
    )(place, lengths, proj, dctx, lse, *sums, dattended, context, tokens)
    return dproj, grads, column_sums


def input_grad_kernel(proj_ref, w_hbm_ref, dz_ref, out_ref, w_ref, sems):
    block, width = out_ref.shape
    here = rows_at(pl.program_id(0), block)

    def body(ready):
        grad = dz_ref[here, :].astype(F32)
        for unit in range(3):
            ready(unit)
            grad += dot_nt(proj_ref[here, unit * width : (unit + 1) * width], w_ref[unit])
        ready(3)
        out_ref[...] = grad.astype(BF)

    first_and_later(Bring(WHOLE, (0, 0, 0), [w_hbm_ref], w_ref, sems), body)


def input_grad(dproj, w_qkvo, dz, block=256):
    rows, width = dz.shape
    return call(
        input_grad_kernel,
        in_specs=[HELD, FAR, HELD],
        out_specs=[rows_of(block, width)],
        out_shape=[jax.ShapeDtypeStruct((rows, width), BF)],
        grid=(rows // block,),
        scalars=0,
        scratch_shapes=[pltpu.VMEM((4, width, width), BF), pltpu.SemaphoreType.DMA((4,))],
        vmem=28,
        name="input_grad",
    )(dproj, w_qkvo, dz)[0]


def finish_pair_kernel(place, up_ref, down_ref, one_ref, two_ref, far_ref, up_out_ref, down_out_ref, turned_ref):
    depth, width = up_ref.shape
    half = width // 2
    for position, (up, down) in enumerate(
        [(up_ref[...], down_ref[...])] + [(ref[:depth, :], ref[depth:, :]) for ref in (one_ref, two_ref, far_ref)]
    ):
        unit = place[0] ^ flip_of(position, place[2])
        up_out_ref[:, pl.ds(pl.multiple_of(unit * width, width), width)] = up.astype(F32)
        down = down.astype(F32)
        turned_ref[rows_at(unit, 2 * depth), :] = jnp.concatenate([down[:, :half], down[:, half:]], axis=0)
    down_out_ref[...] = turned_ref[...].T


def finish_pair(place, up, down, backs):
    depth, width = up.shape
    out_shape = [jax.ShapeDtypeStruct((depth, 4 * width), F32), jax.ShapeDtypeStruct((width // 2, width), F32)]
    return call(
        finish_pair_kernel,
        in_specs=[whole(up.shape), whole(down.shape)] + [whole(back.shape) for back in backs],
        out_specs=[whole(shape.shape) for shape in out_shape],
        out_shape=out_shape,
        grid=(1,),
        scalars=1,
        scratch_shapes=[pltpu.VMEM((width, width // 2), F32)],
        vmem=28,
        name="finish_pair",
    )(place, up, down, *backs)


def finish_attention_kernel(place, own_ref, one_ref, two_ref, far_ref, qkv_ref, out_ref):
    width = own_ref.shape[1]
    for position, ref in enumerate((own_ref, one_ref, two_ref, far_ref)):
        unit = place[0] ^ flip_of(position, place[2])
        values = ref[...].astype(F32)

        @pl.when(unit < 3)
        def _():
            qkv_ref[:, pl.ds(pl.multiple_of(unit * width, width), width)] = values

        @pl.when(unit == 3)
        def _():
            out_ref[...] = values


def finish_attention(place, own, backs):
    depth, width = own.shape
    out_shape = [jax.ShapeDtypeStruct((depth, 3 * width), F32), jax.ShapeDtypeStruct((depth, width), F32)]
    return call(
        finish_attention_kernel,
        in_specs=[whole(own.shape)] + [whole(back.shape) for back in backs],
        out_specs=[whole(shape.shape) for shape in out_shape],
        out_shape=out_shape,
        grid=(1,),
        scalars=1,
        scratch_shapes=[],
        vmem=28,
        name="finish_attention",
    )(place, own, *backs)


CORES = [(i, i ^ 1) for i in range(8)]


def from_core(value):
    return lax.ppermute(value, "shard", CORES)


def from_chip(value, ahead):
    return lax.ppermute(value, "shard", [((i + 2 * ahead) % 8, i) for i in range(8)])


def to_chip(value, ahead):
    return lax.ppermute(value, "shard", [(i, (i + 2 * ahead) % 8) for i in range(8)])


def from_flip(value, which):
    flip = lambda s: which if s % 2 == 0 else 3 - which
    pairs = [(r * 8 + s, (r ^ flip(s)) * 8 + s) for r in range(4) for s in range(8)]
    return lax.ppermute(value, ("rep", "shard"), pairs)


def from_far(value):
    return lax.ppermute(value, "rep", [(i, i ^ 3) for i in range(4)])


def joined(*parts):
    return jnp.concatenate(parts, 0)


def after(value, *earlier):
    return lax.optimization_barrier((value,) + earlier)[0]


class Gather:
    def __init__(self, mine, own, other, own_places, depth):
        self.hops = [from_chip(mine, ahead) for ahead in (1, 2, 3)]
        self.own, self.other, self.own_places, self.depth = own, other, own_places, depth

    def collect(self, *earlier):
        hops = [hop[: self.depth] for hop in self.hops]
        self.got = joined(after(hops[0], *earlier), *hops[1:])

    def first(self, *earlier):
        self.collect(*earlier)
        self.one = from_flip(self.got, 1)

    def second(self, *earlier):
        self.low = joined(self.got, after(self.one, *earlier))
        self.high = from_flip(self.low, 2)

    def direct(self, *earlier):
        self.collect(*earlier)
        self.others = [lax.ppermute(self.got, "rep", [(i, i ^ flip) for i in range(4)]) for flip in (1, 2, 3)]

    def hold(self, *earlier):
        self.others = [after(other, *earlier) for other in self.others]

    def weight_direct(self):
        return self.planned([self.got] + self.others, "direct")

    def weight(self):
        return self.planned([self.low, self.high], "skew")

    def planned(self, mine, kind):
        own = [pltpu.with_memory_space_constraint(piece, pltpu.HBM) for piece in self.own]
        pieces = own + self.other + mine + [from_core(piece) for piece in mine]
        count = len(own)
        entries = [
            (i + count * other, at, unit, None, 0, self.depth, other)
            for other in (0, 1)
            for i, places in enumerate(self.own_places)
            for at, unit in places
        ]
        each = 4 // len(mine)
        arriving = []
        for position in range(4):
            for other in (0, 1):
                source = SWAPPED[position] if kind == "skew" and other else position
                piece = 2 * count + len(mine) * other + source // each
                for ahead in (1, 2, 3):
                    at = pl.ds((3 * (source % each) + ahead - 1) * self.depth, self.depth)
                    arriving.append((piece, at, None, source, ahead, self.depth, other))
        if self.own_places[0][0][1] is None:
            arriving.sort(key=lambda entry: entry[4])
        return (kind, tuple(entries + arriving)), pieces


def wide(value):
    return value.astype(F32)


def share(total):
    return [from_flip(total, 1), from_flip(total, 2), from_far(total)]


class Reduce:
    def __init__(self, grads, extra=0):
        self.keep, self.send = grads
        self.extra = extra
        self.quarter = (self.keep.shape[0] - extra) // 4
        self.depth = self.quarter // 4

    def cores(self, *earlier):
        self.other = from_core(after(self.send, *earlier) if earlier else self.send)

    def first(self, *earlier):
        self.other = after(self.other, *earlier)
        n = 2 * self.quarter
        self.sent = (wide(self.keep[n:]) + wide(self.other[n:])).astype(BF)
        self.one = from_flip(self.sent, 1)

    def second(self, *earlier):
        self.one = after(self.one, *earlier)
        n, x = self.quarter, self.extra
        total = wide(self.keep[n : 2 * n]) + wide(self.other[n : 2 * n]) + wide(self.one[x + n :])
        if x:
            at = slice(2 * n, 2 * n + x)
            self.vector = wide(self.keep[at]) + wide(self.other[at]) + wide(self.one[:x])
            total = joined(total, self.vector)
        self.sent = total.astype(BF)
        self.two = from_flip(self.sent, 2)

    def chips(self, *earlier):
        self.two = after(self.two, *earlier)
        n, x, depth = self.quarter, self.extra, self.depth
        total = wide(self.keep[:n]) + wide(self.other[:n]) + wide(self.one[x : x + n]) + wide(self.two[:n])
        if x:
            self.vector = self.vector + wide(self.two[n:])
        self.total = total[:depth]
        self.hops = []
        self.sents = []
        for ahead in (1, 2, 3):
            part = total[ahead * depth : (ahead + 1) * depth]
            if x:
                part = joined(part, self.vector)
            self.sents.append(part.astype(BF))
            self.hops.append(to_chip(self.sents[-1], ahead))

    def collect(self, *earlier):
        self.hops[0] = after(self.hops[0], *earlier)
        for hop in self.hops:
            self.total = self.total + wide(hop[: self.depth])
            if self.extra:
                self.vector = self.vector + wide(hop[self.depth :])
        self.total = self.total.astype(BF)

    def share(self, *earlier):
        self.collect(*earlier)
        self.backs = share(self.total)


def row_weights(task, lengths, task_masks):
    token_task = jnp.repeat(task, LEN)
    chosen = jnp.where(token_task == 0, task_masks[0], jnp.where(token_task == 1, task_masks[1], task_masks[2]))
    valid = jnp.arange(LEN, dtype=jnp.int32)[None, :] < lengths[:, None]
    return (chosen * valid.astype(jnp.int32).reshape(-1)).astype(F32)[:, None]


def per_device(mesh_shape, *arrays):
    (tokens, cotangent, task, lengths, task_masks, w_qkv, qv_bias, w_out, out_bias, ln1_gain, ln1_bias, w_up, up_bias, w_down, down_bias, ln2_gain, ln2_bias) = arrays
    rows, width = tokens.shape
    shards = mesh_shape["shard"]
    hidden = up_bias.shape[0] * shards
    fast = shards == 8 and mesh_shape["rep"] == 4
    place = jnp.stack([lax.axis_index("rep"), lax.axis_index("shard") // 2, lax.axis_index("shard") % 2]).astype(jnp.int32)
    shard = lax.axis_index("shard")

    vectors = (qv_bias, out_bias, ln1_gain, ln1_bias, down_bias, ln2_gain, ln2_bias, up_bias)
    sizes = [v.shape[0] for v in vectors]

    if fast:
        depth = w_qkv.shape[0]
        rep = place[0]
        every = slice(None)

        def columns(first, count):
            return [((every, pl.ds(unit * width, width)), first + unit) for unit in range(count)]

        mine = lax.dynamic_slice(w_qkv, (0, jnp.minimum(rep, 2) * width), (depth, width))
        mine = jnp.where(rep == 3, w_out, mine)
        other_qkv, other_out, other_up, other_down = [from_core(after(own, mine)) for own in (w_qkv, w_out, w_up, w_down)]
        gather_a = Gather(mine, [w_qkv, w_out], [other_qkv, other_out], [columns(0, 3), columns(3, 1)], depth)
        gather_a.direct(other_qkv, other_out, other_up, other_down)
        packed = jnp.concatenate(after(vectors, gather_a.got))
        packed_rows = jnp.pad(packed, (0, 16 * width - packed.shape[0])).reshape(16, width)
        mine = joined(lax.dynamic_slice(w_up, (0, rep * width), (depth, width)), packed_rows)
        gather_b = Gather(mine, [w_up], [other_up], [columns(0, 4)], depth)
        vec_hops = [after(gather_b.hops[0], gather_a.got)] + gather_b.hops[1:]
        vec_rows = jnp.stack([packed_rows] + [hop[depth:] for hop in vec_hops])
        vec_rows = jnp.stack([vec_rows, from_core(vec_rows)], 1).reshape(8, -1)[:, : packed.shape[0]]
        index = jnp.arange(8)
        slot = 2 * ((index // 2 - place[1]) % 4) + ((index % 2) ^ place[2])
        pick = (slot[:, None] == index[None, :]).astype(BF)
        all_vectors = jnp.dot(pick, vec_rows, preferred_element_type=F32)
        row_weight = row_weights(*after((task, lengths, task_masks), gather_a.got))
    else:
        row_weight = row_weights(task, lengths, task_masks)
        packed = jnp.concatenate(vectors)
        all_vectors = lax.all_gather(packed, "shard", axis=0).astype(F32)
        full_a = jnp.concatenate([lax.all_gather(w_qkv, "shard", axis=0, tiled=True), lax.all_gather(w_out, "shard", axis=0, tiled=True)], 1)
        full_b = lax.all_gather(w_up, "shard", axis=0, tiled=True)
        weight_a = (WHOLE, [full_a.reshape(width, 4, width).transpose(1, 0, 2)])
        weight_b = (WHOLE, [full_b.reshape(width, 4, width).transpose(1, 0, 2)])
        full_c = lax.all_gather(w_down, "shard", axis=0, tiled=True)
        weight_c = (WHOLE, [full_c.reshape(4, -1, width)])

    full, start = [], 0
    for size in sizes:
        full.append(all_vectors[:, start : start + size].reshape(-1))
        start += size
    qv, out_shift, gain_one, shift_one, down_shift, gain_two, shift_two, up_shift = full
    qkv_shift = jnp.concatenate([qv[:width], jnp.zeros((width,), F32), qv[width:]])[None]
    vecs = jnp.stack([out_shift, gain_one, shift_one, down_shift, gain_two, shift_two, shift_two, shift_two])
    up_shift = up_shift[None]

    if fast:
        gather_a.hold(qkv_shift, vecs, up_shift, row_weight)
        weight_a = gather_a.weight_direct()
        gather_b.first()
        gather_b.second(*gather_a.others)
        mine = lax.dynamic_slice(w_down, (rep * depth, 0), (depth, width))
        own = [[(pl.ds(0, 4 * depth), None)]]
        mine = after(mine, gather_b.low)
        gather_c = Gather(mine, [w_down], [other_down], own, depth)
        qkv_shift = after(qkv_shift, gather_b.low, mine)
    proj, context, lse, w_a = attention_forward(place, lengths, tokens, qkv_shift, weight_a)
    if fast:
        gather_c.direct(context)
        gather_b.high = after(gather_b.high, gather_c.got)
        weight_b = gather_b.weight()
        context = after(context, gather_c.got)
    norm_one, scale_one, first_low, act, slope, w_b = middle(place, tokens, context, w_a, vecs, up_shift, weight_b)
    if fast:
        gather_c.hold(act)
        weight_c = gather_c.weight_direct()
    output, dffn, sums_two, down_full, grads_c = ffn(place, act, weight_c, norm_one, cotangent, row_weight, vecs, shards, fast)
    if fast:
        group_c = Reduce(grads_c)
        group_c.cores()
    dinner, sums_up, grads_b = inner_grads(place, dffn, first_low, down_full, slope, fast)
    if fast:
        group_c.first(dinner)
        group_b = Reduce(grads_b)
        group_b.cores(group_c.sent)
        dinner = after(dinner, group_c.sent)
    dattended, dcontext, sums_one = first_grad(dinner, w_b, dffn, norm_one, scale_one, vecs, w_a)
    if fast:
        group_b.first(dcontext)
        group_c.second(dcontext)
        lse = after(lse, group_b.sent, group_c.sent)
    sums = (sums_one, sums_two, sums_up)
    dproj, grads_a, sums_qkv = attention_back(place, lengths, proj, dcontext, lse, tokens, context, dattended, sums, fast)
    if fast:
        group_a = Reduce(grads_a, 16)
        group_c.two, group_b.one = after(group_c.two, *grads_a), after(group_b.one, *grads_a)
        group_a.cores(group_c.two, group_b.one)
        group_c.chips()
        group_a.first(*group_c.sents)
        group_b.second(group_a.sent)
        dproj = after(dproj, group_b.sent)
    grad_input = input_grad(dproj, w_a, dattended)

    starts = [0]
    for size in sizes:
        starts.append(starts[-1] + size * shards)
    if fast:
        group_c.collect(grad_input)
        group_b.chips(group_c.total)
        group_a.second(*group_b.sents)
        group_a.chips()
        group_b.collect(*group_a.sents)
        half = group_c.total.shape[0] // 2
        down = jnp.concatenate([group_c.total[:half], group_c.total[half:]], 1)
        backs = share(joined(group_b.total, down))
        group_a.share()
        wide_b, final_c = finish_pair(place, group_b.total, down, [after(back, *group_a.hops) for back in backs])
        wide_a, final_out = finish_attention(place, group_a.total, group_a.backs)
        sums = group_a.vector.reshape(-1)
    else:
        units = []
        for (grads,) in (grads_b, grads_a):
            summed = lax.psum_scatter(grads, "shard", scatter_dimension=1, tiled=True)
            units.append([wide(unit) for unit in lax.psum(summed.astype(BF), "rep")])
        units_b, units_a = units
        summed = lax.psum(lax.psum_scatter(grads_c[0], "shard", scatter_dimension=0, tiled=True), "rep")[0]
        units_c = [wide(unit) for unit in jnp.split(summed, 4)]
        wide_a, wide_b = jnp.concatenate(units_a[:3], 1), jnp.concatenate(units_b, 1)
        final_out, final_c = units_a[3], jnp.concatenate(units_c, 0).T
        sums = jnp.concatenate([sums_qkv[0, :width], sums_qkv[0, 2 * width :], sums_one[2], sums_one[0], sums_one[1], sums_two[2], sums_two[0], sums_two[1], sums_up[0]])
        sums = lax.psum(sums, ("rep", "shard"))
    final = [lax.dynamic_slice(sums, (start + shard * size,), (size,)) for start, size in zip(starts, sizes)]
    f_qv, f_out_shift, f_gain_one, f_shift_one, f_down_shift, f_gain_two, f_shift_two, f_up_shift = final
    return (output, grad_input, wide_a, f_qv, final_out, f_out_shift, f_gain_one, f_shift_one, wide_b, f_up_shift, final_c, f_down_shift, f_gain_two, f_shift_two)


def solution(mesh):
    split, shard = P(("rep", "shard"), None), P("shard")
    flat, matrix = P(("rep", "shard")), P("shard", None)
    in_specs = (split, split, flat, flat, P(None, ("rep", "shard")), matrix, shard, matrix, shard, shard, shard, matrix, shard, matrix, shard, shard, shard)
    out_specs = (split, split, matrix, shard, matrix, shard, shard, shard, matrix, shard, matrix, shard, shard, shard)
    return jax.shard_map(
        functools.partial(per_device, dict(mesh.shape)), mesh=mesh, in_specs=in_specs, out_specs=out_specs, check_vma=False
    )
```
